256 devices in a mesh: grp: 2 (over x_lo), tx: 8 (over z), ty: 16 (over x_hi, y, core).
Axes of the slice: x: 4 (x_hi: 2, x_lo: 2; x = x_hi * 2 + x_lo), y: 4, z: 8, core: 2. Of those that a mesh axis runs over, the one named last changes fastest.
Arguments:
- features: bfloat16 [2, 128, 512, 8, 96], P('grp', 'tx', 'ty'), may hold values from -6 to 6
- voxel_mask: int32 [2, 128, 512, 8], P('grp', 'tx', 'ty'), may hold values 0 or 1
- brick_order: int32 [256, 8], P(('grp', 'tx', 'ty')), may hold values from 0 to 7, each once within a row
- brick_count: int32 [256], P(('grp', 'tx', 'ty')), may hold values from 1 to 2, 320 in all
- w_conv1: bfloat16 [27, 9216], P(None, ('tx', 'ty')), may hold values from -0.125 to 0.125
- w_down: bfloat16 [8, 18432], P(None, ('tx', 'ty')), may hold values from -0.21875 to 0.21875
- w_conv2: bfloat16 [27, 36864], P(None, ('tx', 'ty')), may hold values from -0.078125 to 0.078125
- cotangent: bfloat16 [2, 64, 256, 4, 192], P('grp', 'tx', 'ty'), may hold values from -0.019897461 to 0.019897461
Outputs:
- output: bfloat16 [2, 64, 256, 4, 192], P('grp', 'tx', 'ty')
- grad_conv1: float32 [27, 9216], P(None, ('tx', 'ty'))
- grad_down: float32 [8, 18432], P(None, ('tx', 'ty'))
- grad_conv2: float32 [27, 36864], P(None, ('tx', 'ty'))
The draws below stay inside these ranges and needn't reach their ends.
Inputs may be any that keep to these rules, and one draw needn't show every extreme that they name: `brick_order`: each row lists every brick position of its tile once. `brick_count`: some tile has exactly 2 active bricks.
All inputs are finite; a program needn't handle non-finite values. No bound on the sum of `voxel_mask` or of `brick_count` on one device may be relied on, other than what follows from the above.
Results may differ from the reference program's by a relative error of at most 0.01.
Values may be sent and summed in bfloat16 or wider, within the bound.
A program may use at most 128 MiB of HBM per device.

```python
import math
import jax
import jax.numpy as jnp
import numpy as np
from jax import lax

C1 = 96
C2 = 192
GX = 2
GY = 4
CAP = 2
NB = 8
TILES = 256
XG = 128
YG = 512
ACTIVE = 320
N_GRP = 2
N_TX = 8
N_TY = 16


def plant(drawn, stream_key, least, high):
    longest = drawn.shape.index(max(drawn.shape))
    spots = []
    for shift in (0, 1):
        where = [jax.random.randint(jax.random.fold_in(stream_key, axis), (), 0, length) for axis, length in enumerate(drawn.shape)]
        where[longest] = (where[longest] + shift) % drawn.shape[longest]
        spots.append(tuple(where))
    return drawn.at[spots[0]].set(least).at[spots[1]].set(high)


def shard_levels(rng, shape, cuts, smallest, largest):
    level = 1.0
    for dim, shards_of in cuts:
        draws = jax.random.uniform(jax.random.fold_in(jax.random.fold_in(rng, 6), dim), (shards_of,), jnp.float32, smallest / len(cuts), largest / len(cuts))
        level = level * jnp.repeat(jnp.exp(draws), shape[dim] // shards_of).reshape((-1,) + (1,) * (len(shape) - 1 - dim))
    return level


def length_profile(number_of, total, reach, slope):
    weights = [(1 << 20) // math.isqrt(grade ** slope) + 1 for grade in range(2, number_of + 1)]
    spare, holding = total - reach - (number_of - 1), [1] * (number_of - 1)
    while spare > 0:
        free = [i for i in range(number_of - 1) if holding[i] < reach]
        mass, budget = sum([weights[i] for i in free]), spare
        for i in free:
            more = min(reach - holding[i], max(1, budget * weights[i] // mass), spare)
            holding[i] = holding[i] + more
            spare = spare - more
    return np.array([reach] + holding)


def uneven(own_key, count, total, reach, skew):
    if count == 2:
        one = jax.random.randint(own_key, (), max(1, total - reach), min(reach, total - 1) + 1)
        return jnp.stack([one, total - one])
    tallies = jnp.asarray(length_profile(count, total, reach, skew), jnp.int32)
    twos = (count - 1) // 2
    giver, taker = tallies[1:1 + 2 * twos:2], tallies[2:2 + 2 * twos:2]
    margin = jnp.minimum(giver - 1, reach - taker)
    moved = jax.random.randint(jax.random.fold_in(own_key, 1), (twos,), 0, 1 << 20) % (margin + 1)
    tallies = tallies.at[1:1 + 2 * twos:2].set(giver - moved).at[2:2 + 2 * twos:2].set(taker + moved)
    return tallies[jax.random.permutation(jax.random.fold_in(own_key, 2), count)]


def noise(stream_key, dims, spread, most, split=(), kind=jnp.bfloat16):
    result = jax.random.normal(stream_key, dims, jnp.float32) * spread
    if len(split) > 0:
        result = shard_levels(stream_key, dims, split, -0.22, 0.18) * result
    return jnp.clip(result, min=-most, max=most).astype(kind)


def setup_inputs(seed: int = 0) -> dict:
    streams_of = jax.random.split(jax.random.key(seed), 9)
    return {
        "features": noise(streams_of[0], (N_GRP, XG, YG, 8, C1), 1.0, 6.0, ((0, 2), (1, 8), (2, 16))),
        "voxel_mask": plant((jax.random.randint(streams_of[1], (N_GRP, XG, YG, 8), 0, 4) < 3).astype(jnp.int32), jax.random.fold_in(streams_of[1], 1), 0, 1),
        "brick_order": jax.vmap(lambda own: jax.random.permutation(own, NB))(jax.random.split(streams_of[2], TILES)).reshape((TILES, NB)).astype(jnp.int32),
        "brick_count": uneven(streams_of[3], TILES, ACTIVE, CAP, 2).astype(jnp.int32),
        "w_conv1": noise(streams_of[4], (27, C1 * C1), (27 * C1) ** -0.5, 0.125, ((1, 128),)),
        "w_down": noise(streams_of[5], (8, C1 * C2), (8 * C1) ** -0.5, 0.21875, ((1, 128),)),
        "w_conv2": noise(streams_of[6], (27, C2 * C2), (27 * C2) ** -0.5, 0.078125, ((1, 128),)),
        "cotangent": noise(streams_of[7], (N_GRP, XG // 2, YG // 2, 4, C2), 0.003, 0.019897461, ((0, 2), (1, 8), (2, 16))),
    }


tap_offsets = [(ox, oy, oz) for ox in range(3) for oy in range(3) for oz in range(3)]


def live_flags(order, count, bricks):
    places = jnp.arange(bricks, dtype=jnp.int32)
    ranks = jnp.arange(order.shape[0], dtype=jnp.int32)
    match = (order[:, None] == places[None, :]) & (ranks[:, None] < count)
    return jnp.any(match, axis=0).astype(jnp.float32)


def to_blocks(tile, cols_x, cols_y, edge):
    return tile.reshape(cols_x, edge, cols_y, edge, tile.shape[2], tile.shape[3]).transpose(0, 2, 1, 3, 4, 5).reshape(cols_x * cols_y, edge, edge, tile.shape[2], tile.shape[3])


def from_blocks(blocks, cols_x, cols_y):
    edge = blocks.shape[1]
    return blocks.reshape(cols_x, cols_y, edge, edge, blocks.shape[3], blocks.shape[4]).transpose(0, 2, 1, 3, 4, 5).reshape(cols_x * edge, cols_y * edge, blocks.shape[3], blocks.shape[4])


def windows(padded, slots, cols_y, edge):
    span = edge + 2

    def single(place):
        start_x = (place // cols_y) * edge
        start_y = (place % cols_y) * edge
        nought = jnp.zeros((), jnp.int32)
        return lax.dynamic_slice(padded, (start_x.astype(jnp.int32), start_y.astype(jnp.int32), nought, nought), (span, span, padded.shape[2], padded.shape[3]))

    return jax.vmap(single)(slots)


def conv_taps(wins, weight, edge):
    total = None
    for index, (ox, oy, oz) in enumerate(tap_offsets):
        piece = wins[:, ox:ox + edge, oy:oy + edge, oz:oz + edge, :].reshape(-1, wins.shape[-1])
        term = jnp.dot(piece, weight[index], preferred_element_type=jnp.float32)
        total = term if total is None else total + term
    return total.reshape(wins.shape[0], edge, edge, edge, weight.shape[2])


def conv_back(wins, weight, edge):
    total = None
    for index, (ox, oy, oz) in enumerate(tap_offsets):
        piece = wins[:, 2 - ox:2 - ox + edge, 2 - oy:2 - oy + edge, 2 - oz:2 - oz + edge, :].reshape(-1, wins.shape[-1])
        term = jnp.dot(piece, weight[index].T, preferred_element_type=jnp.float32)
        total = term if total is None else total + term
    return total.reshape(wins.shape[0], edge, edge, edge, weight.shape[1])


def tap_grads(wins, grads, edge):
    flat_grads = grads.reshape(-1, grads.shape[-1])
    terms = []
    for ox, oy, oz in tap_offsets:
        piece = wins[:, ox:ox + edge, oy:oy + edge, oz:oz + edge, :].reshape(-1, wins.shape[-1])
        terms.append(jnp.dot(piece.T, flat_grads, preferred_element_type=jnp.float32))
    return jnp.stack(terms)


def down_patches(tile):
    size_x, size_y, depth, chans = tile.shape
    return tile.reshape(size_x // 2, 2, size_y // 2, 2, depth // 2, 2, chans).transpose(0, 2, 4, 1, 3, 5, 6).reshape(-1, 8 * chans)


def undo_patches(flat, size_x, size_y, depth, chans):
    return flat.reshape(size_x // 2, size_y // 2, depth // 2, 2, 2, 2, chans).transpose(0, 3, 1, 4, 2, 5, 6).reshape(size_x, size_y, depth, chans)


def silu_slope(value):
    sig = jax.nn.sigmoid(value)
    return sig * (1.0 + value * (1.0 - sig))


def reference(features, voxel_mask, brick_order, brick_count, w_conv1, w_down, w_conv2, cotangent):
    size_x = 8 * GX
    size_y = 8 * GY
    half_x = size_x // 2
    half_y = size_y // 2
    kern_one = w_conv1.reshape(27, C1, C1)
    kern_down = w_down.reshape(8 * C1, C2)
    kern_two = w_conv2.reshape(27, C2, C2)
    live = jax.vmap(lambda order, count: live_flags(order, count, NB))(brick_order, brick_count)
    live_map = live.reshape(N_GRP, N_TX, N_TY, GX, GY).transpose(0, 1, 3, 2, 4).reshape(N_GRP, N_TX * GX, N_TY * GY)
    live_map = jnp.repeat(jnp.repeat(live_map, 8, axis=1), 8, axis=2)
    live_mask = voxel_mask.astype(jnp.float32) * live_map[..., None]
    masked = features * live_mask[..., None].astype(jnp.bfloat16)
    padded_one = jnp.pad(masked, ((0, 0), (1, 1), (1, 1), (1, 1), (0, 0)))
    coarse_mask = live_mask.reshape(N_GRP, XG // 2, 2, YG // 2, 2, 4, 2).max(axis=(2, 4, 6))
    nought = jnp.zeros((), jnp.int32)

    def place_of(tile_id):
        region = tile_id // (N_TX * N_TY)
        along_x = (tile_id // N_TY) % N_TX
        along_y = tile_id % N_TY
        return region, along_x, along_y

    def first(carry, tile_id):
        region, along_x, along_y = place_of(tile_id)
        tile = lax.dynamic_slice(padded_one, (region, along_x * size_x, along_y * size_y, nought, nought), (1, size_x + 2, size_y + 2, 10, C1))[0]
        mask_tile = lax.dynamic_slice(live_mask, (region, along_x * size_x, along_y * size_y, nought), (1, size_x, size_y, 8))[0]
        coarse_tile = lax.dynamic_slice(coarse_mask, (region, along_x * half_x, along_y * half_y, nought), (1, half_x, half_y, 4))[0]
        slots = brick_order[tile_id, :CAP]
        wins_one = windows(tile, slots, GY, 8)
        act_one = conv_taps(wins_one, kern_one, 8)
        mask_blocks = to_blocks(mask_tile[..., None], GX, GY, 8)[slots]
        hidden_blocks = (mask_blocks * jax.nn.silu(act_one)).astype(jnp.bfloat16)
        hidden = from_blocks(jnp.zeros((NB, 8, 8, 8, C1), jnp.bfloat16).at[slots].set(hidden_blocks), GX, GY)
        raw = jnp.dot(down_patches(hidden), kern_down, preferred_element_type=jnp.float32).reshape(half_x, half_y, 4, C2)
        down = (coarse_tile[..., None] * raw).astype(jnp.bfloat16)
        return carry, (down, act_one, hidden)

    _, (down_tiles, act_tiles, hidden_tiles) = lax.scan(first, jnp.zeros((), jnp.float32), jnp.arange(TILES, dtype=jnp.int32))

    def assemble(tiles):
        return tiles.reshape(N_GRP, N_TX, N_TY, half_x, half_y, 4, C2).transpose(0, 1, 3, 2, 4, 5, 6).reshape(N_GRP, XG // 2, YG // 2, 4, C2)

    down_all = assemble(down_tiles)
    padded_down = jnp.pad(down_all, ((0, 0), (1, 1), (1, 1), (1, 1), (0, 0)))
    grad_two_all = coarse_mask[..., None].astype(jnp.bfloat16) * cotangent
    padded_grad = jnp.pad(grad_two_all, ((0, 0), (1, 1), (1, 1), (1, 1), (0, 0)))

    def second(totals, tile_id):
        region, along_x, along_y = place_of(tile_id)
        slots = brick_order[tile_id, :CAP]
        tile_down = lax.dynamic_slice(padded_down, (region, along_x * half_x, along_y * half_y, nought, nought), (1, half_x + 2, half_y + 2, 6, C2))[0]
        tile_grad = lax.dynamic_slice(padded_grad, (region, along_x * half_x, along_y * half_y, nought, nought), (1, half_x + 2, half_y + 2, 6, C2))[0]
        cot_tile = lax.dynamic_slice(cotangent, (region, along_x * half_x, along_y * half_y, nought, nought), (1, half_x, half_y, 4, C2))[0]
        coarse_tile = lax.dynamic_slice(coarse_mask, (region, along_x * half_x, along_y * half_y, nought), (1, half_x, half_y, 4))[0]
        mask_tile = lax.dynamic_slice(live_mask, (region, along_x * size_x, along_y * size_y, nought), (1, size_x, size_y, 8))[0]
        tile_one = lax.dynamic_slice(padded_one, (region, along_x * size_x, along_y * size_y, nought, nought), (1, size_x + 2, size_y + 2, 10, C1))[0]
        down = tile_down[1:-1, 1:-1, 1:-1]
        grad_two = tile_grad[1:-1, 1:-1, 1:-1]
        wins_two = windows(tile_down, slots, GY, 4)
        act_two = conv_taps(wins_two, kern_two, 4)
        act_tile = from_blocks(jnp.zeros((NB, 4, 4, 4, C2), jnp.float32).at[slots].set(act_two), GX, GY)
        out_tile = (coarse_tile[..., None] * (down.astype(jnp.float32) + act_tile)).astype(jnp.bfloat16)
        grad_blocks = to_blocks(grad_two, GX, GY, 4)[slots]
        grad_conv2 = tap_grads(wins_two, grad_blocks, 4)
        back = conv_back(windows(tile_grad, slots, GY, 4), kern_two, 4)
        back_tile = from_blocks(jnp.zeros((NB, 4, 4, 4, C2), jnp.float32).at[slots].set(back), GX, GY)
        grad_down_in = (coarse_tile[..., None] * (cot_tile.astype(jnp.float32) + back_tile)).astype(jnp.bfloat16)
        flat_in = grad_down_in.reshape(-1, C2)
        patches = down_patches(hidden_tiles[tile_id])
        grad_down = jnp.dot(patches.T, flat_in, preferred_element_type=jnp.float32)
        grad_hidden = undo_patches(jnp.dot(flat_in, kern_down.T, preferred_element_type=jnp.float32), size_x, size_y, 8, C1)
        hidden_grad_blocks = to_blocks(grad_hidden, GX, GY, 8)[slots]
        mask_blocks = to_blocks(mask_tile[..., None], GX, GY, 8)[slots]
        grad_one = (mask_blocks * hidden_grad_blocks * silu_slope(act_tiles[tile_id])).astype(jnp.bfloat16)
        grad_conv1 = tap_grads(windows(tile_one, slots, GY, 8), grad_one, 8)
        return (totals[0] + grad_conv1, totals[1] + grad_down, totals[2] + grad_conv2), out_tile

    start = (jnp.zeros((27, C1, C1), jnp.float32), jnp.zeros((8 * C1, C2), jnp.float32), jnp.zeros((27, C2, C2), jnp.float32))
    totals, out_tiles = lax.scan(second, start, jnp.arange(TILES, dtype=jnp.int32))
    output = assemble(out_tiles)
    return output, totals[0].reshape(27, C1 * C1), totals[1].reshape(8, C1 * C2), totals[2].reshape(27, C2 * C2)
```

```python
import jax
import jax.numpy as jnp
from jax import lax
from jax.experimental import pallas as pl
from jax.experimental.pallas import tpu as pltpu
from jax.sharding import PartitionSpec as P

C1 = 96
C2 = 192
GX = 2
GY = 4
CAP = 2
GROUPS = 32
N_TX = 8
N_TY = 16
MESH = pl.DeviceIdType.MESH
f32 = jnp.float32
bf16 = jnp.bfloat16
TAPS = [(ox, oy, oz) for ox in range(3) for oy in range(3) for oz in range(3)]
VMEM_LIMIT = 60 * 1024 * 1024


def lane_tiles(rows):
    return [rows[:, i * 128 : (i + 1) * 128] for i in range(rows.shape[1] // 128)]


def relane(count, segments):
    lanes = lax.broadcasted_iota(jnp.int32, segments[0][0][0].shape, 1)
    out = [None] * count
    rolled = {}
    for tiles, src, dst, length in segments:
        while length > 0:
            step = min(length, 128 - src % 128, 128 - dst % 128)
            tile, shift = tiles[src // 128], (dst - src) % 128
            key = (id(tile), shift)
            if key not in rolled:
                rolled[key] = pltpu.roll(tile, shift, 1) if shift else tile
            low, high, target = dst % 128, dst % 128 + step, dst // 128
            base = jnp.zeros_like(tile) if out[target] is None else out[target]
            if step == 128:
                out[target] = rolled[key]
            else:
                inside = lanes < high
                if low:
                    inside = inside & (lanes >= low)
                out[target] = jnp.where(inside, rolled[key], base)
            src, dst, length = src + step, dst + step, length - step
    return [jnp.zeros_like(segments[0][0][0]) if t is None else t for t in out]


PIECES_ONE = [[(0, 0, 0, 72), (1, 0, 72, 24)], [(1, 24, 0, 48), (2, 0, 48, 48)], [(2, 48, 0, 24), (3, 0, 24, 72)]]
PIECES_DOWN = [
    [(0, 0, 0, 144), (1, 0, 144, 48)],
    [(1, 48, 0, 96), (2, 0, 96, 96)],
    [(2, 96, 0, 48), (3, 0, 48, 144)],
]
PIECES_TWO = [
    [(0, 0, 0, 192)],
    [(0, 192, 0, 96), (1, 0, 96, 96)],
    [(1, 96, 0, 192)],
    [(2, 0, 0, 192)],
    [(2, 192, 0, 96), (3, 0, 96, 96)],
    [(3, 96, 0, 192)],
]
BASE_ONE = 288


def to_row(shards, pieces, base, count):
    return relane(count, [(shards[s], base + a, b, n) for s, a, b, n in pieces])


def join(tiles):
    return tiles[0] if len(tiles) == 1 else jnp.concatenate(tiles, axis=1)


def depth_shifts(slab):
    axis = slab.ndim - 2
    depth = lax.broadcasted_iota(jnp.int32, slab.shape, axis)
    below = jnp.where(depth == 0, 0.0, pltpu.roll(slab, 1, axis))
    above = jnp.where(depth == 7, 0.0, pltpu.roll(slab, 7, axis))
    return below, slab, above


def first_level(slots, mp, mask, cm, wg, x1, act, pm, down, wd, w1g, wde, wdo, w1, hs):
    w1g[pl.ds(C1 * 32, 32 * 32), :] = jnp.zeros((32 * 32, 128), f32)
    wde[:, pl.ds(C1 * 8, 32 * 8), :] = jnp.zeros((2, 32 * 8, 128), f32)
    wdo[:, pl.ds(C1 * 8, 32 * 8), :] = jnp.zeros((2, 32 * 8, 128), f32)

    def unpack(a, carry):
        shards = [lane_tiles(wg[a * 4 + b].astype(f32)) for b in range(4)]
        for k in range(3):
            row = a * 3 + k
            w1g[pl.ds(pl.multiple_of(row * 32, 32), 32), :] = join(to_row(shards, PIECES_ONE[k], BASE_ONE, 1))
        last = [[tile[24:32] for tile in tiles] for tiles in shards]
        for k in range(3):
            at = pl.ds(pl.multiple_of((a * 3 + k) * 8, 8), 8)
            for dst, base in ((wde, 0), (wdo, 144)):
                for c, tile in enumerate(to_row(last, PIECES_DOWN[k], base, 2)):
                    dst[c, at, :] = tile
        return carry

    lax.fori_loop(0, GROUPS, unpack, 0)
    for t in range(27):
        w1[t * 128 : (t + 1) * 128, :] = w1g[pl.ds(t, 128, stride=32), :].astype(bf16)
    for t in range(8):
        src = wdo if t % 2 else wde
        for c in range(2):
            wd[t * 128 : (t + 1) * 128, c * 128 : (c + 1) * 128] = src[
                c, pl.ds(3 + t // 2, 128, stride=8), :
            ].astype(bf16)

    down[...] = jnp.zeros_like(down)
    hs[...] = jnp.zeros_like(hs)
    for i in range(CAP):
        place = slots[i]
        px, py = place // GY, place % GY
        window = mp[pl.ds(px * 8, 10), pl.ds(py * 8, 10)]
        shifted = depth_shifts(window)
        for t, (ox, oy, oz) in enumerate(TAPS):
            piece = shifted[oz][ox : ox + 8, oy : oy + 8].reshape(512, 128)
            x1[i * 512 : (i + 1) * 512, t * 128 : (t + 1) * 128] = piece.astype(bf16)
        value = jnp.dot(x1[i * 512 : (i + 1) * 512, :], w1[...], preferred_element_type=f32)
        act[i * 512 : (i + 1) * 512, :] = value
        live = mask[pl.ds(px * 8, 8), pl.ds(py * 8, 8)].reshape(512, 128)
        hidden = (live * jax.nn.silu(value)).astype(bf16).astype(f32).reshape(4, 2, 4, 2, 8, 128)
        for p in range(2):
            for q in range(2):
                for b in range(4):
                    hs[:, p * 2 + q, b * 16 : b * 16 + 8, :] = hidden[:, p, b, q]
        for t in range(8):
            patch = hs[:, t // 2, pl.ds(t % 2, 32, stride=2), :].reshape(128, 128)
            pm[i * 128 : (i + 1) * 128, t * 128 : (t + 1) * 128] = patch.astype(bf16)
        raw = jnp.dot(pm[i * 128 : (i + 1) * 128, :], wd[...], preferred_element_type=f32)
        coarse = cm[pl.ds(px * 4, 4), pl.ds(py * 4, 4)]
        down[pl.ds(px * 4, 4), pl.ds(py * 4, 4)] = (
            (coarse * raw.reshape(4, 4, 8, 256)).astype(bf16).astype(f32)
        )


def level_one(slots, mp, mask, cm, wg):
    return pl.pallas_call(
        first_level,
        grid_spec=pltpu.PrefetchScalarGridSpec(
            num_scalar_prefetch=1,
            grid=(1,),
            in_specs=[pl.BlockSpec(memory_space=pltpu.VMEM)] * 4,
            out_specs=[pl.BlockSpec(memory_space=pltpu.VMEM)] * 5,
            scratch_shapes=[
                pltpu.VMEM((128 * 32, 128), f32),
                pltpu.VMEM((2, 128 * 8, 128), f32),
                pltpu.VMEM((2, 128 * 8, 128), f32),
                pltpu.VMEM((27 * 128, 128), bf16),
                pltpu.VMEM((4, 4, 64, 128), f32),
            ],
        ),
        out_shape=[
            jax.ShapeDtypeStruct((1024, 27 * 128), bf16),
            jax.ShapeDtypeStruct((1024, 128), f32),
            jax.ShapeDtypeStruct((256, 1024), bf16),
            jax.ShapeDtypeStruct((8, 16, 8, 256), f32),
            jax.ShapeDtypeStruct((1024, 256), bf16),
        ],
        compiler_params=pltpu.CompilerParams(vmem_limit_bytes=VMEM_LIMIT),
        name="level_one",
    )(slots, mp, mask, cm, wg)


def second_level(slots, dp, gp, mask, cm, wg, x1, act, pm, wd, out, packed, big, w2, x2, r1, rde, rdo, gs):
    def unpack(a, carry):
        shards = [lane_tiles(wg[a * 4 + b].astype(f32)) for b in range(4)]
        for k in range(6):
            row = a * 6 + k
            for c, tile in enumerate(to_row(shards, PIECES_TWO[k], 0, 2)):
                big[c, pl.ds(pl.multiple_of(row * 32, 32), 32), :] = tile
        return carry

    lax.fori_loop(0, GROUPS, unpack, 0)
    big[:, pl.ds(C2 * 32, 64 * 32), :] = jnp.zeros((2, 64 * 32, 128), f32)

    def order(t, carry):
        for c in range(2):
            w2[pl.ds(pl.multiple_of(t * 256, 256), 256), c * 128 : (c + 1) * 128] = big[
                c, pl.ds(t, 256, stride=32), :
            ].astype(bf16)
        return carry

    lax.fori_loop(0, 27, order, 0)
    out[...] = jnp.zeros_like(out)
    grads, coarses, downs = [], [], []
    for i in range(CAP):
        place = slots[i]
        px, py = place // GY, place % GY
        shifted = depth_shifts(dp[pl.ds(px * 4, 6), pl.ds(py * 4, 6)])
        for t, (ox, oy, oz) in enumerate(TAPS):
            piece = shifted[oz][ox : ox + 4, oy : oy + 4].reshape(128, 256)
            x2[i * 128 : (i + 1) * 128, t * 256 : (t + 1) * 256] = piece.astype(bf16)
        downs.append(shifted[1][1:5, 1:5].reshape(128, 256))
        grads.append(gp[pl.ds(px * 4 + 1, 4), pl.ds(py * 4 + 1, 4)].reshape(128, 256))
        coarses.append(cm[pl.ds(px * 4, 4), pl.ds(py * 4, 4)].reshape(128, 256))
    grad_two = jnp.concatenate(grads, axis=0)
    coarse = jnp.concatenate(coarses, axis=0)
    value = jnp.dot(x2[...], w2[...], preferred_element_type=f32)
    result = coarse * (jnp.concatenate(downs, axis=0) + value)
    for i in range(CAP):
        place = slots[i]
        px, py = place // GY, place % GY
        out[pl.ds(px * 4, 4), pl.ds(py * 4, 4)] = result[i * 128 : (i + 1) * 128].reshape(4, 4, 8, 256)

    turned = grad_two.T.astype(bf16)
    for t in range(27):
        flipped = jnp.dot(turned, x2[:, t * 256 : (t + 1) * 256], preferred_element_type=f32)
        flipped = flipped.T
        for c in range(2):
            big[c, t * 256 : (t + 1) * 256, :] = flipped[:, c * 128 : (c + 1) * 128]

    for i in range(CAP):
        place = slots[i]
        px, py = place // GY, place % GY
        shifted = depth_shifts(gp[pl.ds(px * 4, 6), pl.ds(py * 4, 6)])
        for t, (ox, oy, oz) in enumerate(TAPS):
            piece = shifted[2 - oz][2 - ox : 6 - ox, 2 - oy : 6 - oy].reshape(128, 256)
            x2[i * 128 : (i + 1) * 128, t * 256 : (t + 1) * 256] = piece.astype(bf16)
    back = None
    for t in range(27):
        term = lax.dot_general(
            x2[:, t * 256 : (t + 1) * 256],
            w2[t * 256 : (t + 1) * 256, :],
            (((1,), (1,)), ((), ())),
            preferred_element_type=f32,
        )
        back = term if back is None else back + term
    grad_in = (grad_two + coarse * back).astype(bf16)

    rde[...] = jnp.zeros_like(rde)
    rdo[...] = jnp.zeros_like(rdo)
    turned_in = grad_in.astype(f32).T.astype(bf16)
    for t in range(8):
        flipped = jnp.dot(turned_in, pm[:, t * 128 : (t + 1) * 128], preferred_element_type=f32)
        dst = rdo if t % 2 else rde
        flipped = flipped.T
        for c in range(2):
            dst[c, (3 + t // 2) * 128 : (4 + t // 2) * 128, :] = flipped[:, c * 128 : (c + 1) * 128]

    for i in range(CAP):
        place = slots[i]
        px, py = place // GY, place % GY
        for t in range(8):
            part = lax.dot_general(
                grad_in[i * 128 : (i + 1) * 128],
                wd[t * 128 : (t + 1) * 128, :],
                (((1,), (1,)), ((), ())),
                preferred_element_type=f32,
            )
            gs[:, t // 2, pl.ds(t % 2, 32, stride=2), :] = part.reshape(4, 32, 128)
        rows = []
        for p in range(2):
            for b in range(4):
                for q in range(2):
                    rows.append(gs[:, p * 2 + q, b * 16 : b * 16 + 8, :])
        hidden = jnp.stack(rows, axis=1).reshape(512, 128)
        live = mask[pl.ds(px * 8, 8), pl.ds(py * 8, 8)].reshape(512, 128)
        value = act[i * 512 : (i + 1) * 512, :]
        sig = jax.nn.sigmoid(value)
        grad_one = live * hidden * (sig * (1.0 + value * (1.0 - sig)))
        turned_one = grad_one.astype(bf16).astype(f32).T.astype(bf16)
        for t in range(27):
            flipped = jnp.dot(
                turned_one, x1[i * 512 : (i + 1) * 512, t * 128 : (t + 1) * 128], preferred_element_type=f32
            ).T
            at = pl.ds(t * 128, 128)
            if i:
                r1[at, :] = r1[at, :] + flipped
            else:
                r1[at, :] = flipped

    edge = lax.broadcasted_iota(jnp.int32, (8, 128), 0) < 3

    def pack(a, carry):
        segs = [[] for _ in range(4)]
        lasts = [[] for _ in range(4)]
        for k in range(6):
            ci = a * 6 + k
            tiles = [big[c, pl.ds(ci, 32, stride=256), :] for c in range(2)]
            for s, at, lane, n in PIECES_TWO[k]:
                segs[s].append((tiles, lane, at, n))
        for k in range(3):
            ci = a * 3 + k
            tiles = [r1[pl.ds(ci, 32, stride=128), :]]
            for s, at, lane, n in PIECES_ONE[k]:
                segs[s].append((tiles, lane, BASE_ONE + at, n))
            for src, base in ((rde, 0), (rdo, 144)):
                tiles = [src[c, pl.ds(ci, 8, stride=128), :] for c in range(2)]
                for s, at, lane, n in PIECES_DOWN[k]:
                    lasts[s].append((tiles, lane, base + at, n))
        for s in range(4):
            wide = relane(3, segs[s])
            tail = relane(3, lasts[s])
            done = [
                jnp.concatenate([w[:24], jnp.where(edge, w[24:], l)], axis=0) for w, l in zip(wide, tail)
            ]
            packed[a * 4 + s] = join(done).astype(bf16)
        return carry

    lax.fori_loop(0, GROUPS, pack, 0)


def level_two(slots, dp, gp, mask, cm, wg, x1, act, pm, wd):
    return pl.pallas_call(
        second_level,
        grid_spec=pltpu.PrefetchScalarGridSpec(
            num_scalar_prefetch=1,
            grid=(1,),
            in_specs=[pl.BlockSpec(memory_space=pltpu.VMEM)] * 9,
            out_specs=[pl.BlockSpec(memory_space=pltpu.VMEM)] * 2,
            scratch_shapes=[
                pltpu.VMEM((2, 32 * 256, 128), f32),
                pltpu.VMEM((27 * 256, 256), bf16),
                pltpu.VMEM((256, 27 * 256), bf16),
                pltpu.VMEM((32 * 128, 128), f32),
                pltpu.VMEM((2, 8 * 128, 128), f32),
                pltpu.VMEM((2, 8 * 128, 128), f32),
                pltpu.VMEM((4, 4, 64, 128), f32),
            ],
        ),
        out_shape=[
            jax.ShapeDtypeStruct((8, 16, 8, 256), f32),
            jax.ShapeDtypeStruct((128, 32, 384), bf16),
        ],
        compiler_params=pltpu.CompilerParams(vmem_limit_bytes=VMEM_LIMIT),
        name="level_two",
    )(slots, dp, gp, mask, cm, wg, x1, act, pm, wd)


def pack_shard(w_conv1, w_down, w_conv2):
    top = jnp.concatenate([w_conv2, w_conv1, jnp.zeros((27, 24), w_conv1.dtype)], axis=1)
    low = jnp.pad(w_down.reshape(4, 288), ((0, 1), (0, 96)))
    return jnp.concatenate([top, low], axis=0)


def unpack_shard(total):
    return total[:27, 288:360], total[27:31, :288].reshape(8, 144), total[:27, :288]


def barrier_with(peers):
    barrier = pltpu.get_barrier_semaphore()
    for peer in peers:
        pl.semaphore_signal(barrier, inc=1, device_id=peer, device_id_type=MESH)
    pl.semaphore_wait(barrier, len(peers))


def place():
    grp, tx, ty = lax.axis_index("grp"), lax.axis_index("tx"), lax.axis_index("ty")
    return grp, tx, ty, ty // 8, (ty // 2) % 4, ty % 2


def other(value, bits):
    if bits == 1:
        return value + 1 - 2 * (value % 2)
    if bits == 2:
        return (value + 2) % 4
    return 3 - value


def ring_peers(grp, tx, ty):
    return [(grp, (tx + d) % N_TX, ty) for d in range(1, N_TX)]


def cube_peers(grp, tx, hi, y, core):
    def ty_of(h, v, c):
        return h * 8 + v * 2 + c

    return {
        "core": (grp, tx, ty_of(hi, y, 1 - core)),
        "y1": (grp, tx, ty_of(hi, other(y, 1), core)),
        "y3": (grp, tx, ty_of(hi, other(y, 3), core)),
        "x": (1 - grp, tx, ty_of(1 - hi, y, core)),
        "grp": (1 - grp, tx, ty_of(hi, y, core)),
    }


STEPS = [(dx, dy) for dx in (-1, 0, 1) for dy in (-1, 0, 1) if dx or dy]


def halo_peers(grp, tx, ty):
    return [(grp, (tx + dx + N_TX) % N_TX, (ty + dy + N_TY) % N_TY) for dx, dy in STEPS]


def edge_out(step, size):
    return pl.ds(0, 1) if step < 0 else pl.ds(size - 1, 1) if step > 0 else pl.ds(0, size)


def edge_in(step, size):
    return pl.ds(size + 1, 1) if step < 0 else pl.ds(0, 1) if step > 0 else pl.ds(1, size)


def halo_copies(src, dst, peers, send, recv, base):
    size_x, size_y = src.shape[0], src.shape[1]
    copies = []
    for k, (dx, dy) in enumerate(STEPS):
        copies.append(
            pltpu.make_async_remote_copy(
                src_ref=src.at[edge_out(dx, size_x), edge_out(dy, size_y)],
                dst_ref=dst.at[edge_in(dx, size_x), edge_in(dy, size_y)],
                send_sem=send.at[base + k],
                recv_sem=recv.at[base + k],
                device_id=peers[k],
                device_id_type=MESH,
            )
        )
    return copies


def clear_edges(dst, tx, ty):
    size_x, size_y = dst.shape[0], dst.shape[1]

    @pl.when(tx == 0)
    def _():
        dst[0:1] = jnp.zeros((1,) + dst.shape[1:], dst.dtype)

    @pl.when(tx == N_TX - 1)
    def _():
        dst[size_x - 1 : size_x] = jnp.zeros((1,) + dst.shape[1:], dst.dtype)

    @pl.when(ty == 0)
    def _():
        dst[:, 0:1] = jnp.zeros((size_x, 1) + dst.shape[2:], dst.dtype)

    @pl.when(ty == N_TY - 1)
    def _():
        dst[:, size_y - 1 : size_y] = jnp.zeros((size_x, 1) + dst.shape[2:], dst.dtype)


def gather_kernel(shard, tile, grad, wg, mp, gp, send, recv, own):
    grp, tx, ty, hi, y, core = place()
    cube = cube_peers(grp, tx, hi, y, core)
    line = ring_peers(grp, tx, ty)
    around = halo_peers(grp, tx, ty)
    barrier_with(line + [cube["core"], cube["y1"], cube["y3"], cube["x"]] + around)
    sent = []

    def start(k, src, dst, peer):
        copy = pltpu.make_async_remote_copy(
            src_ref=src, dst_ref=dst, send_sem=send.at[k], recv_sem=recv.at[k], device_id=peer, device_id_type=MESH
        )
        copy.start()
        sent.append(copy)
        return copy

    line_copies = [start(16 + d, shard, wg.at[tx, hi, y, core], line[d]) for d in range(N_TX - 1)]
    mine = pltpu.make_async_copy(shard, wg.at[tx, hi, y, core], own.at[0])
    mine.start()
    halos = halo_copies(tile, mp, around, send, recv, 0) + halo_copies(grad, gp, around, send, recv, 8)
    for copy in halos:
        copy.start()
    inner = [
        pltpu.make_async_copy(tile, mp.at[pl.ds(1, 16), pl.ds(1, 32)], own.at[1]),
        pltpu.make_async_copy(grad, gp.at[pl.ds(1, 8), pl.ds(1, 16)], own.at[2]),
    ]
    for copy in inner:
        copy.start()

    mine.wait()
    for copy in line_copies:
        copy.wait_recv()
    column = wg.at[:, hi, y, core]
    across = start(23, column, column, cube["x"])
    partner = [start(30, column, column, cube["core"])]
    across.wait_recv()
    first, second = pl.ds(0, 16), pl.ds(16, 16)

    def part(v, rows):
        return wg.at[:, :, v, core, rows]

    near = start(24, part(y, first), part(y, first), cube["y1"])
    far = start(25, part(y, second), part(y, second), cube["y3"])
    twin = wg.at[:, 1 - hi, y, core]
    partner.append(start(31, twin, twin, cube["core"]))
    y1, y2, y3 = other(y, 1), other(y, 2), other(y, 3)
    near.wait_recv()
    far.wait_recv()
    last = [
        start(26, part(y, first), part(y, first), cube["y3"]),
        start(27, part(y1, first), part(y1, first), cube["y3"]),
        start(28, part(y, second), part(y, second), cube["y1"]),
        start(29, part(y3, second), part(y3, second), cube["y1"]),
    ]
    partner.append(start(32, part(y1, first), part(y1, first), cube["core"]))
    partner.append(start(33, part(y3, second), part(y3, second), cube["core"]))
    arrived = [part(y3, first), part(y2, first), part(y1, second), part(y2, second)]
    for k, (copy, ref) in enumerate(zip(last, arrived)):
        copy.wait_recv()
        partner.append(start(34 + k, ref, ref, cube["core"]))
    for copy in halos:
        copy.wait()
    for copy in inner:
        copy.wait()
    for copy in partner:
        copy.wait_recv()
    for copy in sent:
        copy.wait_send()
    clear_edges(mp, tx, ty)
    clear_edges(gp, tx, ty)


def gather(shard, tile, grad):
    return pl.pallas_call(
        gather_kernel,
        in_specs=[pl.BlockSpec(memory_space=pltpu.VMEM)] * 3,
        out_specs=[pl.BlockSpec(memory_space=pltpu.VMEM)] * 3,
        out_shape=[
            jax.ShapeDtypeStruct((8, 2, 4, 2, 32, 384), bf16),
            jax.ShapeDtypeStruct((18, 34, 8, 128), f32),
            jax.ShapeDtypeStruct((10, 18, 8, 256), f32),
        ],
        scratch_shapes=[
            pltpu.SemaphoreType.DMA((38,)),
            pltpu.SemaphoreType.DMA((38,)),
            pltpu.SemaphoreType.DMA((3,)),
        ],
        compiler_params=pltpu.CompilerParams(collective_id=0, has_side_effects=True, vmem_limit_bytes=VMEM_LIMIT),
        name="gather",
    )(shard, tile, grad)


def halo_kernel(tile, dst, send, recv, own):
    grp, tx, ty, _, _, _ = place()
    around = halo_peers(grp, tx, ty)
    barrier_with(around)
    halos = halo_copies(tile, dst, around, send, recv, 0)
    for copy in halos:
        copy.start()
    inner = pltpu.make_async_copy(tile, dst.at[pl.ds(1, 8), pl.ds(1, 16)], own.at[0])
    inner.start()
    inner.wait()
    for copy in halos:
        copy.wait()
    clear_edges(dst, tx, ty)


def halo(tile):
    return pl.pallas_call(
        halo_kernel,
        in_specs=[pl.BlockSpec(memory_space=pltpu.VMEM)],
        out_specs=pl.BlockSpec(memory_space=pltpu.VMEM),
        out_shape=jax.ShapeDtypeStruct((10, 18, 8, 256), f32),
        scratch_shapes=[
            pltpu.SemaphoreType.DMA((8,)),
            pltpu.SemaphoreType.DMA((8,)),
            pltpu.SemaphoreType.DMA((1,)),
        ],
        compiler_params=pltpu.CompilerParams(collective_id=1, has_side_effects=True, vmem_limit_bytes=VMEM_LIMIT),
        name="halo",
    )(tile)


def scatter_kernel(packed, total, sums, rd, ry2, ry1, rx, rz, half, rg, send, recv):
    grp, tx, ty, hi, y, core = place()
    cube = cube_peers(grp, tx, hi, y, core)
    line = ring_peers(grp, tx, ty)
    barrier_with(line + [cube[k] for k in ("core", "y1", "y3", "x", "grp")])
    y1, y2, y3 = other(y, 1), other(y, 2), other(y, 3)
    sent = []

    def start(k, src, dst, peer):
        copy = pltpu.make_async_remote_copy(
            src_ref=src, dst_ref=dst, send_sem=send.at[k], recv_sem=recv.at[k], device_id=peer, device_id_type=MESH
        )
        copy.start()
        sent.append(copy)
        return copy

    def add(z, h, v, rows, left, right):
        both = left[...].astype(f32) + right[...].astype(f32)
        sums[z, h, v, rows, :] = both.astype(bf16)

    first, second, whole = pl.ds(0, 16), pl.ds(16, 16), pl.ds(0, 32)

    order = [y2, y3, y1, y]
    pieces = [start(k, packed.at[:, :, v, 1 - core], rd.at[:, :, v], cube["core"]) for k, v in enumerate(order)]
    for k, v in enumerate(order):
        pieces[k].wait_recv()

        def take(z, carry):
            for h in range(2):
                add(z, h, v, whole, packed.at[z, h, v, core], rd.at[z, h, v])
            return carry

        lax.fori_loop(0, 8, take, 0)

    def part(v, rows):
        return sums.at[:, :, v, rows]

    last = [
        start(4, part(y3, first), ry2.at[0, :, :, first], cube["y3"]),
        start(5, part(y2, first), ry2.at[1, :, :, first], cube["y3"]),
        start(6, part(y1, second), ry2.at[0, :, :, second], cube["y1"]),
        start(7, part(y2, second), ry2.at[1, :, :, second], cube["y1"]),
    ]
    for copy in last:
        copy.wait_recv()

    def take_far(z, carry):
        for h in range(2):
            add(z, h, y, whole, sums.at[z, h, y], ry2.at[0, z, h])
            add(z, h, y1, first, sums.at[z, h, y1, first], ry2.at[1, z, h, first])
            add(z, h, y3, second, sums.at[z, h, y3, second], ry2.at[1, z, h, second])
        return carry

    lax.fori_loop(0, 8, take_far, 0)
    near = [
        start(8, part(y1, first), ry1.at[:, :, first], cube["y1"]),
        start(9, part(y3, second), ry1.at[:, :, second], cube["y3"]),
    ]
    for copy in near:
        copy.wait_recv()

    def take_near(z, carry):
        for h in range(2):
            add(z, h, y, whole, sums.at[z, h, y], ry1.at[z, h])
        return carry

    lax.fori_loop(0, 8, take_near, 0)

    across = start(10, sums.at[:, 1 - hi, y], rx, cube["x"])
    across.wait_recv()

    def take_across(z, carry):
        add(z, hi, y, whole, sums.at[z, hi, y], rx.at[z])
        return carry

    lax.fori_loop(0, 8, take_across, 0)
    spread = [
        start(11 + d, sums.at[(tx + d + 1) % N_TX, hi, y], rz.at[d], line[d]) for d in range(N_TX - 1)
    ]
    value = sums[tx, hi, y].astype(f32)
    for d, copy in enumerate(spread):
        copy.wait_recv()
        value = value + rz[d].astype(f32)
    half[...] = value
    swap = start(18, half, rg, cube["grp"])
    swap.wait_recv()
    total[...] = half[...] + rg[...]
    for copy in sent:
        copy.wait_send()


def scatter(packed):
    return pl.pallas_call(
        scatter_kernel,
        in_specs=[pl.BlockSpec(memory_space=pltpu.VMEM)],
        out_specs=pl.BlockSpec(memory_space=pltpu.VMEM),
        out_shape=jax.ShapeDtypeStruct((32, 384), f32),
        scratch_shapes=[
            pltpu.VMEM((8, 2, 4, 32, 384), bf16),
            pltpu.VMEM((8, 2, 4, 32, 384), bf16),
            pltpu.VMEM((2, 8, 2, 32, 384), bf16),
            pltpu.VMEM((8, 2, 32, 384), bf16),
            pltpu.VMEM((8, 32, 384), bf16),
            pltpu.VMEM((7, 32, 384), bf16),
            pltpu.VMEM((32, 384), f32),
            pltpu.VMEM((32, 384), f32),
            pltpu.SemaphoreType.DMA((19,)),
            pltpu.SemaphoreType.DMA((19,)),
        ],
        compiler_params=pltpu.CompilerParams(collective_id=2, has_side_effects=True, vmem_limit_bytes=VMEM_LIMIT),
        name="scatter",
    )(packed)


def live_flags(order, count, bricks):
    places = jnp.arange(bricks, dtype=jnp.int32)
    ranks = jnp.arange(order.shape[0], dtype=jnp.int32)
    match = (order[:, None] == places[None, :]) & (ranks[:, None] < count)
    return jnp.any(match, axis=0).astype(f32)


def local(features, voxel_mask, brick_order, brick_count, w_conv1, w_down, w_conv2, cotangent):
    order = brick_order[0]
    slots = order[:CAP]
    shard = pack_shard(w_conv1, w_down, w_conv2)
    live = live_flags(order, brick_count[0], GX * GY).reshape(GX, GY)
    live_map = jnp.repeat(jnp.repeat(live, 8, axis=0), 8, axis=1)
    live_mask = voxel_mask[0].astype(f32) * live_map[..., None]
    mask = jnp.broadcast_to(live_mask[..., None], (16, 32, 8, 128))
    masked = jnp.pad(features[0].astype(f32), ((0, 0), (0, 0), (0, 0), (0, 32))) * mask
    coarse = live_mask.reshape(8, 2, 16, 2, 4, 2).max(axis=(1, 3, 5))
    coarse = jnp.broadcast_to(jnp.pad(coarse, ((0, 0), (0, 0), (0, 4)))[..., None], (8, 16, 8, 256))
    grad_two = jnp.pad(cotangent[0].astype(f32), ((0, 0), (0, 0), (0, 4), (0, 64))) * coarse
    wg, mp, gp = gather(shard, masked, grad_two)
    wg = wg.reshape(128, 32, 384)
    x1, act, pm, down, wd = level_one(slots, mp, mask, coarse, wg)
    dp = halo(down)
    out, packed = level_two(slots, dp, gp, mask, coarse, wg, x1, act, pm, wd)
    total = scatter(packed.reshape(8, 2, 4, 2, 32, 384))
    one, low, two = unpack_shard(total)
    return out[None, :, :, :4, :C2].astype(bf16), one, low, two


def solution(mesh):
    return jax.shard_map(
        local,
        mesh=mesh,
        in_specs=(
            P("grp", "tx", "ty", None, None),
            P("grp", "tx", "ty", None),
            P(("grp", "tx", "ty"), None),
            P(("grp", "tx", "ty")),
            P(None, ("tx", "ty")),
            P(None, ("tx", "ty")),
            P(None, ("tx", "ty")),
            P("grp", "tx", "ty", None, None),
        ),
        out_specs=(
            P("grp", "tx", "ty", None, None),
            P(None, ("tx", "ty")),
            P(None, ("tx", "ty")),
            P(None, ("tx", "ty")),
        ),
        check_vma=False,
    )
```

```python
import jax
import jax.numpy as jnp
from jax import lax
from jax.experimental import pallas as pl
from jax.experimental.pallas import tpu as pltpu
from jax.sharding import PartitionSpec as P

C1 = 96
C2 = 192
GX = 2
GY = 4
CAP = 2
GROUPS = 32
N_TX = 8
N_TY = 16
PITCH_W = 33
PITCH_R = 264
PITCH_S = 136
MESH = pl.DeviceIdType.MESH
f32 = jnp.float32
bf16 = jnp.bfloat16
TAPS = [(ox, oy, oz) for ox in range(3) for oy in range(3) for oz in range(3)]
VMEM_LIMIT = 60 * 1024 * 1024


def lane_tiles(rows):
    return [rows[:, i * 128 : (i + 1) * 128] for i in range(rows.shape[1] // 128)]


def relane(count, segments):
    lanes = lax.broadcasted_iota(jnp.int32, segments[0][0][0].shape, 1)
    out = [None] * count
    rolled = {}
    for tiles, src, dst, length in segments:
        while length > 0:
            step = min(length, 128 - src % 128, 128 - dst % 128)
            tile, shift = tiles[src // 128], (dst - src) % 128
            key = (id(tile), shift)
            if key not in rolled:
                rolled[key] = pltpu.roll(tile, shift, 1) if shift else tile
            low, high, target = dst % 128, dst % 128 + step, dst // 128
            base = jnp.zeros_like(tile) if out[target] is None else out[target]
            if step == 128:
                out[target] = rolled[key]
            else:
                inside = lanes < high
                if low:
                    inside = inside & (lanes >= low)
                out[target] = jnp.where(inside, rolled[key], base)
            src, dst, length = src + step, dst + step, length - step
    return [jnp.zeros_like(segments[0][0][0]) if t is None else t for t in out]


PIECES_ONE = [[(0, 0, 0, 72), (1, 0, 72, 24)], [(1, 24, 0, 48), (2, 0, 48, 48)], [(2, 48, 0, 24), (3, 0, 24, 72)]]
PIECES_TWO = [
    [(0, 0, 0, 192)],
    [(0, 192, 0, 96), (1, 0, 96, 96)],
    [(1, 96, 0, 192)],
    [(2, 0, 0, 192)],
    [(2, 192, 0, 96), (3, 0, 96, 96)],
    [(3, 96, 0, 192)],
]
BASE_DOWN = 72


def to_row(shards, pieces, base, count):
    return relane(count, [(shards[s], base + a, b, n) for s, a, b, n in pieces])


def join(tiles):
    return tiles[0] if len(tiles) == 1 else jnp.concatenate(tiles, axis=1)


def depth_shifts(slab):
    axis = slab.ndim - 2
    depth = lax.broadcasted_iota(jnp.int32, slab.shape, axis)
    below = jnp.where(depth == 0, 0.0, pltpu.roll(slab, 1, axis))
    above = jnp.where(depth == 7, 0.0, pltpu.roll(slab, 7, axis))
    return below, slab, above


FIRST, SECOND, WHOLE = pl.ds(0, 16), pl.ds(16, 16), pl.ds(0, 32)


def barrier_with(peers):
    barrier = pltpu.get_barrier_semaphore()
    for peer in peers:
        pl.semaphore_signal(barrier, inc=1, device_id=peer, device_id_type=MESH)
    pl.semaphore_wait(barrier, len(peers))


def place():
    grp, tx, ty = lax.axis_index("grp"), lax.axis_index("tx"), lax.axis_index("ty")
    return grp, tx, ty, ty // 8, (ty // 2) % 4, ty % 2


def other(value, bits):
    if bits == 1:
        return value + 1 - 2 * (value % 2)
    if bits == 2:
        return (value + 2) % 4
    return 3 - value


def ring_peers(grp, tx, ty):
    return [(grp, (tx + d) % N_TX, ty) for d in range(1, N_TX)]


def cube_peers(grp, tx, hi, y, core):
    def ty_of(h, v, c):
        return h * 8 + v * 2 + c

    return {
        "core": (grp, tx, ty_of(hi, y, 1 - core)),
        "y1": (grp, tx, ty_of(hi, other(y, 1), core)),
        "y3": (grp, tx, ty_of(hi, other(y, 3), core)),
        "x": (1 - grp, tx, ty_of(1 - hi, y, core)),
        "grp": (1 - grp, tx, ty_of(hi, y, core)),
    }


STEPS = [(dx, dy) for dx in (-1, 0, 1) for dy in (-1, 0, 1) if dx or dy]


def halo_peers(grp, tx, ty):
    return [(grp, (tx + dx + N_TX) % N_TX, (ty + dy + N_TY) % N_TY) for dx, dy in STEPS]


def edge_out(step, size, shift):
    return pl.ds(shift, 1) if step < 0 else pl.ds(size - 1 + shift, 1) if step > 0 else pl.ds(shift, size)


def edge_in(step, size):
    return pl.ds(size + 1, 1) if step < 0 else pl.ds(0, 1) if step > 0 else pl.ds(1, size)


def clear_edges(dst, tx, ty):
    size_x, size_y = dst.shape[0], dst.shape[1]

    @pl.when(tx == 0)
    def _():
        dst[0:1] = jnp.zeros((1,) + dst.shape[1:], dst.dtype)

    @pl.when(tx == N_TX - 1)
    def _():
        dst[size_x - 1 : size_x] = jnp.zeros((1,) + dst.shape[1:], dst.dtype)

    @pl.when(ty == 0)
    def _():
        dst[:, 0:1] = jnp.zeros((size_x, 1) + dst.shape[2:], dst.dtype)

    @pl.when(ty == N_TY - 1)
    def _():
        dst[:, size_y - 1 : size_y] = jnp.zeros((size_x, 1) + dst.shape[2:], dst.dtype)


class Links:
    def __init__(self, send, recv):
        self.send, self.recv, self.sent = send, recv, []

    def start(self, src, dst, peer):
        k = len(self.sent)
        copy = pltpu.make_async_remote_copy(
            src_ref=src,
            dst_ref=dst,
            send_sem=self.send.at[k],
            recv_sem=self.recv.at[k],
            device_id=peer,
            device_id_type=MESH,
        )
        copy.start()
        self.sent.append(copy)
        return copy

    def halo(self, src, dst, peers, inside):
        size_x, size_y = dst.shape[0] - 2, dst.shape[1] - 2
        shift = 1 if inside else 0
        copies = []
        for peer, (dx, dy) in zip(peers, STEPS):
            copies.append(
                self.start(
                    src.at[edge_out(dx, size_x, shift), edge_out(dy, size_y, shift)],
                    dst.at[edge_in(dx, size_x), edge_in(dy, size_y)],
                    peer,
                )
            )
        return copies


class Gather:
    def __init__(self, links, where, shard, full, own):
        self.links, self.where, self.full = links, where, full
        grp, tx, ty, hi, y, core = where
        self.cube = cube_peers(grp, tx, hi, y, core)
        mine = full.at[tx, hi, y, core]
        self.line = [links.start(shard, mine, peer) for peer in ring_peers(grp, tx, ty)]
        self.own = pltpu.make_async_copy(shard, mine, own)
        self.own.start()
        self.partner = []

    def part(self, v, rows):
        return self.full.at[:, :, v, self.where[5], rows]

    def to_core(self, ref):
        self.partner.append(self.links.start(ref, ref, self.cube["core"]))

    def across(self):
        grp, tx, ty, hi, y, core = self.where
        self.own.wait()
        for copy in self.line:
            copy.wait_recv()
        column = self.full.at[:, hi, y, core]
        self.step = [self.links.start(column, column, self.cube["x"])]
        self.to_core(column)

    def near(self):
        grp, tx, ty, hi, y, core = self.where
        for copy in self.step:
            copy.wait_recv()
        first, second = self.part(y, FIRST), self.part(y, SECOND)
        self.step = [
            self.links.start(first, first, self.cube["y1"]),
            self.links.start(second, second, self.cube["y3"]),
        ]
        self.to_core(self.full.at[:, 1 - hi, y, core])

    def far(self):
        y = self.where[4]
        y1, y3 = other(y, 1), other(y, 3)
        for copy in self.step:
            copy.wait_recv()
        self.step = []
        for v, rows, name in ((y, FIRST, "y3"), (y1, FIRST, "y3"), (y, SECOND, "y1"), (y3, SECOND, "y1")):
            self.step.append(self.links.start(self.part(v, rows), self.part(v, rows), self.cube[name]))
        self.to_core(self.part(y1, FIRST))
        self.to_core(self.part(y3, SECOND))

    def last(self):
        y = self.where[4]
        y1, y2, y3 = other(y, 1), other(y, 2), other(y, 3)
        arrived = [(y3, FIRST), (y2, FIRST), (y1, SECOND), (y2, SECOND)]
        for copy, (v, rows) in zip(self.step, arrived):
            copy.wait_recv()
            self.to_core(self.part(v, rows))

    def done(self):
        for copy in self.partner:
            copy.wait_recv()


class Scatter:
    def __init__(self, links, where, packed, total, sums, rd, ry2, ry1, rx, rz, half, rg):
        self.links, self.where, self.packed, self.total = links, where, packed, total
        self.sums, self.rd, self.ry2, self.ry1 = sums, rd, ry2, ry1
        self.rx, self.rz, self.half, self.rg = rx, rz, half, rg
        grp, tx, ty, hi, y, core = where
        self.cube = cube_peers(grp, tx, hi, y, core)
        self.line = ring_peers(grp, tx, ty)
        self.ys = [other(y, 2), other(y, 3), other(y, 1), y]

    def add(self, z, h, v, rows, left, right):
        both = left[...].astype(f32) + right[...].astype(f32)
        self.sums[z, h, v, rows, :] = both.astype(bf16)

    def part(self, v, rows):
        return self.sums.at[:, :, v, rows]

    def wait(self):
        for copy in self.step:
            copy.wait_recv()

    def cores(self):
        core = self.where[5]
        self.step = [
            self.links.start(self.packed.at[:, :, v, 1 - core], self.rd.at[:, :, v], self.cube["core"])
            for v in self.ys
        ]

    def far(self):
        core = self.where[5]
        y2, y3, y1, y = self.ys
        for copy, v in zip(self.step, self.ys):
            copy.wait_recv()

            def take(z, carry):
                for h in range(2):
                    self.add(z, h, v, WHOLE, self.packed.at[z, h, v, core], self.rd.at[z, h, v])
                return carry

            lax.fori_loop(0, 8, take, 0)
        self.step = [
            self.links.start(self.part(y3, FIRST), self.ry2.at[0, :, :, FIRST], self.cube["y3"]),
            self.links.start(self.part(y2, FIRST), self.ry2.at[1, :, :, FIRST], self.cube["y3"]),
            self.links.start(self.part(y1, SECOND), self.ry2.at[0, :, :, SECOND], self.cube["y1"]),
            self.links.start(self.part(y2, SECOND), self.ry2.at[1, :, :, SECOND], self.cube["y1"]),
        ]

    def near(self):
        y2, y3, y1, y = self.ys
        self.wait()

        def take(z, carry):
            for h in range(2):
                self.add(z, h, y, WHOLE, self.sums.at[z, h, y], self.ry2.at[0, z, h])
                self.add(z, h, y1, FIRST, self.sums.at[z, h, y1, FIRST], self.ry2.at[1, z, h, FIRST])
                self.add(z, h, y3, SECOND, self.sums.at[z, h, y3, SECOND], self.ry2.at[1, z, h, SECOND])
            return carry

        lax.fori_loop(0, 8, take, 0)
        self.step = [
            self.links.start(self.part(y1, FIRST), self.ry1.at[:, :, FIRST], self.cube["y1"]),
            self.links.start(self.part(y3, SECOND), self.ry1.at[:, :, SECOND], self.cube["y3"]),
        ]

    def across(self):
        hi, y = self.where[3], self.where[4]
        self.wait()

        def take(z, carry):
            for h in range(2):
                self.add(z, h, y, WHOLE, self.sums.at[z, h, y], self.ry1.at[z, h])
            return carry

        lax.fori_loop(0, 8, take, 0)
        self.step = [self.links.start(self.sums.at[:, 1 - hi, y], self.rx, self.cube["x"])]

    def along(self):
        tx, hi, y = self.where[1], self.where[3], self.where[4]
        self.wait()

        def take(z, carry):
            self.add(z, hi, y, WHOLE, self.sums.at[z, hi, y], self.rx.at[z])
            return carry

        lax.fori_loop(0, 8, take, 0)
        self.step = [
            self.links.start(self.sums.at[(tx + d + 1) % N_TX, hi, y], self.rz.at[d], peer)
            for d, peer in enumerate(self.line)
        ]

    def swap(self):
        tx, hi, y = self.where[1], self.where[3], self.where[4]
        self.wait()
        value = self.sums[tx, hi, y].astype(f32)
        for d in range(N_TX - 1):
            value = value + self.rz[d].astype(f32)
        self.half[...] = value
        self.step = [self.links.start(self.half, self.rg, self.cube["grp"])]

    def done(self):
        self.wait()
        self.total[...] = self.half[...] + self.rg[...]


def choose(slots, place, blocks):
    value = None
    for i, block in enumerate(blocks):
        term = jnp.where(slots[i] == place, block, 0.0)
        value = term if value is None else value + term
    return value


def corner(slots, i):
    return slots[i] // GY, slots[i] % GY


def unpack_first(full, w9, wd, w1g, wdg, tmp):
    def unpack(a, carry):
        shards = []
        for b in range(4):
            value = full[a // 4, (a // 2) % 2, (a % 2) * 2 + b // 2, b % 2].astype(f32)
            tmp[b] = value
            shards.append([value])
        for k in range(3):
            w1g[pl.ds((a * 3 + k) * PITCH_W, 32), :] = to_row(shards, PIECES_ONE[k], 0, 1)[0]
        chunks = [[tmp[b, pl.ds(j, 8, stride=3), :]] for b in range(4) for j in range(3)]
        for k in range(3):
            segments = [(chunks[4 * k + n], BASE_DOWN, 48 * n, 48) for n in range(4)]
            for c, tile in enumerate(relane(2, segments)):
                wdg[c, pl.ds(pl.multiple_of((a * 3 + k) * 8, 8), 8), :] = tile
        return carry

    lax.fori_loop(0, GROUPS, unpack, 0)
    for t in range(27):
        k, oz = t // 3, t % 3
        w9[k * 128 : k * 128 + C1, oz * 128 : (oz + 1) * 128] = w1g[pl.ds(t, C1, stride=PITCH_W), :].astype(bf16)
    for k in range(9):
        w9[k * 128 + C1 : (k + 1) * 128, :] = jnp.zeros((128 - C1, 384), bf16)
    for t in range(8):
        for c in range(2):
            wd[t * 128 : t * 128 + C1, c * 128 : (c + 1) * 128] = wdg[c, pl.ds(t, C1, stride=8), :].astype(bf16)
        wd[t * 128 + C1 : (t + 1) * 128, :] = jnp.zeros((128 - C1, 256), bf16)


def unpack_second(full, w2, big):
    def unpack(a, carry):
        shards = [
            lane_tiles(full[a // 4, (a // 2) % 2, (a % 2) * 2 + b // 2, b % 2].astype(f32)) for b in range(4)
        ]
        for k in range(6):
            for c, tile in enumerate(to_row(shards, PIECES_TWO[k], 0, 2)):
                big[c, pl.ds((a * 6 + k) * PITCH_W, 32), :] = tile
        return carry

    lax.fori_loop(0, GROUPS, unpack, 0)

    def order(k, carry):
        for oz in range(3):
            for c in range(2):
                w2[pl.ds(pl.multiple_of(k * 256, 256), C2), oz * 256 + c * 128 : oz * 256 + (c + 1) * 128] = big[
                    c, pl.ds(k * 3 + oz, C2, stride=PITCH_W), :
                ].astype(bf16)
        w2[pl.ds(pl.multiple_of(k * 256 + C2, 64), 256 - C2), :] = jnp.zeros((256 - C2, 768), bf16)
        return carry

    lax.fori_loop(0, 9, order, 0)


def windows(dst, i, window, edge, flip):
    lanes = window.shape[-1]
    rows = edge * edge * 8
    for k in range(9):
        ox, oy = k // 3, k % 3
        if flip:
            ox, oy = 2 - ox, 2 - oy
        piece = window[ox : ox + edge, oy : oy + edge].reshape(rows, lanes)
        dst[i * rows : (i + 1) * rows, k * lanes : (k + 1) * lanes] = piece.astype(bf16)


def three(rows, lanes):
    return [rows[:, n * lanes : (n + 1) * lanes].reshape(-1, 8, lanes) for n in range(3)]


def conv(parts):
    low, mid, high = parts
    return (depth_shifts(low)[0] + mid + depth_shifts(high)[2]).reshape(-1, mid.shape[-1])


def spread(value):
    below, mid, above = depth_shifts(value.reshape(-1, 8, value.shape[-1]))
    return jnp.concatenate([v.reshape(value.shape).astype(bf16) for v in (above, mid, below)], axis=1)


def pack_first(packed, r1, rdn, tmp):
    tmp[...] = jnp.zeros_like(tmp)

    def pack(a, carry):
        segments = [[] for _ in range(4)]
        downs = []
        for k in range(3):
            ci = a * 3 + k
            tiles = [r1[pl.ds(ci, 32, stride=PITCH_S), :]]
            for s, at, lane, n in PIECES_ONE[k]:
                segments[s].append((tiles, lane, at, n))
            downs.append([rdn[c, pl.ds(ci, 8, stride=PITCH_S), :] for c in range(2)])
        for b in range(4):
            for j in range(3):
                m = 3 * b + j
                tmp[b, pl.ds(j, 8, stride=3), :] = relane(1, [(downs[m // 4], m % 4 * 48, BASE_DOWN, 48)])[0]
            value = relane(1, segments[b])[0] + tmp[b]
            packed[a // 4, (a // 2) % 2, (a % 2) * 2 + b // 2, b % 2] = value.astype(bf16)
        return carry

    lax.fori_loop(0, GROUPS, pack, 0)


def pack_second(packed, big):
    def pack(a, carry):
        segments = [[] for _ in range(4)]
        for k in range(6):
            tiles = [big[c, pl.ds(a * 6 + k, 32, stride=PITCH_R), :] for c in range(2)]
            for s, at, lane, n in PIECES_TWO[k]:
                segments[s].append((tiles, lane, at, n))
        for b in range(4):
            packed[a // 4, (a // 2) % 2, (a % 2) * 2 + b // 2, b % 2] = join(relane(3, segments[b])).astype(bf16)
        return carry

    lax.fori_loop(0, GROUPS, pack, 0)


def whole_kernel(
    slots, tile, grad, mask, coarse, shard_a, shard_b, out, total_a, total_b,
    full_a, full_b, mp, gp, dp, x9, x2, x3, w9, wd, w2, w1g, wdg, tmp, big, act, pm, hs, gs, r1, rdn,
    packed_a, packed_b, sums_a, rd_a, ry2_a, ry1_a, rx_a, rz_a, half_a, rg_a,
    sums_b, rd_b, ry2_b, ry1_b, rx_b, rz_b, half_b, rg_b, send, recv, own,
):
    where = place()
    grp, tx, ty, hi, y, core = where
    cube = cube_peers(grp, tx, hi, y, core)
    around = halo_peers(grp, tx, ty)
    links = Links(send, recv)
    barrier_with(ring_peers(grp, tx, ty) + [cube[n] for n in ("core", "y1", "y3", "x", "grp")] + around)

    first = Gather(links, where, shard_a, full_a, own.at[0])
    halo_m = links.halo(tile, mp, around, False)
    inner_m = pltpu.make_async_copy(tile, mp.at[pl.ds(1, 16), pl.ds(1, 32)], own.at[2])
    inner_m.start()
    second = Gather(links, where, shard_b, full_b, own.at[1])
    halo_g = links.halo(grad, gp, around, False)
    inner_g = pltpu.make_async_copy(grad, gp.at[pl.ds(1, 8), pl.ds(1, 16)], own.at[3])
    inner_g.start()

    first.across()
    inner_m.wait()
    for copy in halo_m:
        copy.wait_recv()
    clear_edges(mp, tx, ty)
    for i in range(CAP):
        px, py = corner(slots, i)
        windows(x9, i, mp[pl.ds(px * 8, 10), pl.ds(py * 8, 10)], 8, False)
    first.near()
    second.across()
    first.far()
    second.near()
    first.last()
    second.far()
    first.done()
    unpack_first(full_a, w9, wd, w1g, wdg, tmp)
    second.last()

    hs[...] = jnp.zeros_like(hs)
    downs = []
    for i in range(CAP):
        px, py = corner(slots, i)
        value = conv(three(jnp.dot(x9[i * 512 : (i + 1) * 512, :], w9[...], preferred_element_type=f32), 128))
        act[i * 512 : (i + 1) * 512, :] = value
        live = mask[pl.ds(px * 8, 8), pl.ds(py * 8, 8)].reshape(512, 128)
        hidden = (live * jax.nn.silu(value)).astype(bf16).astype(f32).reshape(4, 2, 4, 2, 8, 128)
        for p in range(2):
            for q in range(2):
                for b in range(4):
                    hs[:, p * 2 + q, b * 16 : b * 16 + 8, :] = hidden[:, p, b, q]
        for t in range(8):
            patch = hs[:, t // 2, pl.ds(t % 2, 32, stride=2), :].reshape(128, 128)
            pm[i * 128 : (i + 1) * 128, t * 128 : (t + 1) * 128] = patch.astype(bf16)
        raw = jnp.dot(pm[i * 128 : (i + 1) * 128, :], wd[...], preferred_element_type=f32)
        edge = coarse[pl.ds(px * 4, 4), pl.ds(py * 4, 4)]
        downs.append((edge * raw.reshape(4, 4, 8, 256)).astype(bf16).astype(f32))
    for p in range(GX * GY):
        px, py = p // GY, p % GY
        dp[1 + px * 4 : 5 + px * 4, 1 + py * 4 : 5 + py * 4] = choose(slots, p, downs)
    halo_d = links.halo(dp, dp, around, True)

    inner_g.wait()
    for copy in halo_g:
        copy.wait_recv()
    clear_edges(gp, tx, ty)
    grads, edges = [], []
    for i in range(CAP):
        px, py = corner(slots, i)
        windows(x3, i, gp[pl.ds(px * 4, 6), pl.ds(py * 4, 6)], 4, True)
        grads.append(gp[pl.ds(px * 4 + 1, 4), pl.ds(py * 4 + 1, 4)].reshape(128, 256))
        edges.append(coarse[pl.ds(px * 4, 4), pl.ds(py * 4, 4)].reshape(128, 256))
    grad_two = jnp.concatenate(grads, axis=0)
    edge = jnp.concatenate(edges, axis=0)
    spread_two = spread(grad_two)
    big[:, 27 * PITCH_R : 32 * PITCH_R, :] = jnp.zeros((2, 5 * PITCH_R, 128), f32)
    for copy in halo_d:
        copy.wait_recv()
    clear_edges(dp, tx, ty)
    for i in range(CAP):
        px, py = corner(slots, i)
        windows(x2, i, dp[pl.ds(px * 4, 6), pl.ds(py * 4, 6)], 4, False)
    for k in range(9):
        product = lax.dot_general(
            x2[:, k * 256 : (k + 1) * 256], spread_two, (((0,), (0,)), ((), ())), preferred_element_type=f32
        )
        for oz in range(3):
            for c in range(2):
                at = oz * 256 + c * 128
                big[c, (3 * k + oz) * PITCH_R : (3 * k + oz) * PITCH_R + 256, :] = product[:, at : at + 128]
    pack_second(packed_b, big)
    sum_b = Scatter(
        links, where, packed_b, total_b, sums_b, rd_b, ry2_b, ry1_b, rx_b, rz_b, half_b, rg_b
    )
    sum_b.cores()

    second.done()
    unpack_second(full_b, w2, big)
    sum_b.far()
    parts = []
    for oz in range(3):
        part = None
        for k in range(9):
            term = lax.dot_general(
                x3[:, k * 256 : (k + 1) * 256],
                w2[k * 256 : (k + 1) * 256, oz * 256 : (oz + 1) * 256],
                (((1,), (1,)), ((), ())),
                preferred_element_type=f32,
            )
            part = term if part is None else part + term
        parts.append(part.reshape(-1, 8, 256))
    back = conv(parts[::-1])
    grad_in = (grad_two + edge * back).astype(bf16)
    sum_b.near()

    rdn[...] = jnp.zeros_like(rdn)
    for t in range(8):
        product = lax.dot_general(
            pm[:, t * 128 : (t + 1) * 128], grad_in, (((0,), (0,)), ((), ())), preferred_element_type=f32
        )
        for c in range(2):
            rdn[c, t * PITCH_S : t * PITCH_S + 128, :] = product[:, c * 128 : (c + 1) * 128]
    spreads = []
    for i in range(CAP):
        px, py = corner(slots, i)
        for t in range(8):
            part = lax.dot_general(
                grad_in[i * 128 : (i + 1) * 128],
                wd[t * 128 : (t + 1) * 128, :],
                (((1,), (1,)), ((), ())),
                preferred_element_type=f32,
            )
            gs[:, t // 2, pl.ds(t % 2, 32, stride=2), :] = part.reshape(4, 32, 128)
        rows = []
        for p in range(2):
            for b in range(4):
                for q in range(2):
                    rows.append(gs[:, p * 2 + q, b * 16 : b * 16 + 8, :])
        hidden = jnp.stack(rows, axis=1).reshape(512, 128)
        live = mask[pl.ds(px * 8, 8), pl.ds(py * 8, 8)].reshape(512, 128)
        value = act[i * 512 : (i + 1) * 512, :]
        sig = jax.nn.sigmoid(value)
        spreads.append(spread(live * hidden * (sig * (1.0 + value * (1.0 - sig)))))
    spread_one = jnp.concatenate(spreads, axis=0)
    sum_b.across()
    r1[27 * PITCH_S : 32 * PITCH_S, :] = jnp.zeros((5 * PITCH_S, 128), f32)
    for k in range(9):
        product = lax.dot_general(
            x9[:, k * 128 : (k + 1) * 128], spread_one, (((0,), (0,)), ((), ())), preferred_element_type=f32
        )
        for oz in range(3):
            at = (3 * k + oz) * PITCH_S
            r1[at : at + 128, :] = product[:, oz * 128 : (oz + 1) * 128]
    pack_first(packed_a, r1, rdn, tmp)
    sum_a = Scatter(
        links, where, packed_a, total_a, sums_a, rd_a, ry2_a, ry1_a, rx_a, rz_a, half_a, rg_a
    )
    sum_a.cores()
    sum_b.along()

    value = conv(three(jnp.dot(x2[...], w2[...], preferred_element_type=f32), 256))
    blocks = []
    for i in range(CAP):
        px, py = corner(slots, i)
        down = dp[pl.ds(px * 4 + 1, 4), pl.ds(py * 4 + 1, 4)].reshape(128, 256)
        rows = slice(i * 128, (i + 1) * 128)
        blocks.append((edges[i] * (down + value[rows])).reshape(4, 4, 8, 256))
    sum_a.far()
    for p in range(GX * GY):
        px, py = p // GY, p % GY
        out[px * 4 : px * 4 + 4, py * 4 : py * 4 + 4] = choose(slots, p, blocks)
    sum_a.near()
    sum_b.swap()
    sum_a.across()
    sum_a.along()
    sum_b.done()
    sum_a.swap()
    sum_a.done()
    for copy in links.sent:
        copy.wait_send()


def whole(slots, tile, grad, mask, coarse, shard_a, shard_b):
    def sums(lanes):
        return [
            pltpu.VMEM((8, 2, 4, 32, lanes), bf16),
            pltpu.VMEM((8, 2, 4, 32, lanes), bf16),
            pltpu.VMEM((2, 8, 2, 32, lanes), bf16),
            pltpu.VMEM((8, 2, 32, lanes), bf16),
            pltpu.VMEM((8, 32, lanes), bf16),
            pltpu.VMEM((7, 32, lanes), bf16),
            pltpu.VMEM((32, lanes), f32),
            pltpu.VMEM((32, lanes), f32),
        ]

    copies = 2 * 23 + 24 + 2 * 19
    return pl.pallas_call(
        whole_kernel,
        in_specs=[pl.BlockSpec(memory_space=pltpu.SMEM)] + [pl.BlockSpec(memory_space=pltpu.VMEM)] * 6,
        out_specs=[pl.BlockSpec(memory_space=pltpu.VMEM)] * 3,
        out_shape=[
            jax.ShapeDtypeStruct((8, 16, 8, 256), f32),
            jax.ShapeDtypeStruct((32, 128), f32),
            jax.ShapeDtypeStruct((32, 384), f32),
        ],
        scratch_shapes=[
            pltpu.VMEM((8, 2, 4, 2, 32, 128), bf16),
            pltpu.VMEM((8, 2, 4, 2, 32, 384), bf16),
            pltpu.VMEM((18, 34, 8, 128), f32),
            pltpu.VMEM((10, 18, 8, 256), f32),
            pltpu.VMEM((10, 18, 8, 256), f32),
            pltpu.VMEM((1024, 9 * 128), bf16),
            pltpu.VMEM((256, 9 * 256), bf16),
            pltpu.VMEM((256, 9 * 256), bf16),
            pltpu.VMEM((9 * 128, 384), bf16),
            pltpu.VMEM((1024, 256), bf16),
            pltpu.VMEM((9 * 256, 768), bf16),
            pltpu.VMEM((C1 * PITCH_W + 8, 128), f32),
            pltpu.VMEM((2, C1 * 8, 128), f32),
            pltpu.VMEM((4, 32, 128), f32),
            pltpu.VMEM((2, 32 * PITCH_R, 128), f32),
            pltpu.VMEM((1024, 128), f32),
            pltpu.VMEM((256, 1024), bf16),
            pltpu.VMEM((4, 4, 64, 128), f32),
            pltpu.VMEM((4, 4, 64, 128), f32),
            pltpu.VMEM((32 * PITCH_S, 128), f32),
            pltpu.VMEM((2, 8 * PITCH_S, 128), f32),
            pltpu.VMEM((8, 2, 4, 2, 32, 128), bf16),
            pltpu.VMEM((8, 2, 4, 2, 32, 384), bf16),
        ]
        + sums(128)
        + sums(384)
        + [
            pltpu.SemaphoreType.DMA((copies,)),
            pltpu.SemaphoreType.DMA((copies,)),
            pltpu.SemaphoreType.DMA((4,)),
        ],
        compiler_params=pltpu.CompilerParams(collective_id=0, has_side_effects=True, vmem_limit_bytes=VMEM_LIMIT),
        name="whole",
    )(slots, tile, grad, mask, coarse, shard_a, shard_b)


def live_flags(order, count, bricks):
    places = jnp.arange(bricks, dtype=jnp.int32)
    ranks = jnp.arange(order.shape[0], dtype=jnp.int32)
    match = (order[:, None] == places[None, :]) & (ranks[:, None] < count)
    return jnp.any(match, axis=0).astype(f32)


def local(features, voxel_mask, brick_order, brick_count, w_conv1, w_down, w_conv2, cotangent):
    order = brick_order[0]
    slots = order[:CAP]
    shard_a = jnp.pad(w_conv1, ((0, 5), (0, 56))) + jnp.pad(w_down.reshape(24, 48), ((0, 8), (72, 8)))
    shard_b = jnp.pad(w_conv2, ((0, 5), (0, 96)))
    live = live_flags(order, brick_count[0], GX * GY).reshape(GX, GY)
    live_map = jnp.repeat(jnp.repeat(live, 8, axis=0), 8, axis=1)
    live_mask = voxel_mask[0].astype(f32) * live_map[..., None]
    mask = jnp.broadcast_to(live_mask[..., None], (16, 32, 8, 128))
    masked = jnp.pad(features[0].astype(f32), ((0, 0), (0, 0), (0, 0), (0, 32))) * mask
    coarse = live_mask.reshape(8, 2, 16, 2, 4, 2).max(axis=(1, 3, 5))
    coarse = jnp.broadcast_to(jnp.pad(coarse, ((0, 0), (0, 0), (0, 4)))[..., None], (8, 16, 8, 256))
    grad_two = jnp.pad(cotangent[0].astype(f32), ((0, 0), (0, 0), (0, 4), (0, 64))) * coarse
    out, total_a, total_b = whole(slots, masked, grad_two, mask, coarse, shard_a, shard_b)
    one = total_a[:27, :72]
    low = total_a[:24, 72:120].reshape(8, 144)
    two = total_b[:27, :288]
    return out[None, :, :, :4, :C2].astype(bf16), one, low, two


def solution(mesh):
    return jax.shard_map(
        local,
        mesh=mesh,
        in_specs=(
            P("grp", "tx", "ty", None, None),
            P("grp", "tx", "ty", None),
            P(("grp", "tx", "ty"), None),
            P(("grp", "tx", "ty")),
            P(None, ("tx", "ty")),
            P(None, ("tx", "ty")),
            P(None, ("tx", "ty")),
            P("grp", "tx", "ty", None, None),
        ),
        out_specs=(
            P("grp", "tx", "ty", None, None),
            P(None, ("tx", "ty")),
            P(None, ("tx", "ty")),
            P(None, ("tx", "ty")),
        ),
        check_vma=False,
    )
```

```python
import jax
import jax.numpy as jnp
from jax import lax
from jax.experimental import pallas as pl
from jax.experimental.pallas import tpu as pltpu
from jax.sharding import PartitionSpec as P

C1 = 96
C2 = 192
GX = 2
GY = 4
CAP = 2
GROUPS = 32
N_TX = 8
N_TY = 16
PITCH_W = 33
PITCH_R = 264
PITCH_S = 136
MESH = pl.DeviceIdType.MESH
f32 = jnp.float32
bf16 = jnp.bfloat16
TAPS = [(ox, oy, oz) for ox in range(3) for oy in range(3) for oz in range(3)]
VMEM_LIMIT = 60 * 1024 * 1024


def lane_tiles(rows):
    return [rows[:, i * 128 : (i + 1) * 128] for i in range(rows.shape[1] // 128)]


def relane(count, segments):
    lanes = lax.broadcasted_iota(jnp.int32, segments[0][0][0].shape, 1)
    out = [None] * count
    rolled = {}
    for tiles, src, dst, length in segments:
        while length > 0:
            step = min(length, 128 - src % 128, 128 - dst % 128)
            tile, shift = tiles[src // 128], (dst - src) % 128
            key = (id(tile), shift)
            if key not in rolled:
                rolled[key] = pltpu.roll(tile, shift, 1) if shift else tile
            low, high, target = dst % 128, dst % 128 + step, dst // 128
            base = jnp.zeros_like(tile) if out[target] is None else out[target]
            if step == 128:
                out[target] = rolled[key]
            else:
                inside = lanes < high
                if low:
                    inside = inside & (lanes >= low)
                out[target] = jnp.where(inside, rolled[key], base)
            src, dst, length = src + step, dst + step, length - step
    return [jnp.zeros_like(segments[0][0][0]) if t is None else t for t in out]


PIECES_ONE = [[(0, 0, 0, 72), (1, 0, 72, 24)], [(1, 24, 0, 48), (2, 0, 48, 48)], [(2, 48, 0, 24), (3, 0, 24, 72)]]
PIECES_TWO = [
    [(0, 0, 0, 192)],
    [(0, 192, 0, 96), (1, 0, 96, 96)],
    [(1, 96, 0, 192)],
    [(2, 0, 0, 192)],
    [(2, 192, 0, 96), (3, 0, 96, 96)],
    [(3, 96, 0, 192)],
]
BASE_DOWN = 72


def to_row(shards, pieces, base, count):
    return relane(count, [(shards[s], base + a, b, n) for s, a, b, n in pieces])


def join(tiles):
    return tiles[0] if len(tiles) == 1 else jnp.concatenate(tiles, axis=1)


def depth_shifts(slab):
    axis = slab.ndim - 2
    depth = lax.broadcasted_iota(jnp.int32, slab.shape, axis)
    below = jnp.where(depth == 0, 0.0, pltpu.roll(slab, 1, axis))
    above = jnp.where(depth == 7, 0.0, pltpu.roll(slab, 7, axis))
    return below, slab, above


def barrier_with(peers):
    barrier = pltpu.get_barrier_semaphore()
    for peer in peers:
        pl.semaphore_signal(barrier, inc=1, device_id=peer, device_id_type=MESH)
    pl.semaphore_wait(barrier, len(peers))


def place():
    grp, tx, ty = lax.axis_index("grp"), lax.axis_index("tx"), lax.axis_index("ty")
    return grp, tx, ty, ty // 8, (ty // 2) % 4, ty % 2


def other(value, bits):
    if bits == 1:
        return value + 1 - 2 * (value % 2)
    if bits == 2:
        return (value + 2) % 4
    return 3 - value


def ring_peers(grp, tx, ty):
    return [(grp, (tx + d) % N_TX, ty) for d in range(1, N_TX)]


def cube_peers(grp, tx, hi, y, core):
    def ty_of(h, v, c):
        return h * 8 + v * 2 + c

    return {
        "core": (grp, tx, ty_of(hi, y, 1 - core)),
        "y1": (grp, tx, ty_of(hi, other(y, 1), core)),
        "y3": (grp, tx, ty_of(hi, other(y, 3), core)),
        "x": (1 - grp, tx, ty_of(1 - hi, y, core)),
        "grp": (1 - grp, tx, ty_of(hi, y, core)),
    }


STEPS = [(dx, dy) for dx in (-1, 0, 1) for dy in (-1, 0, 1) if dx or dy]


def halo_peers(grp, tx, ty):
    return [(grp, (tx + dx + N_TX) % N_TX, (ty + dy + N_TY) % N_TY) for dx, dy in STEPS]


def edge_out(step, size, shift):
    return pl.ds(shift, 1) if step < 0 else pl.ds(size - 1 + shift, 1) if step > 0 else pl.ds(shift, size)


def edge_in(step, size):
    return pl.ds(size + 1, 1) if step < 0 else pl.ds(0, 1) if step > 0 else pl.ds(1, size)


def clear_edges(dst, tx, ty):
    size_x, size_y = dst.shape[0], dst.shape[1]

    @pl.when(tx == 0)
    def _():
        dst[0:1] = jnp.zeros((1,) + dst.shape[1:], dst.dtype)

    @pl.when(tx == N_TX - 1)
    def _():
        dst[size_x - 1 : size_x] = jnp.zeros((1,) + dst.shape[1:], dst.dtype)

    @pl.when(ty == 0)
    def _():
        dst[:, 0:1] = jnp.zeros((size_x, 1) + dst.shape[2:], dst.dtype)

    @pl.when(ty == N_TY - 1)
    def _():
        dst[:, size_y - 1 : size_y] = jnp.zeros((size_x, 1) + dst.shape[2:], dst.dtype)


class Links:
    def __init__(self, send, recv):
        self.send, self.recv, self.sent = send, recv, []

    def start(self, src, dst, peer):
        k = len(self.sent)
        copy = pltpu.make_async_remote_copy(
            src_ref=src,
            dst_ref=dst,
            send_sem=self.send.at[k],
            recv_sem=self.recv.at[k],
            device_id=peer,
            device_id_type=MESH,
        )
        copy.start()
        self.sent.append(copy)
        return copy

    def halo(self, src, dst, peers, inside):
        size_x, size_y = dst.shape[0] - 2, dst.shape[1] - 2
        shift = 1 if inside else 0
        copies = []
        for peer, (dx, dy) in zip(peers, STEPS):
            copies.append(
                self.start(
                    src.at[edge_out(dx, size_x, shift), edge_out(dy, size_y, shift)],
                    dst.at[edge_in(dx, size_x), edge_in(dy, size_y)],
                    peer,
                )
            )
        return copies


def halves(rows):
    return pl.ds(0, rows // 2), pl.ds(rows // 2, rows // 2)


class Gather:
    def __init__(self, links, where, shard, full, own):
        self.links, self.where, self.full = links, where, full
        self.first, self.second = halves(shard.shape[0])
        grp, tx, ty, hi, y, core = where
        self.cube = cube_peers(grp, tx, hi, y, core)
        mine = full.at[tx, hi, y, core]
        self.line = [links.start(shard, mine, peer) for peer in ring_peers(grp, tx, ty)]
        self.own = pltpu.make_async_copy(shard, mine, own)
        self.own.start()
        self.partner = []

    def part(self, v, rows):
        return self.full.at[:, :, v, self.where[5], rows]

    def to_core(self, ref):
        self.partner.append(self.links.start(ref, ref, self.cube["core"]))

    def across(self):
        grp, tx, ty, hi, y, core = self.where
        self.own.wait()
        for copy in self.line:
            copy.wait_recv()
        column = self.full.at[:, hi, y, core]
        self.step = [self.links.start(column, column, self.cube["x"])]
        self.to_core(column)

    def near(self):
        grp, tx, ty, hi, y, core = self.where
        for copy in self.step:
            copy.wait_recv()
        first, second = self.part(y, self.first), self.part(y, self.second)
        self.step = [
            self.links.start(first, first, self.cube["y1"]),
            self.links.start(second, second, self.cube["y3"]),
        ]
        self.to_core(self.full.at[:, 1 - hi, y, core])

    def far(self):
        y = self.where[4]
        y1, y3 = other(y, 1), other(y, 3)
        for copy in self.step:
            copy.wait_recv()
        self.step = []
        for v, rows, name in ((y, self.first, "y3"), (y1, self.first, "y3"), (y, self.second, "y1"), (y3, self.second, "y1")):
            self.step.append(self.links.start(self.part(v, rows), self.part(v, rows), self.cube[name]))
        self.to_core(self.part(y1, self.first))
        self.to_core(self.part(y3, self.second))

    def last(self):
        y = self.where[4]
        y1, y2, y3 = other(y, 1), other(y, 2), other(y, 3)
        arrived = [(y3, self.first), (y2, self.first), (y1, self.second), (y2, self.second)]
        for copy, (v, rows) in zip(self.step, arrived):
            copy.wait_recv()
            self.to_core(self.part(v, rows))

    def done(self):
        for copy in self.partner:
            copy.wait_recv()


class Scatter:
    def __init__(self, links, where, packed, total, sums, rd, ry2, ry1, rx, rz, half, rg):
        self.links, self.where, self.packed, self.total = links, where, packed, total
        self.sums, self.rd, self.ry2, self.ry1 = sums, rd, ry2, ry1
        self.rx, self.rz, self.half, self.rg = rx, rz, half, rg
        grp, tx, ty, hi, y, core = where
        self.cube = cube_peers(grp, tx, hi, y, core)
        self.line = ring_peers(grp, tx, ty)
        rows = half.shape[0]
        self.whole, (self.first, self.second) = pl.ds(0, rows), halves(rows)
        self.ys = [other(y, 2), other(y, 3), other(y, 1), y]

    def add(self, z, h, v, rows, left, right):
        both = left[...].astype(f32) + right[...].astype(f32)
        self.sums[z, h, v, rows, :] = both.astype(bf16)

    def part(self, v, rows):
        return self.sums.at[:, :, v, rows]

    def wait(self):
        for copy in self.step:
            copy.wait_recv()

    def cores(self):
        core = self.where[5]
        self.step = [
            self.links.start(self.packed.at[:, :, v, 1 - core], self.rd.at[:, :, v], self.cube["core"])
            for v in self.ys
        ]

    def far(self):
        core = self.where[5]
        y2, y3, y1, y = self.ys
        pieces, self.step = self.step, []
        for k, (copy, v) in enumerate(zip(pieces, self.ys)):
            copy.wait_recv()

            def take(z, carry):
                for h in range(2):
                    self.add(z, h, v, self.whole, self.packed.at[z, h, v, core], self.rd.at[z, h, v])
                return carry

            lax.fori_loop(0, 8, take, 0)
            if k in (1, 2):
                rows, name = (self.first, "y3") if k == 1 else (self.second, "y1")
                for n, u in enumerate((v, y2)):
                    self.step.append(
                        self.links.start(self.part(u, rows), self.ry2.at[n, :, :, rows], self.cube[name])
                    )

    def near(self):
        y2, y3, y1, y = self.ys
        self.wait()

        def take(z, carry):
            for h in range(2):
                self.add(z, h, y, self.whole, self.sums.at[z, h, y], self.ry2.at[0, z, h])
                self.add(z, h, y1, self.first, self.sums.at[z, h, y1, self.first], self.ry2.at[1, z, h, self.first])
                self.add(z, h, y3, self.second, self.sums.at[z, h, y3, self.second], self.ry2.at[1, z, h, self.second])
            return carry

        lax.fori_loop(0, 8, take, 0)
        self.step = [
            self.links.start(self.part(y1, self.first), self.ry1.at[:, :, self.first], self.cube["y1"]),
            self.links.start(self.part(y3, self.second), self.ry1.at[:, :, self.second], self.cube["y3"]),
        ]

    def across(self):
        hi, y = self.where[3], self.where[4]
        self.wait()

        def take(z, carry):
            for h in range(2):
                self.add(z, h, y, self.whole, self.sums.at[z, h, y], self.ry1.at[z, h])
            return carry

        lax.fori_loop(0, 8, take, 0)
        self.step = [self.links.start(self.sums.at[:, 1 - hi, y], self.rx, self.cube["x"])]

    def along(self):
        tx, hi, y = self.where[1], self.where[3], self.where[4]
        self.wait()

        def take(z, carry):
            self.add(z, hi, y, self.whole, self.sums.at[z, hi, y], self.rx.at[z])
            return carry

        lax.fori_loop(0, 8, take, 0)
        self.step = [
            self.links.start(self.sums.at[(tx + d + 1) % N_TX, hi, y], self.rz.at[d], peer)
            for d, peer in enumerate(self.line)
        ]

    def swap(self):
        tx, hi, y = self.where[1], self.where[3], self.where[4]
        self.wait()
        value = self.sums[tx, hi, y].astype(f32)
        for d in range(N_TX - 1):
            value = value + self.rz[d].astype(f32)
        self.half[...] = value
        self.step = [self.links.start(self.half, self.rg, self.cube["grp"])]

    def done(self):
        self.wait()
        self.total[...] = self.half[...] + self.rg[...]


def fold(tiles):
    wide, mid, rest = tiles
    lanes = lax.broadcasted_iota(jnp.int32, (8, 128), 1)
    rows = lax.broadcasted_iota(jnp.int32, (8, 128), 0)
    tail = jnp.zeros((8, 128), f32)
    for n in range(4):
        piece = rest[8 * n : 8 * n + 8]
        piece = pltpu.roll(piece, 32 * n, 1) if n else piece
        tail = jnp.where((lanes >= 32 * n) & (lanes < 32 * n + 32), piece, tail)
    last = jnp.where(rows < 3, wide[24:32], jnp.where(rows < 6, pltpu.roll(mid[24:32], 3, 0), 0.0))
    return jnp.concatenate([wide[:24], mid[:24], tail, last], axis=0)


def unfold(rows):
    tail, last = rows[48:56], rows[56:64]
    rest = jnp.concatenate([tail] + [pltpu.roll(tail, 128 - 32 * n, 1) for n in range(1, 4)], axis=0)
    return [
        jnp.concatenate([rows[:24], last], axis=0),
        jnp.concatenate([rows[24:48], pltpu.roll(last, 5, 0)], axis=0),
        rest,
    ]


def choose(slots, place, blocks):
    value = None
    for i, block in enumerate(blocks):
        term = jnp.where(slots[0, i] == place, block, 0.0)
        value = term if value is None else value + term
    return value


def corner(slots, i):
    return slots[0, i] // GY, slots[0, i] % GY


def prepare(slots, count, feats, occupancy, cot, w_conv1, w_down, w_conv2, mask, coarse, mp, gp, shard_a, shard_b, tmp, wide):
    tmp[...] = jnp.zeros_like(tmp)
    wide[...] = jnp.zeros_like(wide)
    tmp[0, 0:27, 0:72] = w_conv1[...].astype(f32)
    wide[0:8, 0:144] = w_down[...].astype(f32)
    low = lane_tiles(wide[0:8, 0:256])
    for j in range(3):
        tmp[1, pl.ds(j, 8, stride=3), :] = relane(1, [(low, 48 * j, BASE_DOWN, 48)])[0]
    shard_a[...] = (tmp[0] + tmp[1]).astype(bf16)
    wide[0:27, 0:288] = w_conv2[...].astype(f32)
    shard_b[...] = fold(lane_tiles(wide[...])).astype(bf16)

    flags = []
    for p in range(GX * GY):
        flag = jnp.where(slots[0, 0] == p, 1.0, 0.0)
        for i in range(1, CAP):
            flag = flag + jnp.where((slots[0, i] == p) & (count[0] > i), 1.0, 0.0)
        flags.append(flag)

    def iotas(rows, lanes):
        return [lax.broadcasted_iota(jnp.int32, (rows, lanes), d) for d in range(2)]

    row, lane = iotas(256, 32)
    pick_y = jnp.where(row // 8 == lane, 1.0, 0.0).astype(bf16)
    row, lane = iotas(256, 8)
    pick_z = row % 8 == lane
    row, lane = iotas(128, 32)
    pair_y = jnp.where(row // 8 == lane // 2, 1.0, 0.0).astype(bf16)
    row, lane = iotas(128, 8)
    pair_z = row % 8 == lane // 2
    ones = jnp.ones((8, 256), bf16)
    mp[1:17, 1:33] = jnp.zeros((16, 32, 8, 128), f32)
    gp[1:9, 1:17] = jnp.zeros((8, 16, 8, 256), f32)
    for px in range(GX):

        def first(x, carry):
            plane = occupancy[0, x].astype(f32).astype(bf16)
            column = jnp.dot(pick_y, plane, preferred_element_type=f32)
            column = jnp.where(pick_z, column, 0.0).astype(bf16)
            value = jnp.dot(column, ones[:, :128], preferred_element_type=f32).reshape(32, 8, 128)
            for py in range(GY):
                at = slice(py * 8, py * 8 + 8)
                live = value[at] * flags[px * GY + py]
                mask[x, at] = live
                mp[1 + x, 1 + py * 8 : 9 + py * 8, :, 0:C1] = feats[0, x, at].astype(f32) * live[:, :, 0:C1]
            return carry

        def second(a, carry):
            plane = (occupancy[0, 2 * a] + occupancy[0, 2 * a + 1]).astype(f32).astype(bf16)
            column = jnp.dot(pair_y, plane, preferred_element_type=f32)
            column = jnp.where(pair_z, column, 0.0).astype(bf16)
            value = jnp.minimum(jnp.dot(column, ones, preferred_element_type=f32), 1.0).reshape(16, 8, 256)
            for py in range(GY):
                at = slice(py * 4, py * 4 + 4)
                live = value[at] * flags[px * GY + py]
                coarse[a, at] = live
                grad = cot[0, a, at].astype(f32) * live[:, 0:4, 0:C2]
                gp[1 + a, 1 + py * 4 : 5 + py * 4, 0:4, 0:C2] = grad
            return carry

        lax.fori_loop(px * 8, px * 8 + 8, first, 0)
        lax.fori_loop(px * 4, px * 4 + 4, second, 0)


def unpack_first(full, w9, wd, w1g, wdg, tmp):
    def unpack(a, carry):
        shards = []
        for b in range(4):
            value = full[a // 4, (a // 2) % 2, (a % 2) * 2 + b // 2, b % 2].astype(f32)
            tmp[b] = value
            shards.append([value])
        for k in range(3):
            w1g[pl.ds((a * 3 + k) * PITCH_W, 32), :] = to_row(shards, PIECES_ONE[k], 0, 1)[0]
        chunks = [[tmp[b, pl.ds(j, 8, stride=3), :]] for b in range(4) for j in range(3)]
        for k in range(3):
            segments = [(chunks[4 * k + n], BASE_DOWN, 48 * n, 48) for n in range(4)]
            for c, tile in enumerate(relane(2, segments)):
                wdg[c, pl.ds(pl.multiple_of((a * 3 + k) * 8, 8), 8), :] = tile
        return carry

    lax.fori_loop(0, GROUPS, unpack, 0)
    for t in range(27):
        k, oz = t // 3, t % 3
        w9[k * 128 : k * 128 + C1, oz * 128 : (oz + 1) * 128] = w1g[pl.ds(t, C1, stride=PITCH_W), :].astype(bf16)
    for k in range(9):
        w9[k * 128 + C1 : (k + 1) * 128, :] = jnp.zeros((128 - C1, 384), bf16)
    for t in range(8):
        for c in range(2):
            wd[t * 128 : t * 128 + C1, c * 128 : (c + 1) * 128] = wdg[c, pl.ds(t, C1, stride=8), :].astype(bf16)
        wd[t * 128 + C1 : (t + 1) * 128, :] = jnp.zeros((128 - C1, 256), bf16)


def unpack_second(full, w2, big):
    def unpack(a, carry):
        shards = [unfold(full[a // 4, (a // 2) % 2, (a % 2) * 2 + b // 2, b % 2].astype(f32)) for b in range(4)]
        for k in range(6):
            for c, tile in enumerate(to_row(shards, PIECES_TWO[k], 0, 2)):
                big[c, pl.ds((a * 6 + k) * PITCH_W, 32), :] = tile
        return carry

    lax.fori_loop(0, GROUPS, unpack, 0)

    def order(k, carry):
        for oz in range(3):
            for c in range(2):
                w2[pl.ds(pl.multiple_of(k * 256, 256), C2), oz * 256 + c * 128 : oz * 256 + (c + 1) * 128] = big[
                    c, pl.ds(k * 3 + oz, C2, stride=PITCH_W), :
                ].astype(bf16)
        w2[pl.ds(pl.multiple_of(k * 256 + C2, 64), 256 - C2), :] = jnp.zeros((256 - C2, 768), bf16)
        return carry

    lax.fori_loop(0, 9, order, 0)


def windows(dst, i, window, edge, flip):
    lanes = window.shape[-1]
    rows = edge * edge * 8
    for k in range(9):
        ox, oy = k // 3, k % 3
        if flip:
            ox, oy = 2 - ox, 2 - oy
        piece = window[ox : ox + edge, oy : oy + edge].reshape(rows, lanes)
        dst[i * rows : (i + 1) * rows, k * lanes : (k + 1) * lanes] = piece.astype(bf16)


def three(rows, lanes):
    return [rows[:, n * lanes : (n + 1) * lanes].reshape(-1, 8, lanes) for n in range(3)]


def conv(parts):
    low, mid, high = parts
    return (depth_shifts(low)[0] + mid + depth_shifts(high)[2]).reshape(-1, mid.shape[-1])


def spread(value):
    below, mid, above = depth_shifts(value.reshape(-1, 8, value.shape[-1]))
    return jnp.concatenate([v.reshape(value.shape).astype(bf16) for v in (above, mid, below)], axis=1)


def pack_first(packed, r1, rdn, tmp):
    tmp[...] = jnp.zeros_like(tmp)

    def pack(a, carry):
        segments = [[] for _ in range(4)]
        downs = []
        for k in range(3):
            ci = a * 3 + k
            tiles = [r1[pl.ds(ci, 32, stride=PITCH_S), :]]
            for s, at, lane, n in PIECES_ONE[k]:
                segments[s].append((tiles, lane, at, n))
            downs.append([rdn[c, pl.ds(ci, 8, stride=PITCH_S), :] for c in range(2)])
        for b in range(4):
            for j in range(3):
                m = 3 * b + j
                tmp[b, pl.ds(j, 8, stride=3), :] = relane(1, [(downs[m // 4], m % 4 * 48, BASE_DOWN, 48)])[0]
            value = relane(1, segments[b])[0] + tmp[b]
            packed[a // 4, (a // 2) % 2, (a % 2) * 2 + b // 2, b % 2] = value.astype(bf16)
        return carry

    lax.fori_loop(0, GROUPS, pack, 0)


def pack_second(packed, big):
    def pack(a, carry):
        segments = [[] for _ in range(4)]
        for k in range(6):
            tiles = [big[c, pl.ds(a * 6 + k, 32, stride=PITCH_R), :] for c in range(2)]
            for s, at, lane, n in PIECES_TWO[k]:
                segments[s].append((tiles, lane, at, n))
        for b in range(4):
            packed[a // 4, (a // 2) % 2, (a % 2) * 2 + b // 2, b % 2] = fold(relane(3, segments[b])).astype(bf16)
        return carry

    lax.fori_loop(0, GROUPS, pack, 0)


def whole_kernel(
    slots, count, feats, occupancy, cot, w_conv1, w_down, w_conv2, out, total_a, total_b,
    mask, coarse, shard_a, shard_b, wide,
    full_a, full_b, mp, gp, dp, x9, x2, x3, w9, wd, w2, w1g, wdg, tmp, big, act, pm, hs, gs, r1, rdn,
    packed_a, packed_b, sums_a, rd_a, ry2_a, ry1_a, rx_a, rz_a, half_a, rg_a,
    sums_b, rd_b, ry2_b, ry1_b, rx_b, rz_b, half_b, rg_b, send, recv, own,
):
    where = place()
    grp, tx, ty, hi, y, core = where
    cube = cube_peers(grp, tx, hi, y, core)
    around = halo_peers(grp, tx, ty)
    links = Links(send, recv)
    greeted = ring_peers(grp, tx, ty) + [cube[n] for n in ("core", "y1", "y3", "x", "grp")] + around
    barrier = pltpu.get_barrier_semaphore()
    for peer in greeted:
        pl.semaphore_signal(barrier, inc=1, device_id=peer, device_id_type=MESH)
    prepare(
        slots, count, feats, occupancy, cot, w_conv1, w_down, w_conv2, mask, coarse, mp, gp, shard_a, shard_b, tmp, wide
    )
    pl.semaphore_wait(barrier, len(greeted))

    first = Gather(links, where, shard_a, full_a, own.at[0])
    halo_m = links.halo(mp, mp, around, True)
    first.across()
    first.near()
    second = Gather(links, where, shard_b, full_b, own.at[1])
    halo_g = links.halo(gp, gp, around, True)
    for copy in halo_m:
        copy.wait_recv()
    clear_edges(mp, tx, ty)
    for i in range(CAP):
        px, py = corner(slots, i)
        windows(x9, i, mp[pl.ds(px * 8, 10), pl.ds(py * 8, 10)], 8, False)
    first.far()
    second.across()
    first.last()
    first.done()
    unpack_first(full_a, w9, wd, w1g, wdg, tmp)
    second.near()

    hs[...] = jnp.zeros_like(hs)
    downs = []
    for i in range(CAP):
        px, py = corner(slots, i)
        value = conv(three(jnp.dot(x9[i * 512 : (i + 1) * 512, :], w9[...], preferred_element_type=f32), 128))
        act[i * 512 : (i + 1) * 512, :] = value
        live = mask[pl.ds(px * 8, 8), pl.ds(py * 8, 8)].reshape(512, 128)
        hidden = (live * jax.nn.silu(value)).astype(bf16).astype(f32).reshape(4, 2, 4, 2, 8, 128)
        for p in range(2):
            for q in range(2):
                for b in range(4):
                    hs[:, p * 2 + q, b * 16 : b * 16 + 8, :] = hidden[:, p, b, q]
        for t in range(8):
            patch = hs[:, t // 2, pl.ds(t % 2, 32, stride=2), :].reshape(128, 128)
            pm[i * 128 : (i + 1) * 128, t * 128 : (t + 1) * 128] = patch.astype(bf16)
        raw = jnp.dot(pm[i * 128 : (i + 1) * 128, :], wd[...], preferred_element_type=f32)
        edge = coarse[pl.ds(px * 4, 4), pl.ds(py * 4, 4)]
        downs.append((edge * raw.reshape(4, 4, 8, 256)).astype(bf16).astype(f32))
    second.far()
    for p in range(GX * GY):
        px, py = p // GY, p % GY
        dp[1 + px * 4 : 5 + px * 4, 1 + py * 4 : 5 + py * 4] = choose(slots, p, downs)
    halo_d = links.halo(dp, dp, around, True)

    for copy in halo_g:
        copy.wait_recv()
    clear_edges(gp, tx, ty)
    grads, edges = [], []
    for i in range(CAP):
        px, py = corner(slots, i)
        windows(x3, i, gp[pl.ds(px * 4, 6), pl.ds(py * 4, 6)], 4, True)
        grads.append(gp[pl.ds(px * 4 + 1, 4), pl.ds(py * 4 + 1, 4)].reshape(128, 256))
        edges.append(coarse[pl.ds(px * 4, 4), pl.ds(py * 4, 4)].reshape(128, 256))
    grad_two = jnp.concatenate(grads, axis=0)
    edge = jnp.concatenate(edges, axis=0)
    spread_two = spread(grad_two)
    big[:, 27 * PITCH_R : 32 * PITCH_R, :] = jnp.zeros((2, 5 * PITCH_R, 128), f32)
    second.last()
    for copy in halo_d:
        copy.wait_recv()
    clear_edges(dp, tx, ty)
    for i in range(CAP):
        px, py = corner(slots, i)
        windows(x2, i, dp[pl.ds(px * 4, 6), pl.ds(py * 4, 6)], 4, False)
    for k in range(9):
        product = lax.dot_general(
            x2[:, k * 256 : (k + 1) * 256], spread_two, (((0,), (0,)), ((), ())), preferred_element_type=f32
        )
        for oz in range(3):
            for c in range(2):
                at = oz * 256 + c * 128
                big[c, (3 * k + oz) * PITCH_R : (3 * k + oz) * PITCH_R + 256, :] = product[:, at : at + 128]
    pack_second(packed_b, big)
    sum_b = Scatter(
        links, where, packed_b, total_b, sums_b, rd_b, ry2_b, ry1_b, rx_b, rz_b, half_b, rg_b
    )
    sum_b.cores()

    second.done()
    unpack_second(full_b, w2, big)
    sum_b.far()
    parts = []
    for oz in range(3):
        part = None
        for k in range(9):
            term = lax.dot_general(
                x3[:, k * 256 : (k + 1) * 256],
                w2[k * 256 : (k + 1) * 256, oz * 256 : (oz + 1) * 256],
                (((1,), (1,)), ((), ())),
                preferred_element_type=f32,
            )
            part = term if part is None else part + term
        parts.append(part.reshape(-1, 8, 256))
    back = conv(parts[::-1])
    grad_in = (grad_two + edge * back).astype(bf16)
    sum_b.near()

    rdn[...] = jnp.zeros_like(rdn)
    for t in range(8):
        product = lax.dot_general(
            pm[:, t * 128 : (t + 1) * 128], grad_in, (((0,), (0,)), ((), ())), preferred_element_type=f32
        )
        for c in range(2):
            rdn[c, t * PITCH_S : t * PITCH_S + 128, :] = product[:, c * 128 : (c + 1) * 128]
    spreads = []
    for i in range(CAP):
        px, py = corner(slots, i)
        for t in range(8):
            part = lax.dot_general(
                grad_in[i * 128 : (i + 1) * 128],
                wd[t * 128 : (t + 1) * 128, :],
                (((1,), (1,)), ((), ())),
                preferred_element_type=f32,
            )
            gs[:, t // 2, pl.ds(t % 2, 32, stride=2), :] = part.reshape(4, 32, 128)
        rows = []
        for p in range(2):
            for b in range(4):
                for q in range(2):
                    rows.append(gs[:, p * 2 + q, b * 16 : b * 16 + 8, :])
        hidden = jnp.stack(rows, axis=1).reshape(512, 128)
        live = mask[pl.ds(px * 8, 8), pl.ds(py * 8, 8)].reshape(512, 128)
        value = act[i * 512 : (i + 1) * 512, :]
        sig = jax.nn.sigmoid(value)
        spreads.append(spread(live * hidden * (sig * (1.0 + value * (1.0 - sig)))))
    spread_one = jnp.concatenate(spreads, axis=0)
    sum_b.across()
    r1[27 * PITCH_S : 32 * PITCH_S, :] = jnp.zeros((5 * PITCH_S, 128), f32)
    for k in range(9):
        product = lax.dot_general(
            x9[:, k * 128 : (k + 1) * 128], spread_one, (((0,), (0,)), ((), ())), preferred_element_type=f32
        )
        for oz in range(3):
            at = (3 * k + oz) * PITCH_S
            r1[at : at + 128, :] = product[:, oz * 128 : (oz + 1) * 128]
    pack_first(packed_a, r1, rdn, tmp)
    sum_a = Scatter(
        links, where, packed_a, total_a, sums_a, rd_a, ry2_a, ry1_a, rx_a, rz_a, half_a, rg_a
    )
    sum_a.cores()
    sum_b.along()

    value = conv(three(jnp.dot(x2[...], w2[...], preferred_element_type=f32), 256))
    blocks = []
    for i in range(CAP):
        px, py = corner(slots, i)
        down = dp[pl.ds(px * 4 + 1, 4), pl.ds(py * 4 + 1, 4)].reshape(128, 256)
        rows = slice(i * 128, (i + 1) * 128)
        blocks.append((edges[i] * (down + value[rows])).reshape(4, 4, 8, 256))
    sum_a.far()
    for p in range(GX * GY):
        px, py = p // GY, p % GY
        out[px * 4 : px * 4 + 4, py * 4 : py * 4 + 4] = choose(slots, p, blocks)
    sum_a.near()
    sum_b.swap()
    sum_a.across()
    sum_a.along()
    sum_b.done()
    sum_a.swap()
    sum_a.done()
    for copy in links.sent:
        copy.wait_send()


def whole(order, count, feats, occupancy, cot, w_conv1, w_down, w_conv2):
    def sums(rows):
        return [
            pltpu.VMEM((8, 2, 4, rows, 128), bf16),
            pltpu.VMEM((8, 2, 4, rows, 128), bf16),
            pltpu.VMEM((2, 8, 2, rows, 128), bf16),
            pltpu.VMEM((8, 2, rows, 128), bf16),
            pltpu.VMEM((8, rows, 128), bf16),
            pltpu.VMEM((7, rows, 128), bf16),
            pltpu.VMEM((rows, 128), f32),
            pltpu.VMEM((rows, 128), f32),
        ]

    copies = 2 * 23 + 24 + 2 * 19
    return pl.pallas_call(
        whole_kernel,
        in_specs=[pl.BlockSpec(memory_space=pltpu.SMEM)] * 2 + [pl.BlockSpec(memory_space=pltpu.VMEM)] * 6,
        out_specs=[pl.BlockSpec(memory_space=pltpu.VMEM)] * 3,
        out_shape=[
            jax.ShapeDtypeStruct((8, 16, 8, 256), f32),
            jax.ShapeDtypeStruct((32, 128), f32),
            jax.ShapeDtypeStruct((64, 128), f32),
        ],
        scratch_shapes=[
            pltpu.VMEM((16, 32, 8, 128), f32),
            pltpu.VMEM((8, 16, 8, 256), f32),
            pltpu.VMEM((32, 128), bf16),
            pltpu.VMEM((64, 128), bf16),
            pltpu.VMEM((32, 384), f32),
            pltpu.VMEM((8, 2, 4, 2, 32, 128), bf16),
            pltpu.VMEM((8, 2, 4, 2, 64, 128), bf16),
            pltpu.VMEM((18, 34, 8, 128), f32),
            pltpu.VMEM((10, 18, 8, 256), f32),
            pltpu.VMEM((10, 18, 8, 256), f32),
            pltpu.VMEM((1024, 9 * 128), bf16),
            pltpu.VMEM((256, 9 * 256), bf16),
            pltpu.VMEM((256, 9 * 256), bf16),
            pltpu.VMEM((9 * 128, 384), bf16),
            pltpu.VMEM((1024, 256), bf16),
            pltpu.VMEM((9 * 256, 768), bf16),
            pltpu.VMEM((C1 * PITCH_W + 8, 128), f32),
            pltpu.VMEM((2, C1 * 8, 128), f32),
            pltpu.VMEM((4, 32, 128), f32),
            pltpu.VMEM((2, 32 * PITCH_R, 128), f32),
            pltpu.VMEM((1024, 128), f32),
            pltpu.VMEM((256, 1024), bf16),
            pltpu.VMEM((4, 4, 64, 128), f32),
            pltpu.VMEM((4, 4, 64, 128), f32),
            pltpu.VMEM((32 * PITCH_S, 128), f32),
            pltpu.VMEM((2, 8 * PITCH_S, 128), f32),
            pltpu.VMEM((8, 2, 4, 2, 32, 128), bf16),
            pltpu.VMEM((8, 2, 4, 2, 64, 128), bf16),
        ]
        + sums(32)
        + sums(64)
        + [
            pltpu.SemaphoreType.DMA((copies,)),
            pltpu.SemaphoreType.DMA((copies,)),
            pltpu.SemaphoreType.DMA((2,)),
        ],
        compiler_params=pltpu.CompilerParams(collective_id=0, has_side_effects=True, vmem_limit_bytes=VMEM_LIMIT),
        name="whole",
    )(order, count, feats, occupancy, cot, w_conv1, w_down, w_conv2)


def local(features, voxel_mask, brick_order, brick_count, w_conv1, w_down, w_conv2, cotangent):
    out, total_a, total_b = whole(
        brick_order, brick_count, features, voxel_mask, cotangent, w_conv1, w_down, w_conv2
    )
    one = total_a[:27, :72]
    low = total_a[:24, 72:120].reshape(8, 144)
    main = jnp.concatenate([total_b[0:24], total_b[24:48]], axis=1)
    last = jnp.concatenate([total_b[56:59], total_b[59:62]], axis=1)
    rest = jnp.concatenate([total_b[48:56, 32 * n : 32 * n + 32] for n in range(4)], axis=0)
    two = jnp.concatenate([jnp.concatenate([main, last], axis=0), rest[:27]], axis=1)
    return out[None, :, :, :4, :C2].astype(bf16), one, low, two


def solution(mesh):
    return jax.shard_map(
        local,
        mesh=mesh,
        in_specs=(
            P("grp", "tx", "ty", None, None),
            P("grp", "tx", "ty", None),
            P(("grp", "tx", "ty"), None),
            P(("grp", "tx", "ty")),
            P(None, ("tx", "ty")),
            P(None, ("tx", "ty")),
            P(None, ("tx", "ty")),
            P("grp", "tx", "ty", None, None),
        ),
        out_specs=(
            P("grp", "tx", "ty", None, None),
            P(None, ("tx", "ty")),
            P(None, ("tx", "ty")),
            P(None, ("tx", "ty")),
        ),
        check_vma=False,
    )
```

```python
import jax
import jax.numpy as jnp
from jax import lax
from jax.experimental import pallas as pl
from jax.experimental.pallas import tpu as pltpu
from jax.sharding import PartitionSpec as P

C1 = 96
C2 = 192
GX = 2
GY = 4
CAP = 2
GROUPS = 32
N_TX = 8
N_TY = 16
PITCH_W = 33
PITCH_R = 264
PITCH_S = 136
MESH = pl.DeviceIdType.MESH
f32 = jnp.float32
bf16 = jnp.bfloat16
TAPS = [(ox, oy, oz) for ox in range(3) for oy in range(3) for oz in range(3)]
VMEM_LIMIT = 60 * 1024 * 1024


def lane_tiles(rows):
    return [rows[:, i * 128 : (i + 1) * 128] for i in range(rows.shape[1] // 128)]


def relane(count, segments):
    lanes = lax.broadcasted_iota(jnp.int32, segments[0][0][0].shape, 1)
    out = [None] * count
    rolled = {}
    for tiles, src, dst, length in segments:
        while length > 0:
            step = min(length, 128 - src % 128, 128 - dst % 128)
            tile, shift = tiles[src // 128], (dst - src) % 128
            key = (id(tile), shift)
            if key not in rolled:
                rolled[key] = pltpu.roll(tile, shift, 1) if shift else tile
            low, high, target = dst % 128, dst % 128 + step, dst // 128
            base = jnp.zeros_like(tile) if out[target] is None else out[target]
            if step == 128:
                out[target] = rolled[key]
            else:
                inside = lanes < high
                if low:
                    inside = inside & (lanes >= low)
                out[target] = jnp.where(inside, rolled[key], base)
            src, dst, length = src + step, dst + step, length - step
    return [jnp.zeros_like(segments[0][0][0]) if t is None else t for t in out]


PIECES_ONE = [[(0, 0, 0, 72), (1, 0, 72, 24)], [(1, 24, 0, 48), (2, 0, 48, 48)], [(2, 48, 0, 24), (3, 0, 24, 72)]]
PIECES_TWO = [
    [(0, 0, 0, 192)],
    [(0, 192, 0, 96), (1, 0, 96, 96)],
    [(1, 96, 0, 192)],
    [(2, 0, 0, 192)],
    [(2, 192, 0, 96), (3, 0, 96, 96)],
    [(3, 96, 0, 192)],
]
BASE_DOWN = 72


def to_row(shards, pieces, base, count):
    return relane(count, [(shards[s], base + a, b, n) for s, a, b, n in pieces])


def join(tiles):
    return tiles[0] if len(tiles) == 1 else jnp.concatenate(tiles, axis=1)


def depth_shifts(slab):
    axis = slab.ndim - 2
    depth = lax.broadcasted_iota(jnp.int32, slab.shape, axis)
    below = jnp.where(depth == 0, 0.0, pltpu.roll(slab, 1, axis))
    above = jnp.where(depth == 7, 0.0, pltpu.roll(slab, 7, axis))
    return below, slab, above


def barrier_with(peers):
    barrier = pltpu.get_barrier_semaphore()
    for peer in peers:
        pl.semaphore_signal(barrier, inc=1, device_id=peer, device_id_type=MESH)
    pl.semaphore_wait(barrier, len(peers))


def place():
    grp, tx, ty = lax.axis_index("grp"), lax.axis_index("tx"), lax.axis_index("ty")
    return grp, tx, ty, ty // 8, (ty // 2) % 4, ty % 2


def other(value, bits):
    if bits == 1:
        return value + 1 - 2 * (value % 2)
    if bits == 2:
        return (value + 2) % 4
    return 3 - value


def ring_peers(grp, tx, ty):
    return [(grp, (tx + d) % N_TX, ty) for d in range(1, N_TX)]


def cube_peers(grp, tx, hi, y, core):
    def ty_of(h, v, c):
        return h * 8 + v * 2 + c

    return {
        "core": (grp, tx, ty_of(hi, y, 1 - core)),
        "y1": (grp, tx, ty_of(hi, other(y, 1), core)),
        "y3": (grp, tx, ty_of(hi, other(y, 3), core)),
        "x": (1 - grp, tx, ty_of(1 - hi, y, core)),
        "grp": (1 - grp, tx, ty_of(hi, y, core)),
    }


STEPS = [(dx, dy) for dx in (-1, 0, 1) for dy in (-1, 0, 1) if dx or dy]


def halo_peers(grp, tx, ty):
    return [(grp, (tx + dx + N_TX) % N_TX, (ty + dy + N_TY) % N_TY) for dx, dy in STEPS]


def edge_out(step, size, shift):
    return pl.ds(shift, 1) if step < 0 else pl.ds(size - 1 + shift, 1) if step > 0 else pl.ds(shift, size)


def edge_in(step, size):
    return pl.ds(size + 1, 1) if step < 0 else pl.ds(0, 1) if step > 0 else pl.ds(1, size)


def clear_edges(dst, tx, ty):
    size_x, size_y = dst.shape[0], dst.shape[1]

    @pl.when(tx == 0)
    def _():
        dst[0:1] = jnp.zeros((1,) + dst.shape[1:], dst.dtype)

    @pl.when(tx == N_TX - 1)
    def _():
        dst[size_x - 1 : size_x] = jnp.zeros((1,) + dst.shape[1:], dst.dtype)

    @pl.when(ty == 0)
    def _():
        dst[:, 0:1] = jnp.zeros((size_x, 1) + dst.shape[2:], dst.dtype)

    @pl.when(ty == N_TY - 1)
    def _():
        dst[:, size_y - 1 : size_y] = jnp.zeros((size_x, 1) + dst.shape[2:], dst.dtype)


class Links:
    def __init__(self, send, recv):
        self.send, self.recv, self.sent = send, recv, []

    def start(self, src, dst, peer):
        k = len(self.sent)
        copy = pltpu.make_async_remote_copy(
            src_ref=src,
            dst_ref=dst,
            send_sem=self.send.at[k],
            recv_sem=self.recv.at[k],
            device_id=peer,
            device_id_type=MESH,
        )
        copy.start()
        self.sent.append(copy)
        return copy

    def halo(self, src, dst, peers, inside):
        size_x, size_y = dst.shape[0] - 2, dst.shape[1] - 2
        shift = 1 if inside else 0
        copies = []
        for peer, (dx, dy) in zip(peers, STEPS):
            copies.append(
                self.start(
                    src.at[edge_out(dx, size_x, shift), edge_out(dy, size_y, shift)],
                    dst.at[edge_in(dx, size_x), edge_in(dy, size_y)],
                    peer,
                )
            )
        return copies


def halves(rows):
    return pl.ds(0, rows // 2), pl.ds(rows // 2, rows // 2)


class Gather:
    def __init__(self, links, where, shard, full, own):
        self.links, self.where, self.full = links, where, full
        self.first, self.second = halves(shard.shape[0])
        grp, tx, ty, hi, y, core = where
        self.cube = cube_peers(grp, tx, hi, y, core)
        mine = full.at[tx, hi, y, core]
        self.line = [links.start(shard, mine, peer) for peer in ring_peers(grp, tx, ty)]
        self.own = pltpu.make_async_copy(shard, mine, own)
        self.own.start()
        self.partner = []

    def part(self, v, rows):
        return self.full.at[:, :, v, self.where[5], rows]

    def to_core(self, ref):
        self.partner.append(self.links.start(ref, ref, self.cube["core"]))

    def across(self):
        grp, tx, ty, hi, y, core = self.where
        self.own.wait()
        for copy in self.line:
            copy.wait_recv()
        column = self.full.at[:, hi, y, core]
        self.step = [self.links.start(column, column, self.cube["x"])]
        self.to_core(column)

    def near(self):
        grp, tx, ty, hi, y, core = self.where
        for copy in self.step:
            copy.wait_recv()
        first, second = self.part(y, self.first), self.part(y, self.second)
        self.step = [
            self.links.start(first, first, self.cube["y1"]),
            self.links.start(second, second, self.cube["y3"]),
        ]
        self.to_core(self.full.at[:, 1 - hi, y, core])

    def far(self):
        y = self.where[4]
        y1, y3 = other(y, 1), other(y, 3)
        for copy in self.step:
            copy.wait_recv()
        self.step = []
        for v, rows, name in ((y, self.first, "y3"), (y1, self.first, "y3"), (y, self.second, "y1"), (y3, self.second, "y1")):
            self.step.append(self.links.start(self.part(v, rows), self.part(v, rows), self.cube[name]))
        self.to_core(self.part(y1, self.first))
        self.to_core(self.part(y3, self.second))

    def last(self):
        y = self.where[4]
        y1, y2, y3 = other(y, 1), other(y, 2), other(y, 3)
        arrived = [(y3, self.first), (y2, self.first), (y1, self.second), (y2, self.second)]
        for copy, (v, rows) in zip(self.step, arrived):
            copy.wait_recv()
            self.to_core(self.part(v, rows))

    def done(self):
        for copy in self.partner:
            copy.wait_recv()


class Scatter:
    def __init__(self, links, where, packed, total, sums, rd, ry2, ry1, rx, rz, half, rg):
        self.links, self.where, self.packed, self.total = links, where, packed, total
        self.sums, self.rd, self.ry2, self.ry1 = sums, rd, ry2, ry1
        self.rx, self.rz, self.half, self.rg = rx, rz, half, rg
        grp, tx, ty, hi, y, core = where
        self.cube = cube_peers(grp, tx, hi, y, core)
        self.line = ring_peers(grp, tx, ty)
        rows = half.shape[0]
        self.whole, (self.first, self.second) = pl.ds(0, rows), halves(rows)
        self.ys = [other(y, 2), other(y, 3), other(y, 1), y]

    def add(self, z, h, v, rows, left, right):
        both = left[...].astype(f32) + right[...].astype(f32)
        self.sums[z, h, v, rows, :] = both.astype(bf16)

    def part(self, v, rows):
        return self.sums.at[:, :, v, rows]

    def wait(self):
        for copy in self.step:
            copy.wait_recv()

    def cores(self):
        core = self.where[5]
        self.step = [
            self.links.start(self.packed.at[:, :, v, 1 - core], self.rd.at[:, :, v], self.cube["core"])
            for v in self.ys
        ]

    def far(self):
        core = self.where[5]
        y2, y3, y1, y = self.ys
        pieces, self.step = self.step, []
        for k, (copy, v) in enumerate(zip(pieces, self.ys)):
            copy.wait_recv()

            def take(z, carry):
                for h in range(2):
                    self.add(z, h, v, self.whole, self.packed.at[z, h, v, core], self.rd.at[z, h, v])
                return carry

            lax.fori_loop(0, 8, take, 0)
            if k in (1, 2):
                rows, name = (self.first, "y3") if k == 1 else (self.second, "y1")
                for n, u in enumerate((v, y2)):
                    self.step.append(
                        self.links.start(self.part(u, rows), self.ry2.at[n, :, :, rows], self.cube[name])
                    )

    def near(self):
        y2, y3, y1, y = self.ys
        self.wait()

        def take(z, carry):
            for h in range(2):
                self.add(z, h, y, self.whole, self.sums.at[z, h, y], self.ry2.at[0, z, h])
                self.add(z, h, y1, self.first, self.sums.at[z, h, y1, self.first], self.ry2.at[1, z, h, self.first])
                self.add(z, h, y3, self.second, self.sums.at[z, h, y3, self.second], self.ry2.at[1, z, h, self.second])
            return carry

        lax.fori_loop(0, 8, take, 0)
        self.step = [
            self.links.start(self.part(y1, self.first), self.ry1.at[:, :, self.first], self.cube["y1"]),
            self.links.start(self.part(y3, self.second), self.ry1.at[:, :, self.second], self.cube["y3"]),
        ]

    def across(self):
        hi, y = self.where[3], self.where[4]
        self.wait()

        def take(z, carry):
            for h in range(2):
                self.add(z, h, y, self.whole, self.sums.at[z, h, y], self.ry1.at[z, h])
            return carry

        lax.fori_loop(0, 8, take, 0)
        self.step = [self.links.start(self.sums.at[:, 1 - hi, y], self.rx, self.cube["x"])]

    def along(self):
        tx, hi, y = self.where[1], self.where[3], self.where[4]
        self.wait()

        def take(z, carry):
            self.add(z, hi, y, self.whole, self.sums.at[z, hi, y], self.rx.at[z])
            return carry

        lax.fori_loop(0, 8, take, 0)
        self.step = [
            self.links.start(self.sums.at[(tx + d + 1) % N_TX, hi, y], self.rz.at[d], peer)
            for d, peer in enumerate(self.line)
        ]

    def swap(self):
        tx, hi, y = self.where[1], self.where[3], self.where[4]
        self.wait()
        value = self.sums[tx, hi, y].astype(f32)
        for d in range(N_TX - 1):
            value = value + self.rz[d].astype(f32)
        self.half[...] = value
        self.step = [self.links.start(self.half, self.rg, self.cube["grp"])]

    def done(self):
        self.wait()
        self.total[...] = self.half[...] + self.rg[...]


def fold(tiles):
    wide, mid, rest = tiles
    lanes = lax.broadcasted_iota(jnp.int32, (8, 128), 1)
    rows = lax.broadcasted_iota(jnp.int32, (8, 128), 0)
    tail = jnp.zeros((8, 128), f32)
    for n in range(4):
        piece = rest[8 * n : 8 * n + 8]
        piece = pltpu.roll(piece, 32 * n, 1) if n else piece
        tail = jnp.where((lanes >= 32 * n) & (lanes < 32 * n + 32), piece, tail)
    last = jnp.where(rows < 3, wide[24:32], jnp.where(rows < 6, pltpu.roll(mid[24:32], 3, 0), 0.0))
    return jnp.concatenate([wide[:24], mid[:24], tail, last], axis=0)


def unfold(rows):
    tail, last = rows[48:56], rows[56:64]
    rest = jnp.concatenate([tail] + [pltpu.roll(tail, 128 - 32 * n, 1) for n in range(1, 4)], axis=0)
    return [
        jnp.concatenate([rows[:24], last], axis=0),
        jnp.concatenate([rows[24:48], pltpu.roll(last, 5, 0)], axis=0),
        rest,
    ]


def choose(slots, place, blocks):
    value = None
    for i, block in enumerate(blocks):
        term = jnp.where(slots[0, i] == place, block, 0.0)
        value = term if value is None else value + term
    return value


def corner(slots, i):
    return slots[0, i] // GY, slots[0, i] % GY


def pack_shards(w_conv1, w_down, w_conv2, shard_a, shard_b, tmp, wide):
    tmp[...] = jnp.zeros_like(tmp)
    wide[...] = jnp.zeros_like(wide)
    tmp[0, 0:27, 0:72] = w_conv1[...].astype(f32)
    wide[0:8, 0:144] = w_down[...].astype(f32)
    low = lane_tiles(wide[0:8, 0:256])
    for j in range(3):
        tmp[1, pl.ds(j, 8, stride=3), :] = relane(1, [(low, 48 * j, BASE_DOWN, 48)])[0]
    shard_a[...] = (tmp[0] + tmp[1]).astype(bf16)
    wide[0:27, 0:288] = w_conv2[...].astype(f32)
    shard_b[...] = fold(lane_tiles(wide[...])).astype(bf16)


def prepare(slots, count, feats, occupancy, cot, mask, coarse, mp, gp):
    flags = []
    for p in range(GX * GY):
        flag = jnp.where(slots[0, 0] == p, 1.0, 0.0)
        for i in range(1, CAP):
            flag = flag + jnp.where((slots[0, i] == p) & (count[0] > i), 1.0, 0.0)
        flags.append(flag)

    def iotas(rows, lanes):
        return [lax.broadcasted_iota(jnp.int32, (rows, lanes), d) for d in range(2)]

    row, lane = iotas(256, 8)
    pick_z = jnp.where(row % 8 == lane, 1.0, 0.0).astype(bf16)
    row, lane = iotas(256, 32)
    pick_y = row // 8 == lane
    row, lane = iotas(128, 8)
    pair_z = jnp.where(row % 8 == lane // 2, 1.0, 0.0).astype(bf16)
    row, lane = iotas(128, 32)
    pair_y = row // 8 == lane // 2
    ones = jnp.ones((32, 256), bf16)
    mp[1:17, 1:33] = jnp.zeros((16, 32, 8, 128), f32)
    gp[1:9, 1:17] = jnp.zeros((8, 16, 8, 256), f32)
    for px in range(GX):

        def first(x, carry):
            plane = occupancy[0, x].astype(f32).astype(bf16)
            column = jnp.dot(pick_z, plane, preferred_element_type=f32)
            column = jnp.where(pick_y, column, 0.0).astype(bf16)
            value = jnp.dot(column, ones[:, :128], preferred_element_type=f32).reshape(32, 8, 128)
            for py in range(GY):
                at = slice(py * 8, py * 8 + 8)
                live = value[at] * flags[px * GY + py]
                mask[x, at] = live
                mp[1 + x, 1 + py * 8 : 9 + py * 8, :, 0:C1] = feats[0, x, at].astype(f32) * live[:, :, 0:C1]
            return carry

        def second(a, carry):
            plane = (occupancy[0, 2 * a] + occupancy[0, 2 * a + 1]).astype(f32).astype(bf16)
            column = jnp.dot(pair_z, plane, preferred_element_type=f32)
            column = jnp.where(pair_y, column, 0.0).astype(bf16)
            value = jnp.minimum(jnp.dot(column, ones, preferred_element_type=f32), 1.0).reshape(16, 8, 256)
            for py in range(GY):
                at = slice(py * 4, py * 4 + 4)
                live = value[at] * flags[px * GY + py]
                coarse[a, at] = live
                grad = cot[0, a, at].astype(f32) * live[:, 0:4, 0:C2]
                gp[1 + a, 1 + py * 4 : 5 + py * 4, 0:4, 0:C2] = grad
            return carry

        lax.fori_loop(px * 8, px * 8 + 8, first, 0, unroll=4)
        lax.fori_loop(px * 4, px * 4 + 4, second, 0, unroll=4)


def unpack_first(full, w9, wd, w1g, wdg, tmp):
    def unpack(a, carry):
        shards = []
        for b in range(4):
            value = full[a // 4, (a // 2) % 2, (a % 2) * 2 + b // 2, b % 2].astype(f32)
            tmp[b] = value
            shards.append([value])
        for k in range(3):
            w1g[pl.ds((a * 3 + k) * PITCH_W, 32), :] = to_row(shards, PIECES_ONE[k], 0, 1)[0]
        chunks = [[tmp[b, pl.ds(j, 8, stride=3), :]] for b in range(4) for j in range(3)]
        for k in range(3):
            segments = [(chunks[4 * k + n], BASE_DOWN, 48 * n, 48) for n in range(4)]
            for c, tile in enumerate(relane(2, segments)):
                wdg[c, pl.ds(pl.multiple_of((a * 3 + k) * 8, 8), 8), :] = tile
        return carry

    lax.fori_loop(0, GROUPS, unpack, 0, unroll=4)
    for t in range(27):
        k, oz = t // 3, t % 3
        w9[k * 128 : k * 128 + C1, oz * 128 : (oz + 1) * 128] = w1g[pl.ds(t, C1, stride=PITCH_W), :].astype(bf16)
    for k in range(9):
        w9[k * 128 + C1 : (k + 1) * 128, :] = jnp.zeros((128 - C1, 384), bf16)
    for t in range(8):
        for c in range(2):
            wd[t * 128 : t * 128 + C1, c * 128 : (c + 1) * 128] = wdg[c, pl.ds(t, C1, stride=8), :].astype(bf16)
        wd[t * 128 + C1 : (t + 1) * 128, :] = jnp.zeros((128 - C1, 256), bf16)


def unpack_second(full, w2, big):
    def unpack(a, carry):
        shards = [unfold(full[a // 4, (a // 2) % 2, (a % 2) * 2 + b // 2, b % 2].astype(f32)) for b in range(4)]
        for k in range(6):
            for c, tile in enumerate(to_row(shards, PIECES_TWO[k], 0, 2)):
                big[c, pl.ds((a * 6 + k) * PITCH_W, 32), :] = tile
        return carry

    lax.fori_loop(0, GROUPS, unpack, 0, unroll=4)

    def order(k, carry):
        for oz in range(3):
            for c in range(2):
                w2[pl.ds(pl.multiple_of(k * 256, 256), C2), oz * 256 + c * 128 : oz * 256 + (c + 1) * 128] = big[
                    c, pl.ds(k * 3 + oz, C2, stride=PITCH_W), :
                ].astype(bf16)
        w2[pl.ds(pl.multiple_of(k * 256 + C2, 64), 256 - C2), :] = jnp.zeros((256 - C2, 768), bf16)
        return carry

    lax.fori_loop(0, 9, order, 0, unroll=3)


def windows(dst, i, window, edge, flip):
    lanes = window.shape[-1]
    rows = edge * edge * 8
    for k in range(9):
        ox, oy = k // 3, k % 3
        if flip:
            ox, oy = 2 - ox, 2 - oy
        piece = window[ox : ox + edge, oy : oy + edge].reshape(rows, lanes)
        dst[i * rows : (i + 1) * rows, k * lanes : (k + 1) * lanes] = piece.astype(bf16)


def three(rows, lanes):
    return [rows[:, n * lanes : (n + 1) * lanes].reshape(-1, 8, lanes) for n in range(3)]


def conv(parts):
    low, mid, high = parts
    return (depth_shifts(low)[0] + mid + depth_shifts(high)[2]).reshape(-1, mid.shape[-1])


def spread(value):
    below, mid, above = depth_shifts(value.reshape(-1, 8, value.shape[-1]))
    return jnp.concatenate([v.reshape(value.shape).astype(bf16) for v in (above, mid, below)], axis=1)


def pack_first(packed, r1, rdn, tmp):
    tmp[...] = jnp.zeros_like(tmp)

    def pack(a, carry):
        segments = [[] for _ in range(4)]
        downs = []
        for k in range(3):
            ci = a * 3 + k
            tiles = [r1[pl.ds(ci, 32, stride=PITCH_S), :]]
            for s, at, lane, n in PIECES_ONE[k]:
                segments[s].append((tiles, lane, at, n))
            downs.append([rdn[c, pl.ds(ci, 8, stride=PITCH_S), :] for c in range(2)])
        for b in range(4):
            for j in range(3):
                m = 3 * b + j
                tmp[b, pl.ds(j, 8, stride=3), :] = relane(1, [(downs[m // 4], m % 4 * 48, BASE_DOWN, 48)])[0]
            value = relane(1, segments[b])[0] + tmp[b]
            packed[a // 4, (a // 2) % 2, (a % 2) * 2 + b // 2, b % 2] = value.astype(bf16)
        return carry

    lax.fori_loop(0, GROUPS, pack, 0, unroll=4)


def pack_second(packed, big):
    def pack(a, carry):
        segments = [[] for _ in range(4)]
        for k in range(6):
            tiles = [big[c, pl.ds(a * 6 + k, 32, stride=PITCH_R), :] for c in range(2)]
            for s, at, lane, n in PIECES_TWO[k]:
                segments[s].append((tiles, lane, at, n))
        for b in range(4):
            packed[a // 4, (a // 2) % 2, (a % 2) * 2 + b // 2, b % 2] = fold(relane(3, segments[b])).astype(bf16)
        return carry

    lax.fori_loop(0, GROUPS, pack, 0, unroll=4)


def whole_kernel(
    slots, count, feats, occupancy, cot, w_conv1, w_down, w_conv2, out, grad_conv1, grad_down, grad_conv2,
    total_a, total_b, mask, coarse, shard_a, shard_b, wide,
    full_a, full_b, mp, gp, dp, x9, x2, x3, w9, wd, w2, w1g, wdg, tmp, big, act, pm, hs, gs, r1, rdn,
    packed_a, packed_b, sums_a, rd_a, ry2_a, ry1_a, rx_a, rz_a, half_a, rg_a,
    sums_b, rd_b, ry2_b, ry1_b, rx_b, rz_b, half_b, rg_b, send, recv, own,
):
    where = place()
    grp, tx, ty, hi, y, core = where
    cube = cube_peers(grp, tx, hi, y, core)
    around = halo_peers(grp, tx, ty)
    links = Links(send, recv)
    greeted = ring_peers(grp, tx, ty) + [cube[n] for n in ("core", "y1", "y3", "x", "grp")] + around
    barrier = pltpu.get_barrier_semaphore()
    for peer in greeted:
        pl.semaphore_signal(barrier, inc=1, device_id=peer, device_id_type=MESH)
    pack_shards(w_conv1, w_down, w_conv2, shard_a, shard_b, tmp, wide)
    pl.semaphore_wait(barrier, len(greeted))

    first = Gather(links, where, shard_a, full_a, own.at[0])
    second = Gather(links, where, shard_b, full_b, own.at[1])
    prepare(slots, count, feats, occupancy, cot, mask, coarse, mp, gp)
    first.across()
    halo_m = links.halo(mp, mp, around, True)
    halo_g = links.halo(gp, gp, around, True)
    first.near()
    second.across()
    for copy in halo_m:
        copy.wait_recv()
    clear_edges(mp, tx, ty)
    for i in range(CAP):
        px, py = corner(slots, i)
        windows(x9, i, mp[pl.ds(px * 8, 10), pl.ds(py * 8, 10)], 8, False)
    first.far()
    second.near()
    first.last()
    first.done()
    unpack_first(full_a, w9, wd, w1g, wdg, tmp)
    second.far()

    hs[...] = jnp.zeros_like(hs)
    downs = []
    for i in range(CAP):
        px, py = corner(slots, i)
        value = conv(three(jnp.dot(x9[i * 512 : (i + 1) * 512, :], w9[...], preferred_element_type=f32), 128))
        act[i * 512 : (i + 1) * 512, :] = value
        live = mask[pl.ds(px * 8, 8), pl.ds(py * 8, 8)].reshape(512, 128)
        hidden = (live * jax.nn.silu(value)).astype(bf16).astype(f32).reshape(4, 2, 4, 2, 8, 128)
        for p in range(2):
            for q in range(2):
                for b in range(4):
                    hs[:, p * 2 + q, b * 16 : b * 16 + 8, :] = hidden[:, p, b, q]
        for t in range(8):
            patch = hs[:, t // 2, pl.ds(t % 2, 32, stride=2), :].reshape(128, 128)
            pm[i * 128 : (i + 1) * 128, t * 128 : (t + 1) * 128] = patch.astype(bf16)
        raw = jnp.dot(pm[i * 128 : (i + 1) * 128, :], wd[...], preferred_element_type=f32)
        edge = coarse[pl.ds(px * 4, 4), pl.ds(py * 4, 4)]
        downs.append((edge * raw.reshape(4, 4, 8, 256)).astype(bf16).astype(f32))
    second.last()
    for p in range(GX * GY):
        px, py = p // GY, p % GY
        dp[1 + px * 4 : 5 + px * 4, 1 + py * 4 : 5 + py * 4] = choose(slots, p, downs)
    halo_d = links.halo(dp, dp, around, True)

    for copy in halo_g:
        copy.wait_recv()
    clear_edges(gp, tx, ty)
    grads, edges = [], []
    for i in range(CAP):
        px, py = corner(slots, i)
        windows(x3, i, gp[pl.ds(px * 4, 6), pl.ds(py * 4, 6)], 4, True)
        grads.append(gp[pl.ds(px * 4 + 1, 4), pl.ds(py * 4 + 1, 4)].reshape(128, 256))
        edges.append(coarse[pl.ds(px * 4, 4), pl.ds(py * 4, 4)].reshape(128, 256))
    grad_two = jnp.concatenate(grads, axis=0)
    edge = jnp.concatenate(edges, axis=0)
    spread_two = spread(grad_two)
    big[:, 27 * PITCH_R : 32 * PITCH_R, :] = jnp.zeros((2, 5 * PITCH_R, 128), f32)
    second.done()
    unpack_second(full_b, w2, big)
    for copy in halo_d:
        copy.wait_recv()
    clear_edges(dp, tx, ty)
    for i in range(CAP):
        px, py = corner(slots, i)
        windows(x2, i, dp[pl.ds(px * 4, 6), pl.ds(py * 4, 6)], 4, False)
    for k in range(9):
        product = lax.dot_general(
            x2[:, k * 256 : (k + 1) * 256], spread_two, (((0,), (0,)), ((), ())), preferred_element_type=f32
        )
        for oz in range(3):
            for c in range(2):
                at = oz * 256 + c * 128
                big[c, (3 * k + oz) * PITCH_R : (3 * k + oz) * PITCH_R + 256, :] = product[:, at : at + 128]
    pack_second(packed_b, big)
    sum_b = Scatter(
        links, where, packed_b, total_b, sums_b, rd_b, ry2_b, ry1_b, rx_b, rz_b, half_b, rg_b
    )
    sum_b.cores()

    parts = []
    for oz in range(3):
        part = None
        for k in range(9):
            term = lax.dot_general(
                x3[:, k * 256 : (k + 1) * 256],
                w2[k * 256 : (k + 1) * 256, oz * 256 : (oz + 1) * 256],
                (((1,), (1,)), ((), ())),
                preferred_element_type=f32,
            )
            part = term if part is None else part + term
        parts.append(part.reshape(-1, 8, 256))
    back = conv(parts[::-1])
    grad_in = (grad_two + edge * back).astype(bf16)
    sum_b.far()

    rdn[...] = jnp.zeros_like(rdn)
    for t in range(8):
        product = lax.dot_general(
            pm[:, t * 128 : (t + 1) * 128], grad_in, (((0,), (0,)), ((), ())), preferred_element_type=f32
        )
        for c in range(2):
            rdn[c, t * PITCH_S : t * PITCH_S + 128, :] = product[:, c * 128 : (c + 1) * 128]
    spreads = []
    for i in range(CAP):
        px, py = corner(slots, i)
        for t in range(8):
            part = lax.dot_general(
                grad_in[i * 128 : (i + 1) * 128],
                wd[t * 128 : (t + 1) * 128, :],
                (((1,), (1,)), ((), ())),
                preferred_element_type=f32,
            )
            gs[:, t // 2, pl.ds(t % 2, 32, stride=2), :] = part.reshape(4, 32, 128)
        rows = []
        for p in range(2):
            for b in range(4):
                for q in range(2):
                    rows.append(gs[:, p * 2 + q, b * 16 : b * 16 + 8, :])
        hidden = jnp.stack(rows, axis=1).reshape(512, 128)
        live = mask[pl.ds(px * 8, 8), pl.ds(py * 8, 8)].reshape(512, 128)
        value = act[i * 512 : (i + 1) * 512, :]
        sig = jax.nn.sigmoid(value)
        spreads.append(spread(live * hidden * (sig * (1.0 + value * (1.0 - sig)))))
    spread_one = jnp.concatenate(spreads, axis=0)
    sum_b.near()
    r1[27 * PITCH_S : 32 * PITCH_S, :] = jnp.zeros((5 * PITCH_S, 128), f32)
    for k in range(9):
        product = lax.dot_general(
            x9[:, k * 128 : (k + 1) * 128], spread_one, (((0,), (0,)), ((), ())), preferred_element_type=f32
        )
        for oz in range(3):
            at = (3 * k + oz) * PITCH_S
            r1[at : at + 128, :] = product[:, oz * 128 : (oz + 1) * 128]
    pack_first(packed_a, r1, rdn, tmp)
    sum_a = Scatter(
        links, where, packed_a, total_a, sums_a, rd_a, ry2_a, ry1_a, rx_a, rz_a, half_a, rg_a
    )
    sum_a.cores()
    sum_b.across()

    value = conv(three(jnp.dot(x2[...], w2[...], preferred_element_type=f32), 256))
    blocks = []
    for i in range(CAP):
        px, py = corner(slots, i)
        down = dp[pl.ds(px * 4 + 1, 4), pl.ds(py * 4 + 1, 4)].reshape(128, 256)
        rows = slice(i * 128, (i + 1) * 128)
        blocks.append((edges[i] * (down + value[rows])).reshape(4, 4, 8, 256))
    sum_a.far()
    sum_b.along()
    for p in range(GX * GY):
        px, py = p // GY, p % GY
        out[0, px * 4 : px * 4 + 4, py * 4 : py * 4 + 4] = choose(slots, p, blocks)[:, :, 0:4, 0:C2].astype(bf16)
    sum_a.near()
    sum_a.across()
    sum_b.swap()
    sum_a.along()
    sum_b.done()
    wide = unfold(total_b[...])
    grad_conv2[:, 0:256] = jnp.concatenate(wide[:2], axis=1)[:27]
    grad_conv2[:, 256:288] = wide[2][:27, :32]
    sum_a.swap()
    sum_a.done()
    grad_conv1[...] = total_a[:27, :72]
    low = [(total_a[pl.ds(j, 8, stride=3), :],) for j in range(3)]
    low = relane(2, [(low[j], BASE_DOWN, 48 * j, 48) for j in range(3)])
    grad_down[:, 0:128] = low[0]
    grad_down[:, 128:144] = low[1][:, :16]
    for copy in links.sent:
        copy.wait_send()


def whole(order, count, feats, occupancy, cot, w_conv1, w_down, w_conv2):
    def sums(rows):
        return [
            pltpu.VMEM((8, 2, 4, rows, 128), bf16),
            pltpu.VMEM((8, 2, 4, rows, 128), bf16),
            pltpu.VMEM((2, 8, 2, rows, 128), bf16),
            pltpu.VMEM((8, 2, rows, 128), bf16),
            pltpu.VMEM((8, rows, 128), bf16),
            pltpu.VMEM((7, rows, 128), bf16),
            pltpu.VMEM((rows, 128), f32),
            pltpu.VMEM((rows, 128), f32),
        ]

    copies = 2 * 23 + 24 + 2 * 19
    return pl.pallas_call(
        whole_kernel,
        in_specs=[pl.BlockSpec(memory_space=pltpu.SMEM)] * 2 + [pl.BlockSpec(memory_space=pltpu.VMEM)] * 6,
        out_specs=[pl.BlockSpec(memory_space=pltpu.VMEM)] * 4,
        out_shape=[
            jax.ShapeDtypeStruct((1, 8, 16, 4, C2), bf16),
            jax.ShapeDtypeStruct((27, 72), f32),
            jax.ShapeDtypeStruct((8, 144), f32),
            jax.ShapeDtypeStruct((27, 288), f32),
        ],
        scratch_shapes=[
            pltpu.VMEM((32, 128), f32),
            pltpu.VMEM((64, 128), f32),
            pltpu.VMEM((16, 32, 8, 128), f32),
            pltpu.VMEM((8, 16, 8, 256), f32),
            pltpu.VMEM((32, 128), bf16),
            pltpu.VMEM((64, 128), bf16),
            pltpu.VMEM((32, 384), f32),
            pltpu.VMEM((8, 2, 4, 2, 32, 128), bf16),
            pltpu.VMEM((8, 2, 4, 2, 64, 128), bf16),
            pltpu.VMEM((18, 34, 8, 128), f32),
            pltpu.VMEM((10, 18, 8, 256), f32),
            pltpu.VMEM((10, 18, 8, 256), f32),
            pltpu.VMEM((1024, 9 * 128), bf16),
            pltpu.VMEM((256, 9 * 256), bf16),
            pltpu.VMEM((256, 9 * 256), bf16),
            pltpu.VMEM((9 * 128, 384), bf16),
            pltpu.VMEM((1024, 256), bf16),
            pltpu.VMEM((9 * 256, 768), bf16),
            pltpu.VMEM((C1 * PITCH_W + 8, 128), f32),
            pltpu.VMEM((2, C1 * 8, 128), f32),
            pltpu.VMEM((4, 32, 128), f32),
            pltpu.VMEM((2, 32 * PITCH_R, 128), f32),
            pltpu.VMEM((1024, 128), f32),
            pltpu.VMEM((256, 1024), bf16),
            pltpu.VMEM((4, 4, 64, 128), f32),
            pltpu.VMEM((4, 4, 64, 128), f32),
            pltpu.VMEM((32 * PITCH_S, 128), f32),
            pltpu.VMEM((2, 8 * PITCH_S, 128), f32),
            pltpu.VMEM((8, 2, 4, 2, 32, 128), bf16),
            pltpu.VMEM((8, 2, 4, 2, 64, 128), bf16),
        ]
        + sums(32)
        + sums(64)
        + [
            pltpu.SemaphoreType.DMA((copies,)),
            pltpu.SemaphoreType.DMA((copies,)),
            pltpu.SemaphoreType.DMA((2,)),
        ],
        compiler_params=pltpu.CompilerParams(collective_id=0, has_side_effects=True, vmem_limit_bytes=VMEM_LIMIT),
        name="whole",
    )(order, count, feats, occupancy, cot, w_conv1, w_down, w_conv2)


def local(features, voxel_mask, brick_order, brick_count, w_conv1, w_down, w_conv2, cotangent):
    return tuple(
        whole(brick_order, brick_count, features, voxel_mask.transpose(0, 1, 3, 2), cotangent, w_conv1, w_down, w_conv2)
    )


def solution(mesh):
    return jax.shard_map(
        local,
        mesh=mesh,
        in_specs=(
            P("grp", "tx", "ty", None, None),
            P("grp", "tx", "ty", None),
            P(("grp", "tx", "ty"), None),
            P(("grp", "tx", "ty")),
            P(None, ("tx", "ty")),
            P(None, ("tx", "ty")),
            P(None, ("tx", "ty")),
            P("grp", "tx", "ty", None, None),
        ),
        out_specs=(
            P("grp", "tx", "ty", None, None),
            P(None, ("tx", "ty")),
            P(None, ("tx", "ty")),
            P(None, ("tx", "ty")),
        ),
        check_vma=False,
    )
```

```python
import jax
import jax.numpy as jnp
from jax import lax
from jax.experimental import pallas as pl
from jax.experimental.pallas import tpu as pltpu
from jax.sharding import PartitionSpec as P

C1 = 96
C2 = 192
GX = 2
GY = 4
CAP = 2
GROUPS = 32
N_TX = 8
N_TY = 16
PITCH_W = 33
PITCH_R = 264
PITCH_S = 136
MESH = pl.DeviceIdType.MESH
f32 = jnp.float32
bf16 = jnp.bfloat16
TAPS = [(ox, oy, oz) for ox in range(3) for oy in range(3) for oz in range(3)]
VMEM_LIMIT = 60 * 1024 * 1024


def lane_tiles(rows):
    return [rows[:, i * 128 : (i + 1) * 128] for i in range(rows.shape[1] // 128)]


def relane(count, segments):
    lanes = lax.broadcasted_iota(jnp.int32, segments[0][0][0].shape, 1)
    out = [None] * count
    rolled = {}
    for tiles, src, dst, length in segments:
        while length > 0:
            step = min(length, 128 - src % 128, 128 - dst % 128)
            tile, shift = tiles[src // 128], (dst - src) % 128
            key = (id(tile), shift)
            if key not in rolled:
                rolled[key] = pltpu.roll(tile, shift, 1) if shift else tile
            low, high, target = dst % 128, dst % 128 + step, dst // 128
            base = jnp.zeros_like(tile) if out[target] is None else out[target]
            if step == 128:
                out[target] = rolled[key]
            else:
                inside = lanes < high
                if low:
                    inside = inside & (lanes >= low)
                out[target] = jnp.where(inside, rolled[key], base)
            src, dst, length = src + step, dst + step, length - step
    return [jnp.zeros_like(segments[0][0][0]) if t is None else t for t in out]


PIECES_ONE = [[(0, 0, 0, 72), (1, 0, 72, 24)], [(1, 24, 0, 48), (2, 0, 48, 48)], [(2, 48, 0, 24), (3, 0, 24, 72)]]
PIECES_TWO = [
    [(0, 0, 0, 192)],
    [(0, 192, 0, 96), (1, 0, 96, 96)],
    [(1, 96, 0, 192)],
    [(2, 0, 0, 192)],
    [(2, 192, 0, 96), (3, 0, 96, 96)],
    [(3, 96, 0, 192)],
]
BASE_DOWN = 72


def to_row(shards, pieces, base, count):
    return relane(count, [(shards[s], base + a, b, n) for s, a, b, n in pieces])


def join(tiles):
    return tiles[0] if len(tiles) == 1 else jnp.concatenate(tiles, axis=1)


def depth_shifts(slab):
    axis = slab.ndim - 2
    depth = lax.broadcasted_iota(jnp.int32, slab.shape, axis)
    below = jnp.where(depth == 0, 0.0, pltpu.roll(slab, 1, axis))
    above = jnp.where(depth == 7, 0.0, pltpu.roll(slab, 7, axis))
    return below, slab, above


def barrier_with(peers):
    barrier = pltpu.get_barrier_semaphore()
    for peer in peers:
        pl.semaphore_signal(barrier, inc=1, device_id=peer, device_id_type=MESH)
    pl.semaphore_wait(barrier, len(peers))


def place():
    grp, tx, ty = lax.axis_index("grp"), lax.axis_index("tx"), lax.axis_index("ty")
    return grp, tx, ty, ty // 8, (ty // 2) % 4, ty % 2


def other(value, bits):
    if bits == 1:
        return value + 1 - 2 * (value % 2)
    if bits == 2:
        return (value + 2) % 4
    return 3 - value


def ring_peers(grp, tx, ty):
    return [(grp, (tx + d) % N_TX, ty) for d in range(1, N_TX)]


def cube_peers(grp, tx, hi, y, core):
    def ty_of(h, v, c):
        return h * 8 + v * 2 + c

    return {
        "core": (grp, tx, ty_of(hi, y, 1 - core)),
        "y1": (grp, tx, ty_of(hi, other(y, 1), core)),
        "y3": (grp, tx, ty_of(hi, other(y, 3), core)),
        "x": (1 - grp, tx, ty_of(1 - hi, y, core)),
        "xx": (grp, tx, ty_of(1 - hi, y, core)),
        "grp": (1 - grp, tx, ty_of(hi, y, core)),
    }


STEPS = [(dx, dy) for dx in (-1, 0, 1) for dy in (-1, 0, 1) if dx or dy]


def halo_peers(grp, tx, ty):
    return [(grp, (tx + dx + N_TX) % N_TX, (ty + dy + N_TY) % N_TY) for dx, dy in STEPS]


def edge_out(step, size, shift):
    return pl.ds(shift, 1) if step < 0 else pl.ds(size - 1 + shift, 1) if step > 0 else pl.ds(shift, size)


def edge_in(step, size):
    return pl.ds(size + 1, 1) if step < 0 else pl.ds(0, 1) if step > 0 else pl.ds(1, size)


def clear_edges(dst, tx, ty):
    size_x, size_y = dst.shape[0], dst.shape[1]

    @pl.when(tx == 0)
    def _():
        dst[0:1] = jnp.zeros((1,) + dst.shape[1:], dst.dtype)

    @pl.when(tx == N_TX - 1)
    def _():
        dst[size_x - 1 : size_x] = jnp.zeros((1,) + dst.shape[1:], dst.dtype)

    @pl.when(ty == 0)
    def _():
        dst[:, 0:1] = jnp.zeros((size_x, 1) + dst.shape[2:], dst.dtype)

    @pl.when(ty == N_TY - 1)
    def _():
        dst[:, size_y - 1 : size_y] = jnp.zeros((size_x, 1) + dst.shape[2:], dst.dtype)


class Links:
    def __init__(self, send, recv):
        self.send, self.recv, self.sent = send, recv, []

    def start(self, src, dst, peer):
        k = len(self.sent)
        copy = pltpu.make_async_remote_copy(
            src_ref=src,
            dst_ref=dst,
            send_sem=self.send.at[k],
            recv_sem=self.recv.at[k],
            device_id=peer,
            device_id_type=MESH,
        )
        copy.start()
        self.sent.append(copy)
        return copy

    def halo(self, src, dst, peers, inside):
        size_x, size_y = dst.shape[0] - 2, dst.shape[1] - 2
        shift = 1 if inside else 0
        copies = []
        for peer, (dx, dy) in zip(peers, STEPS):
            copies.append(
                self.start(
                    src.at[edge_out(dx, size_x, shift), edge_out(dy, size_y, shift)],
                    dst.at[edge_in(dx, size_x), edge_in(dy, size_y)],
                    peer,
                )
            )
        return copies


def halves(rows):
    return pl.ds(0, rows // 2), pl.ds(rows // 2, rows // 2)


class Gather:
    def __init__(self, links, where, shard, full, own):
        self.links, self.where, self.full = links, where, full
        self.first, self.second = halves(shard.shape[0])
        grp, tx, ty, hi, y, core = where
        self.cube = cube_peers(grp, tx, hi, y, core)
        mine = full.at[tx, hi, y, core]
        self.line = [links.start(shard, mine, peer) for peer in ring_peers(grp, tx, ty)]
        self.own = pltpu.make_async_copy(shard, mine, own)
        self.own.start()
        self.partner = []

    def part(self, v, rows):
        return self.full.at[:, :, v, self.where[5], rows]

    def to_core(self, ref):
        self.partner.append(self.links.start(ref, ref, self.cube["core"]))

    def across(self):
        grp, tx, ty, hi, y, core = self.where
        self.own.wait()
        for copy in self.line:
            copy.wait_recv()
        column = self.full.at[:, hi, y, core]
        self.step = [self.links.start(column, column, self.cube["x"])]
        self.to_core(column)

    def near(self):
        grp, tx, ty, hi, y, core = self.where
        for copy in self.step:
            copy.wait_recv()
        first, second = self.part(y, self.first), self.part(y, self.second)
        self.step = [
            self.links.start(first, first, self.cube["y1"]),
            self.links.start(second, second, self.cube["y3"]),
        ]
        self.to_core(self.full.at[:, 1 - hi, y, core])

    def far(self):
        y = self.where[4]
        y1, y3 = other(y, 1), other(y, 3)
        for copy in self.step:
            copy.wait_recv()
        self.step = []
        for v, rows, name in ((y, self.first, "y3"), (y1, self.first, "y3"), (y, self.second, "y1"), (y3, self.second, "y1")):
            self.step.append(self.links.start(self.part(v, rows), self.part(v, rows), self.cube[name]))
        self.to_core(self.part(y1, self.first))
        self.to_core(self.part(y3, self.second))

    def last(self):
        y = self.where[4]
        y1, y2, y3 = other(y, 1), other(y, 2), other(y, 3)
        arrived = [(y3, self.first), (y2, self.first), (y1, self.second), (y2, self.second)]
        for copy, (v, rows) in zip(self.step, arrived):
            copy.wait_recv()
            self.to_core(self.part(v, rows))

    def done(self):
        for copy in self.partner:
            copy.wait_recv()


class Scatter:
    def __init__(self, links, where, packed, total, sums, rd, ry2, ry1, rz, half, rg):
        self.links, self.where, self.packed, self.total = links, where, packed, total
        self.sums, self.rd, self.ry2, self.ry1 = sums, rd, ry2, ry1
        self.rz, self.half, self.rg = rz, half, rg
        grp, tx, ty, hi, y, core = where
        self.cube = cube_peers(grp, tx, hi, y, core)
        self.line = ring_peers(grp, tx, ty)
        rows = half.shape[1]
        self.whole, (self.first, self.second) = pl.ds(0, rows), halves(rows)
        self.pieces = {}
        self.ys = [other(y, 2), other(y, 3), other(y, 1), y]

    def add(self, z, h, v, rows, left, right):
        both = left[...].astype(f32) + right[...].astype(f32)
        self.sums[z, h, v, rows, :] = both.astype(bf16)

    def part(self, v, rows):
        return self.sums.at[:, :, v, rows]

    def wait(self):
        for copy in self.step:
            copy.wait_recv()

    def cores(self, pieces, h):
        core = self.where[5]
        for k in pieces:
            v = self.ys[k]
            copy = self.links.start(
                self.packed.at[:, h, v, 1 - core], self.rd.at[:, h, v], self.cube["core"]
            )
            self.pieces[k, h] = copy

    def far(self):
        core = self.where[5]
        y2, y3, y1, y = self.ys
        self.step = []
        for (k, h), copy in self.pieces.items():
            v = self.ys[k]
            copy.wait_recv()

            def take(z, carry):
                self.add(z, h, v, self.whole, self.packed.at[z, h, v, core], self.rd.at[z, h, v])
                return carry

            lax.fori_loop(0, 8, take, 0, unroll=2)
            if k in (1, 2):
                rows, name = (self.first, "y3") if k == 1 else (self.second, "y1")
                for n, u in enumerate((v, y2)):
                    self.step.append(
                        self.links.start(
                            self.sums.at[:, h, u, rows], self.ry2.at[n, :, h, rows], self.cube[name]
                        )
                    )

    def near(self):
        y2, y3, y1, y = self.ys
        far, self.step = self.step, []
        for h in range(2):
            for copy in far[2 * h : 2 * h + 2] + far[4 + 2 * h : 6 + 2 * h]:
                copy.wait_recv()

            def take(z, carry):
                self.add(z, h, y, self.whole, self.sums.at[z, h, y], self.ry2.at[0, z, h])
                self.add(z, h, y1, self.first, self.sums.at[z, h, y1, self.first], self.ry2.at[1, z, h, self.first])
                self.add(
                    z, h, y3, self.second, self.sums.at[z, h, y3, self.second], self.ry2.at[1, z, h, self.second]
                )
                return carry

            lax.fori_loop(0, 8, take, 0, unroll=2)
            for v, rows, name in ((y1, self.first, "y1"), (y3, self.second, "y3")):
                self.step.append(
                    self.links.start(self.sums.at[:, h, v, rows], self.ry1.at[:, h, rows], self.cube[name])
                )

    def along(self):
        tx, y = self.where[1], self.where[4]
        self.wait()

        def take(z, carry):
            for h in range(2):
                self.add(z, h, y, self.whole, self.sums.at[z, h, y], self.ry1.at[z, h])
            return carry

        lax.fori_loop(0, 8, take, 0)
        self.step = [
            self.links.start(self.sums.at[(tx + d + 1) % N_TX, :, y], self.rz.at[d], peer)
            for d, peer in enumerate(self.line)
        ]

    def swap(self):
        tx, hi, y = self.where[1], self.where[3], self.where[4]
        self.wait()
        for h in range(2):
            value = self.sums[tx, h, y].astype(f32)
            for d in range(N_TX - 1):
                value = value + self.rz[d, h].astype(f32)
            self.half[h] = value
        self.step = [
            self.links.start(self.half.at[hi], self.rg.at[0], self.cube["grp"]),
            self.links.start(self.half.at[1 - hi], self.rg.at[1], self.cube["x"]),
            self.links.start(self.half.at[1 - hi], self.rg.at[2], self.cube["xx"]),
        ]

    def done(self):
        self.wait()
        self.total[...] = (self.half[self.where[3]] + self.rg[0]) + (self.rg[1] + self.rg[2])


def fold(tiles):
    wide, mid, rest = tiles
    lanes = lax.broadcasted_iota(jnp.int32, (8, 128), 1)
    rows = lax.broadcasted_iota(jnp.int32, (8, 128), 0)
    tail = jnp.zeros((8, 128), f32)
    for n in range(4):
        piece = rest[8 * n : 8 * n + 8]
        piece = pltpu.roll(piece, 32 * n, 1) if n else piece
        tail = jnp.where((lanes >= 32 * n) & (lanes < 32 * n + 32), piece, tail)
    last = jnp.where(rows < 3, wide[24:32], jnp.where(rows < 6, pltpu.roll(mid[24:32], 3, 0), 0.0))
    return jnp.concatenate([wide[:24], mid[:24], tail, last], axis=0)


def unfold(rows):
    tail, last = rows[48:56], rows[56:64]
    rest = jnp.concatenate([tail] + [pltpu.roll(tail, 128 - 32 * n, 1) for n in range(1, 4)], axis=0)
    return [
        jnp.concatenate([rows[:24], last], axis=0),
        jnp.concatenate([rows[24:48], pltpu.roll(last, 5, 0)], axis=0),
        rest,
    ]


def choose(slots, place, blocks):
    value = None
    for i, block in enumerate(blocks):
        term = jnp.where(slots[0, i] == place, block, 0.0)
        value = term if value is None else value + term
    return value


def corner(slots, i):
    return slots[0, i] // GY, slots[0, i] % GY


def pack_shards(w_conv1, w_down, w_conv2, shard_a, shard_b, tmp, wide):
    tmp[...] = jnp.zeros_like(tmp)
    wide[...] = jnp.zeros_like(wide)
    tmp[0, 0:27, 0:72] = w_conv1[...].astype(f32)
    wide[0:8, 0:144] = w_down[...].astype(f32)
    low = lane_tiles(wide[0:8, 0:256])
    for j in range(3):
        tmp[1, pl.ds(j, 8, stride=3), :] = relane(1, [(low, 48 * j, BASE_DOWN, 48)])[0]
    shard_a[...] = (tmp[0] + tmp[1]).astype(bf16)
    wide[0:27, 0:288] = w_conv2[...].astype(f32)
    shard_b[...] = fold(lane_tiles(wide[...])).astype(bf16)


def prepare(slots, count, feats, occupancy, cot, mask, coarse, mp, gp):
    flags = []
    for p in range(GX * GY):
        flag = jnp.where(slots[0, 0] == p, 1.0, 0.0)
        for i in range(1, CAP):
            flag = flag + jnp.where((slots[0, i] == p) & (count[0] > i), 1.0, 0.0)
        flags.append(flag)

    def iotas(rows, lanes):
        return [lax.broadcasted_iota(jnp.int32, (rows, lanes), d) for d in range(2)]

    row, lane = iotas(256, 8)
    pick_z = jnp.where(row % 8 == lane, 1.0, 0.0).astype(bf16)
    row, lane = iotas(256, 32)
    pick_y = row // 8 == lane
    row, lane = iotas(128, 8)
    pair_z = jnp.where(row % 8 == lane // 2, 1.0, 0.0).astype(bf16)
    row, lane = iotas(128, 32)
    pair_y = row // 8 == lane // 2
    ones = jnp.ones((32, 256), bf16)
    mp[1:17, 1:33] = jnp.zeros((16, 32, 8, 128), f32)
    gp[1:9, 1:17] = jnp.zeros((8, 16, 8, 256), f32)
    for px in range(GX):

        def first(x, carry):
            plane = occupancy[0, x].astype(f32).astype(bf16)
            column = jnp.dot(pick_z, plane, preferred_element_type=f32)
            column = jnp.where(pick_y, column, 0.0).astype(bf16)
            value = jnp.dot(column, ones[:, :128], preferred_element_type=f32).reshape(32, 8, 128)
            for py in range(GY):
                at = slice(py * 8, py * 8 + 8)
                live = value[at] * flags[px * GY + py]
                mask[x, at] = live
                mp[1 + x, 1 + py * 8 : 9 + py * 8, :, 0:C1] = feats[0, x, at].astype(f32) * live[:, :, 0:C1]
            return carry

        def second(a, carry):
            plane = (occupancy[0, 2 * a] + occupancy[0, 2 * a + 1]).astype(f32).astype(bf16)
            column = jnp.dot(pair_z, plane, preferred_element_type=f32)
            column = jnp.where(pair_y, column, 0.0).astype(bf16)
            value = jnp.minimum(jnp.dot(column, ones, preferred_element_type=f32), 1.0).reshape(16, 8, 256)
            for py in range(GY):
                at = slice(py * 4, py * 4 + 4)
                live = value[at] * flags[px * GY + py]
                coarse[a, at] = live
                grad = cot[0, a, at].astype(f32) * live[:, 0:4, 0:C2]
                gp[1 + a, 1 + py * 4 : 5 + py * 4, 0:4, 0:C2] = grad
            return carry

        lax.fori_loop(px * 8, px * 8 + 8, first, 0, unroll=4)
        lax.fori_loop(px * 4, px * 4 + 4, second, 0, unroll=4)


def unpack_first(full, w9, wd, w1g, wdg, tmp):
    def unpack(a, carry):
        shards = []
        for b in range(4):
            value = full[a // 4, (a // 2) % 2, (a % 2) * 2 + b // 2, b % 2].astype(f32)
            tmp[b] = value
            shards.append([value])
        for k in range(3):
            w1g[pl.ds((a * 3 + k) * PITCH_W, 32), :] = to_row(shards, PIECES_ONE[k], 0, 1)[0]
        chunks = [[tmp[b, pl.ds(j, 8, stride=3), :]] for b in range(4) for j in range(3)]
        for k in range(3):
            segments = [(chunks[4 * k + n], BASE_DOWN, 48 * n, 48) for n in range(4)]
            for c, tile in enumerate(relane(2, segments)):
                wdg[c, pl.ds(pl.multiple_of((a * 3 + k) * 8, 8), 8), :] = tile
        return carry

    lax.fori_loop(0, GROUPS, unpack, 0, unroll=4)
    for t in range(27):
        k, oz = t // 3, t % 3
        w9[k * 128 : k * 128 + C1, oz * 128 : (oz + 1) * 128] = w1g[pl.ds(t, C1, stride=PITCH_W), :].astype(bf16)
    for k in range(9):
        w9[k * 128 + C1 : (k + 1) * 128, :] = jnp.zeros((128 - C1, 384), bf16)
    for t in range(8):
        for c in range(2):
            wd[t * 128 : t * 128 + C1, c * 128 : (c + 1) * 128] = wdg[c, pl.ds(t, C1, stride=8), :].astype(bf16)
        wd[t * 128 + C1 : (t + 1) * 128, :] = jnp.zeros((128 - C1, 256), bf16)


def unpack_second(full, w2, big):
    def unpack(a, carry):
        shards = [unfold(full[a // 4, (a // 2) % 2, (a % 2) * 2 + b // 2, b % 2].astype(f32)) for b in range(4)]
        for k in range(6):
            for c, tile in enumerate(to_row(shards, PIECES_TWO[k], 0, 2)):
                big[c, pl.ds((a * 6 + k) * PITCH_W, 32), :] = tile
        return carry

    lax.fori_loop(0, GROUPS, unpack, 0, unroll=4)

    def order(k, carry):
        for oz in range(3):
            for c in range(2):
                w2[pl.ds(pl.multiple_of(k * 256, 256), C2), oz * 256 + c * 128 : oz * 256 + (c + 1) * 128] = big[
                    c, pl.ds(k * 3 + oz, C2, stride=PITCH_W), :
                ].astype(bf16)
        w2[pl.ds(pl.multiple_of(k * 256 + C2, 64), 256 - C2), :] = jnp.zeros((256 - C2, 768), bf16)
        return carry

    lax.fori_loop(0, 9, order, 0, unroll=3)


def windows(dst, i, window, edge, flip):
    lanes = window.shape[-1]
    rows = edge * edge * 8
    for k in range(9):
        ox, oy = k // 3, k % 3
        if flip:
            ox, oy = 2 - ox, 2 - oy
        piece = window[ox : ox + edge, oy : oy + edge].reshape(rows, lanes)
        dst[i * rows : (i + 1) * rows, k * lanes : (k + 1) * lanes] = piece.astype(bf16)


def three(rows, lanes):
    return [rows[:, n * lanes : (n + 1) * lanes].reshape(-1, 8, lanes) for n in range(3)]


def conv(parts):
    low, mid, high = parts
    return (depth_shifts(low)[0] + mid + depth_shifts(high)[2]).reshape(-1, mid.shape[-1])


def spread(value):
    below, mid, above = depth_shifts(value.reshape(-1, 8, value.shape[-1]))
    return jnp.concatenate([v.reshape(value.shape).astype(bf16) for v in (above, mid, below)], axis=1)


def pack_first(packed, r1, rdn, tmp, pair, h):
    def pack(z, carry):
        a = z * 4 + h * 2 + pair
        segments = [[] for _ in range(4)]
        downs = []
        for k in range(3):
            ci = a * 3 + k
            tiles = [r1[pl.ds(ci, 32, stride=PITCH_S), :]]
            for s, at, lane, n in PIECES_ONE[k]:
                segments[s].append((tiles, lane, at, n))
            downs.append([rdn[c, pl.ds(ci, 8, stride=PITCH_S), :] for c in range(2)])
        for b in range(4):
            for j in range(3):
                m = 3 * b + j
                tmp[b, pl.ds(j, 8, stride=3), :] = relane(1, [(downs[m // 4], m % 4 * 48, BASE_DOWN, 48)])[0]
            value = relane(1, segments[b])[0] + tmp[b]
            packed[z, h, pair * 2 + b // 2, b % 2] = value.astype(bf16)
        return carry

    lax.fori_loop(0, 8, pack, 0, unroll=4)


def pack_second(packed, big, pair, h):
    def pack(z, carry):
        a = z * 4 + h * 2 + pair
        segments = [[] for _ in range(4)]
        for k in range(6):
            tiles = [big[c, pl.ds(a * 6 + k, 32, stride=PITCH_R), :] for c in range(2)]
            for s, at, lane, n in PIECES_TWO[k]:
                segments[s].append((tiles, lane, at, n))
        for b in range(4):
            packed[z, h, pair * 2 + b // 2, b % 2] = fold(relane(3, segments[b])).astype(bf16)
        return carry

    lax.fori_loop(0, 8, pack, 0, unroll=4)


def whole_kernel(
    slots, count, feats_in, occupancy_in, cot_in, w_conv1, w_down, w_conv2, out, grad_conv1, grad_down, grad_conv2,
    feats, occupancy, cot, total_a, total_b, mask, coarse, shard_a, shard_b, wide,
    full_a, full_b, mp, gp, dp, x9, x2, x3, w9, wd, w2, w1g, wdg, tmp, big, act, pm, hs, gs, r1, rdn,
    packed_a, packed_b, sums_a, rd_a, ry2_a, ry1_a, rz_a, half_a, rg_a,
    sums_b, rd_b, ry2_b, ry1_b, rz_b, half_b, rg_b, send, recv, own,
):
    where = place()
    grp, tx, ty, hi, y, core = where
    cube = cube_peers(grp, tx, hi, y, core)
    around = halo_peers(grp, tx, ty)
    links = Links(send, recv)
    loads = [
        pltpu.make_async_copy(src, dst, own.at[2 + k])
        for k, (src, dst) in enumerate(((feats_in, feats), (occupancy_in, occupancy), (cot_in, cot)))
    ]
    for load in loads:
        load.start()
    greeted = ring_peers(grp, tx, ty) + [cube[n] for n in ("core", "y1", "y3", "x", "xx", "grp")] + around
    barrier = pltpu.get_barrier_semaphore()
    for peer in greeted:
        pl.semaphore_signal(barrier, inc=1, device_id=peer, device_id_type=MESH)
    pack_shards(w_conv1, w_down, w_conv2, shard_a, shard_b, tmp, wide)
    pl.semaphore_wait(barrier, len(greeted))

    first = Gather(links, where, shard_a, full_a, own.at[0])
    second = Gather(links, where, shard_b, full_b, own.at[1])
    for load in loads:
        load.wait()
    prepare(slots, count, feats, occupancy, cot, mask, coarse, mp, gp)
    hs[...] = jnp.zeros_like(hs)
    rdn[...] = jnp.zeros_like(rdn)
    r1[27 * PITCH_S : 32 * PITCH_S, :] = jnp.zeros((5 * PITCH_S, 128), f32)
    big[:, 27 * PITCH_R : 32 * PITCH_R, :] = jnp.zeros((2, 5 * PITCH_R, 128), f32)
    first.across()
    halo_m = links.halo(mp, mp, around, True)
    halo_g = links.halo(gp, gp, around, True)
    first.near()
    second.across()
    for copy in halo_m:
        copy.wait_recv()
    clear_edges(mp, tx, ty)
    for i in range(CAP):
        px, py = corner(slots, i)
        windows(x9, i, mp[pl.ds(px * 8, 10), pl.ds(py * 8, 10)], 8, False)
    first.far()
    second.near()
    first.last()
    first.done()
    unpack_first(full_a, w9, wd, w1g, wdg, tmp)
    second.far()

    lives, edges = [], []
    for i in range(CAP):
        px, py = corner(slots, i)
        lives.append(mask[pl.ds(px * 8, 8), pl.ds(py * 8, 8)].reshape(512, 128))
        edges.append(coarse[pl.ds(px * 4, 4), pl.ds(py * 4, 4)].reshape(128, 256))
    live = jnp.concatenate(lives, axis=0)
    edge = jnp.concatenate(edges, axis=0)
    value = conv(three(jnp.dot(x9[...], w9[...], preferred_element_type=f32), 128))
    act[...] = value
    hidden = (live * jax.nn.silu(value)).astype(bf16).astype(f32).reshape(CAP, 4, 2, 4, 2, 8, 128)
    for p in range(2):
        for q in range(2):
            for b in range(4):
                hs[:, :, p * 2 + q, b * 16 : b * 16 + 8, :] = hidden[:, :, p, b, q]
    second.last()
    for t in range(8):
        patch = hs[:, :, t // 2, pl.ds(t % 2, 32, stride=2), :].reshape(256, 128)
        pm[:, t * 128 : (t + 1) * 128] = patch.astype(bf16)
    raw = jnp.dot(pm[...], wd[...], preferred_element_type=f32)
    down = (edge * raw).astype(bf16).astype(f32)
    downs = [down[i * 128 : (i + 1) * 128].reshape(4, 4, 8, 256) for i in range(CAP)]
    for p in range(GX * GY):
        px, py = p // GY, p % GY
        dp[1 + px * 4 : 5 + px * 4, 1 + py * 4 : 5 + py * 4] = choose(slots, p, downs)
    halo_d = links.halo(dp, dp, around, True)

    for copy in halo_g:
        copy.wait_recv()
    clear_edges(gp, tx, ty)
    grads = []
    for i in range(CAP):
        px, py = corner(slots, i)
        windows(x3, i, gp[pl.ds(px * 4, 6), pl.ds(py * 4, 6)], 4, True)
        grads.append(gp[pl.ds(px * 4 + 1, 4), pl.ds(py * 4 + 1, 4)].reshape(128, 256))
    grad_two = jnp.concatenate(grads, axis=0)
    spread_two = spread(grad_two)
    second.done()
    unpack_second(full_b, w2, big)
    parts = []
    for oz in range(3):
        part = None
        for k in range(9):
            term = lax.dot_general(
                x3[:, k * 256 : (k + 1) * 256],
                w2[k * 256 : (k + 1) * 256, oz * 256 : (oz + 1) * 256],
                (((1,), (1,)), ((), ())),
                preferred_element_type=f32,
            )
            part = term if part is None else part + term
        parts.append(part.reshape(-1, 8, 256))
    back = conv(parts[::-1])
    grad_in = (grad_two + edge * back).astype(bf16)
    for copy in halo_d:
        copy.wait_recv()
    clear_edges(dp, tx, ty)
    for i in range(CAP):
        px, py = corner(slots, i)
        windows(x2, i, dp[pl.ds(px * 4, 6), pl.ds(py * 4, 6)], 4, False)
    for k in range(9):
        product = lax.dot_general(
            x2[:, k * 256 : (k + 1) * 256], spread_two, (((0,), (0,)), ((), ())), preferred_element_type=f32
        )
        for oz in range(3):
            for c in range(2):
                at = oz * 256 + c * 128
                big[c, (3 * k + oz) * PITCH_R : (3 * k + oz) * PITCH_R + 256, :] = product[:, at : at + 128]
    sum_b = Scatter(links, where, packed_b, total_b, sums_b, rd_b, ry2_b, ry1_b, rz_b, half_b, rg_b)
    for pair, pieces in ((1 - y // 2, (0, 1)), (y // 2, (2, 3))):
        for h in range(2):
            pack_second(packed_b, big, pair, h)
            sum_b.cores(pieces, h)

    for t in range(8):
        product = lax.dot_general(
            pm[:, t * 128 : (t + 1) * 128], grad_in, (((0,), (0,)), ((), ())), preferred_element_type=f32
        )
        for c in range(2):
            rdn[c, t * PITCH_S : t * PITCH_S + 128, :] = product[:, c * 128 : (c + 1) * 128]
    for t in range(8):
        part = lax.dot_general(
            grad_in, wd[t * 128 : (t + 1) * 128, :], (((1,), (1,)), ((), ())), preferred_element_type=f32
        )
        gs[:, :, t // 2, pl.ds(t % 2, 32, stride=2), :] = part.reshape(CAP, 4, 32, 128)
    rows = []
    for p in range(2):
        for b in range(4):
            for q in range(2):
                rows.append(gs[:, :, p * 2 + q, b * 16 : b * 16 + 8, :])
    hidden = jnp.stack(rows, axis=2).reshape(1024, 128)
    value = act[...]
    sig = jax.nn.sigmoid(value)
    spread_one = spread(live * hidden * (sig * (1.0 + value * (1.0 - sig))))
    sum_b.far()
    for k in range(9):
        product = lax.dot_general(
            x9[:, k * 128 : (k + 1) * 128], spread_one, (((0,), (0,)), ((), ())), preferred_element_type=f32
        )
        for oz in range(3):
            at = (3 * k + oz) * PITCH_S
            r1[at : at + 128, :] = product[:, oz * 128 : (oz + 1) * 128]
    tmp[...] = jnp.zeros_like(tmp)
    sum_a = Scatter(links, where, packed_a, total_a, sums_a, rd_a, ry2_a, ry1_a, rz_a, half_a, rg_a)
    for pair, pieces in ((1 - y // 2, (0, 1)), (y // 2, (2, 3))):
        for h in range(2):
            pack_first(packed_a, r1, rdn, tmp, pair, h)
            sum_a.cores(pieces, h)
    sum_b.near()

    parts = [
        jnp.dot(x2[...], w2[:, oz * 256 : (oz + 1) * 256], preferred_element_type=f32).reshape(-1, 8, 256)
        for oz in range(2)
    ]
    sum_a.far()
    parts.append(jnp.dot(x2[...], w2[:, 512:768], preferred_element_type=f32).reshape(-1, 8, 256))
    value = conv(parts)
    sum_b.along()
    blocks = []
    for i in range(CAP):
        px, py = corner(slots, i)
        down = dp[pl.ds(px * 4 + 1, 4), pl.ds(py * 4 + 1, 4)].reshape(128, 256)
        rows = slice(i * 128, (i + 1) * 128)
        blocks.append((edges[i] * (down + value[rows])).reshape(4, 4, 8, 256))
    sum_a.near()
    for p in range(GX * GY):
        px, py = p // GY, p % GY
        out[0, px * 4 : px * 4 + 4, py * 4 : py * 4 + 4] = choose(slots, p, blocks)[:, :, 0:4, 0:C2].astype(bf16)
    sum_a.along()
    sum_b.swap()
    sum_b.done()
    wide = unfold(total_b[...])
    grad_conv2[:, 0:256] = jnp.concatenate(wide[:2], axis=1)[:27]
    grad_conv2[:, 256:288] = wide[2][:27, :32]
    sum_a.swap()
    sum_a.done()
    grad_conv1[...] = total_a[:27, :72]
    low = [(total_a[pl.ds(j, 8, stride=3), :],) for j in range(3)]
    low = relane(2, [(low[j], BASE_DOWN, 48 * j, 48) for j in range(3)])
    grad_down[:, 0:128] = low[0]
    grad_down[:, 128:144] = low[1][:, :16]
    for copy in links.sent:
        copy.wait_send()


def whole(order, count, feats, occupancy, cot, w_conv1, w_down, w_conv2):
    def sums(rows):
        return [
            pltpu.VMEM((8, 2, 4, rows, 128), bf16),
            pltpu.VMEM((8, 2, 4, rows, 128), bf16),
            pltpu.VMEM((2, 8, 2, rows, 128), bf16),
            pltpu.VMEM((8, 2, rows, 128), bf16),
            pltpu.VMEM((7, 2, rows, 128), bf16),
            pltpu.VMEM((2, rows, 128), f32),
            pltpu.VMEM((3, rows, 128), f32),
        ]

    copies = 2 * 23 + 24 + 2 * 30
    return pl.pallas_call(
        whole_kernel,
        in_specs=[pl.BlockSpec(memory_space=pltpu.SMEM)] * 2
        + [pl.BlockSpec(memory_space=pl.ANY)] * 3
        + [pl.BlockSpec(memory_space=pltpu.VMEM)] * 3,
        out_specs=[pl.BlockSpec(memory_space=pltpu.VMEM)] * 4,
        out_shape=[
            jax.ShapeDtypeStruct((1, 8, 16, 4, C2), bf16),
            jax.ShapeDtypeStruct((27, 72), f32),
            jax.ShapeDtypeStruct((8, 144), f32),
            jax.ShapeDtypeStruct((27, 288), f32),
        ],
        scratch_shapes=[
            pltpu.VMEM((1, 16, 32, 8, C1), bf16),
            pltpu.VMEM((1, 16, 8, 32), jnp.int32),
            pltpu.VMEM((1, 8, 16, 4, C2), bf16),
            pltpu.VMEM((32, 128), f32),
            pltpu.VMEM((64, 128), f32),
            pltpu.VMEM((16, 32, 8, 128), f32),
            pltpu.VMEM((8, 16, 8, 256), f32),
            pltpu.VMEM((32, 128), bf16),
            pltpu.VMEM((64, 128), bf16),
            pltpu.VMEM((32, 384), f32),
            pltpu.VMEM((8, 2, 4, 2, 32, 128), bf16),
            pltpu.VMEM((8, 2, 4, 2, 64, 128), bf16),
            pltpu.VMEM((18, 34, 8, 128), f32),
            pltpu.VMEM((10, 18, 8, 256), f32),
            pltpu.VMEM((10, 18, 8, 256), f32),
            pltpu.VMEM((1024, 9 * 128), bf16),
            pltpu.VMEM((256, 9 * 256), bf16),
            pltpu.VMEM((256, 9 * 256), bf16),
            pltpu.VMEM((9 * 128, 384), bf16),
            pltpu.VMEM((1024, 256), bf16),
            pltpu.VMEM((9 * 256, 768), bf16),
            pltpu.VMEM((C1 * PITCH_W + 8, 128), f32),
            pltpu.VMEM((2, C1 * 8, 128), f32),
            pltpu.VMEM((4, 32, 128), f32),
            pltpu.VMEM((2, 32 * PITCH_R, 128), f32),
            pltpu.VMEM((1024, 128), f32),
            pltpu.VMEM((256, 1024), bf16),
            pltpu.VMEM((CAP, 4, 4, 64, 128), f32),
            pltpu.VMEM((CAP, 4, 4, 64, 128), f32),
            pltpu.VMEM((32 * PITCH_S, 128), f32),
            pltpu.VMEM((2, 8 * PITCH_S, 128), f32),
            pltpu.VMEM((8, 2, 4, 2, 32, 128), bf16),
            pltpu.VMEM((8, 2, 4, 2, 64, 128), bf16),
        ]
        + sums(32)
        + sums(64)
        + [
            pltpu.SemaphoreType.DMA((copies,)),
            pltpu.SemaphoreType.DMA((copies,)),
            pltpu.SemaphoreType.DMA((5,)),
        ],
        compiler_params=pltpu.CompilerParams(collective_id=0, has_side_effects=True, vmem_limit_bytes=VMEM_LIMIT),
        name="whole",
    )(order, count, feats, occupancy, cot, w_conv1, w_down, w_conv2)


def local(features, voxel_mask, brick_order, brick_count, w_conv1, w_down, w_conv2, cotangent):
    return tuple(
        whole(brick_order, brick_count, features, voxel_mask.transpose(0, 1, 3, 2), cotangent, w_conv1, w_down, w_conv2)
    )


def solution(mesh):
    return jax.shard_map(
        local,
        mesh=mesh,
        in_specs=(
            P("grp", "tx", "ty", None, None),
            P("grp", "tx", "ty", None),
            P(("grp", "tx", "ty"), None),
            P(("grp", "tx", "ty")),
            P(None, ("tx", "ty")),
            P(None, ("tx", "ty")),
            P(None, ("tx", "ty")),
            P("grp", "tx", "ty", None, None),
        ),
        out_specs=(
            P("grp", "tx", "ty", None, None),
            P(None, ("tx", "ty")),
            P(None, ("tx", "ty")),
            P(None, ("tx", "ty")),
        ),
        check_vma=False,
    )
```

```python
import jax
import jax.numpy as jnp
from jax import lax
from jax.experimental import pallas as pl
from jax.experimental.pallas import tpu as pltpu
from jax.sharding import PartitionSpec as P

C1 = 96
C2 = 192
GX = 2
GY = 4
CAP = 2
GROUPS = 32
N_TX = 8
N_TY = 16
PITCH_W = 33
PITCH_R = 264
PITCH_S = 136
MESH = pl.DeviceIdType.MESH
f32 = jnp.float32
bf16 = jnp.bfloat16
TAPS = [(ox, oy, oz) for ox in range(3) for oy in range(3) for oz in range(3)]
VMEM_LIMIT = 60 * 1024 * 1024


def lane_tiles(rows):
    return [rows[:, i * 128 : (i + 1) * 128] for i in range(rows.shape[1] // 128)]


def relane(count, segments):
    lanes = lax.broadcasted_iota(jnp.int32, segments[0][0][0].shape, 1)
    out = [None] * count
    rolled = {}
    for tiles, src, dst, length in segments:
        while length > 0:
            step = min(length, 128 - src % 128, 128 - dst % 128)
            tile, shift = tiles[src // 128], (dst - src) % 128
            key = (id(tile), shift)
            if key not in rolled:
                rolled[key] = pltpu.roll(tile, shift, 1) if shift else tile
            low, high, target = dst % 128, dst % 128 + step, dst // 128
            base = jnp.zeros_like(tile) if out[target] is None else out[target]
            if step == 128:
                out[target] = rolled[key]
            else:
                inside = lanes < high
                if low:
                    inside = inside & (lanes >= low)
                out[target] = jnp.where(inside, rolled[key], base)
            src, dst, length = src + step, dst + step, length - step
    return [jnp.zeros_like(segments[0][0][0]) if t is None else t for t in out]


PIECES_ONE = [[(0, 0, 0, 72), (1, 0, 72, 24)], [(1, 24, 0, 48), (2, 0, 48, 48)], [(2, 48, 0, 24), (3, 0, 24, 72)]]
PIECES_TWO = [
    [(0, 0, 0, 192)],
    [(0, 192, 0, 96), (1, 0, 96, 96)],
    [(1, 96, 0, 192)],
    [(2, 0, 0, 192)],
    [(2, 192, 0, 96), (3, 0, 96, 96)],
    [(3, 96, 0, 192)],
]
BASE_DOWN = 72


def to_row(shards, pieces, base, count):
    return relane(count, [(shards[s], base + a, b, n) for s, a, b, n in pieces])


def join(tiles):
    return tiles[0] if len(tiles) == 1 else jnp.concatenate(tiles, axis=1)


def depth_shifts(slab):
    axis = slab.ndim - 2
    depth = lax.broadcasted_iota(jnp.int32, slab.shape, axis)
    below = jnp.where(depth == 0, 0.0, pltpu.roll(slab, 1, axis))
    above = jnp.where(depth == 7, 0.0, pltpu.roll(slab, 7, axis))
    return below, slab, above


def barrier_with(peers):
    barrier = pltpu.get_barrier_semaphore()
    for peer in peers:
        pl.semaphore_signal(barrier, inc=1, device_id=peer, device_id_type=MESH)
    pl.semaphore_wait(barrier, len(peers))


def place():
    grp, tx, ty = lax.axis_index("grp"), lax.axis_index("tx"), lax.axis_index("ty")
    return grp, tx, ty, ty // 8, (ty // 2) % 4, ty % 2


def other(value, bits):
    if bits == 1:
        return value + 1 - 2 * (value % 2)
    if bits == 2:
        return (value + 2) % 4
    return 3 - value


def ring_peers(grp, tx, ty):
    return [(grp, (tx + d) % N_TX, ty) for d in range(1, N_TX)]


def across_peers(grp, tx, hi, y, core):
    return [(1 - grp, (tx + d) % N_TX, (1 - hi) * 8 + y * 2 + core) for d in range(N_TX)]


def cube_peers(grp, tx, hi, y, core):
    def ty_of(h, v, c):
        return h * 8 + v * 2 + c

    return {
        "core": (grp, tx, ty_of(hi, y, 1 - core)),
        "y1": (grp, tx, ty_of(hi, other(y, 1), core)),
        "y3": (grp, tx, ty_of(hi, other(y, 3), core)),
        "x": (1 - grp, tx, ty_of(1 - hi, y, core)),
        "xx": (grp, tx, ty_of(1 - hi, y, core)),
        "grp": (1 - grp, tx, ty_of(hi, y, core)),
    }


STEPS = [(dx, dy) for dx in (-1, 0, 1) for dy in (-1, 0, 1) if dx or dy]


def halo_peers(grp, tx, ty):
    return [(grp, (tx + dx + N_TX) % N_TX, (ty + dy + N_TY) % N_TY) for dx, dy in STEPS]


def edge_out(step, size, shift):
    return pl.ds(shift, 1) if step < 0 else pl.ds(size - 1 + shift, 1) if step > 0 else pl.ds(shift, size)


def edge_in(step, size):
    return pl.ds(size + 1, 1) if step < 0 else pl.ds(0, 1) if step > 0 else pl.ds(1, size)


def clear_edges(dst, tx, ty):
    size_x, size_y = dst.shape[0], dst.shape[1]

    @pl.when(tx == 0)
    def _():
        dst[0:1] = jnp.zeros((1,) + dst.shape[1:], dst.dtype)

    @pl.when(tx == N_TX - 1)
    def _():
        dst[size_x - 1 : size_x] = jnp.zeros((1,) + dst.shape[1:], dst.dtype)

    @pl.when(ty == 0)
    def _():
        dst[:, 0:1] = jnp.zeros((size_x, 1) + dst.shape[2:], dst.dtype)

    @pl.when(ty == N_TY - 1)
    def _():
        dst[:, size_y - 1 : size_y] = jnp.zeros((size_x, 1) + dst.shape[2:], dst.dtype)


class Links:
    def __init__(self, send, recv):
        self.send, self.recv, self.sent = send, recv, []

    def start(self, src, dst, peer):
        k = len(self.sent)
        copy = pltpu.make_async_remote_copy(
            src_ref=src,
            dst_ref=dst,
            send_sem=self.send.at[k],
            recv_sem=self.recv.at[k],
            device_id=peer,
            device_id_type=MESH,
        )
        copy.start()
        self.sent.append(copy)
        return copy

    def halo(self, src, dst, peers, inside):
        size_x, size_y = dst.shape[0] - 2, dst.shape[1] - 2
        shift = 1 if inside else 0
        copies = []
        for peer, (dx, dy) in zip(peers, STEPS):
            copies.append(
                self.start(
                    src.at[edge_out(dx, size_x, shift), edge_out(dy, size_y, shift)],
                    dst.at[edge_in(dx, size_x), edge_in(dy, size_y)],
                    peer,
                )
            )
        return copies


def halves(rows):
    return pl.ds(0, rows // 2), pl.ds(rows // 2, rows // 2)


class Gather:
    def __init__(self, links, where, shard, full, own):
        self.links, self.where, self.full = links, where, full
        self.first, self.second = halves(shard.shape[0])
        grp, tx, ty, hi, y, core = where
        self.cube = cube_peers(grp, tx, hi, y, core)
        mine = full.at[tx, hi, y, core]
        self.line = [links.start(shard, mine, peer) for peer in ring_peers(grp, tx, ty)]
        self.line += [links.start(shard, mine, peer) for peer in across_peers(grp, tx, hi, y, core)]
        self.own = pltpu.make_async_copy(shard, mine, own)
        self.own.start()
        self.partner = []

    def part(self, v, rows):
        return self.full.at[:, :, v, self.where[5], rows]

    def to_core(self, ref):
        self.partner.append(self.links.start(ref, ref, self.cube["core"]))

    def near(self):
        grp, tx, ty, hi, y, core = self.where
        self.own.wait()
        for copy in self.line:
            copy.wait_recv()
        first, second = self.part(y, self.first), self.part(y, self.second)
        self.step = [
            self.links.start(first, first, self.cube["y1"]),
            self.links.start(second, second, self.cube["y3"]),
        ]
        self.to_core(self.full.at[:, :, y, core])

    def far(self):
        y = self.where[4]
        y1, y3 = other(y, 1), other(y, 3)
        for copy in self.step:
            copy.wait_recv()
        self.step = []
        for v, rows, name in ((y, self.first, "y3"), (y1, self.first, "y3"), (y, self.second, "y1"), (y3, self.second, "y1")):
            self.step.append(self.links.start(self.part(v, rows), self.part(v, rows), self.cube[name]))
        self.to_core(self.part(y1, self.first))
        self.to_core(self.part(y3, self.second))

    def last(self):
        y = self.where[4]
        y1, y2, y3 = other(y, 1), other(y, 2), other(y, 3)
        arrived = [(y3, self.first), (y2, self.first), (y1, self.second), (y2, self.second)]
        for copy, (v, rows) in zip(self.step, arrived):
            copy.wait_recv()
            self.to_core(self.part(v, rows))

    def done(self):
        for copy in self.partner:
            copy.wait_recv()


class Scatter:
    def __init__(self, links, where, packed, total, sums, rd, ry2, ry1, rz, half, rg):
        self.links, self.where, self.packed, self.total = links, where, packed, total
        self.sums, self.rd, self.ry2, self.ry1 = sums, rd, ry2, ry1
        self.rz, self.half, self.rg = rz, half, rg
        grp, tx, ty, hi, y, core = where
        self.cube = cube_peers(grp, tx, hi, y, core)
        self.line = ring_peers(grp, tx, ty)
        rows = half.shape[1]
        self.whole, (self.first, self.second) = pl.ds(0, rows), halves(rows)
        self.pieces = {}
        self.ys = [other(y, 2), other(y, 3), other(y, 1), y]

    def add(self, z, h, v, rows, left, right):
        both = left[...].astype(f32) + right[...].astype(f32)
        self.sums[z, h, v, rows, :] = both.astype(bf16)

    def part(self, v, rows):
        return self.sums.at[:, :, v, rows]

    def wait(self):
        for copy in self.step:
            copy.wait_recv()

    def cores(self, pieces, h):
        core = self.where[5]
        for k in pieces:
            v = self.ys[k]
            copy = self.links.start(
                self.packed.at[:, h, v, 1 - core], self.rd.at[:, h, v], self.cube["core"]
            )
            self.pieces[k, h] = copy

    def far(self):
        core = self.where[5]
        y2, y3, y1, y = self.ys
        self.step = []
        for (k, h), copy in self.pieces.items():
            v = self.ys[k]
            copy.wait_recv()

            def take(z, carry):
                self.add(z, h, v, self.whole, self.packed.at[z, h, v, core], self.rd.at[z, h, v])
                return carry

            lax.fori_loop(0, 8, take, 0, unroll=2)
            if k in (1, 2):
                rows, name = (self.first, "y3") if k == 1 else (self.second, "y1")
                for n, u in enumerate((v, y2)):
                    self.step.append(
                        self.links.start(
                            self.sums.at[:, h, u, rows], self.ry2.at[n, :, h, rows], self.cube[name]
                        )
                    )

    def near(self):
        y2, y3, y1, y = self.ys
        far, self.step = self.step, []
        for h in range(2):
            for copy in far[2 * h : 2 * h + 2] + far[4 + 2 * h : 6 + 2 * h]:
                copy.wait_recv()

            def take(z, carry):
                self.add(z, h, y, self.whole, self.sums.at[z, h, y], self.ry2.at[0, z, h])
                self.add(z, h, y1, self.first, self.sums.at[z, h, y1, self.first], self.ry2.at[1, z, h, self.first])
                self.add(
                    z, h, y3, self.second, self.sums.at[z, h, y3, self.second], self.ry2.at[1, z, h, self.second]
                )
                return carry

            lax.fori_loop(0, 8, take, 0, unroll=2)
            for v, rows, name in ((y1, self.first, "y1"), (y3, self.second, "y3")):
                self.step.append(
                    self.links.start(self.sums.at[:, h, v, rows], self.ry1.at[:, h, rows], self.cube[name])
                )

    def along(self):
        tx, y = self.where[1], self.where[4]
        self.wait()

        def take(z, carry):
            for h in range(2):
                self.add(z, h, y, self.whole, self.sums.at[z, h, y], self.ry1.at[z, h])
            return carry

        lax.fori_loop(0, 8, take, 0)
        self.step = [
            self.links.start(self.sums.at[(tx + d + 1) % N_TX, :, y], self.rz.at[d], peer)
            for d, peer in enumerate(self.line)
        ]

    def swap(self):
        tx, hi, y = self.where[1], self.where[3], self.where[4]
        self.wait()
        for h in range(2):
            value = self.sums[tx, h, y].astype(f32)
            for d in range(N_TX - 1):
                value = value + self.rz[d, h].astype(f32)
            self.half[h] = value
        self.step = [
            self.links.start(self.half.at[hi], self.rg.at[0], self.cube["grp"]),
            self.links.start(self.half.at[1 - hi], self.rg.at[1], self.cube["x"]),
            self.links.start(self.half.at[1 - hi], self.rg.at[2], self.cube["xx"]),
        ]

    def done(self):
        self.wait()
        self.total[...] = (self.half[self.where[3]] + self.rg[0]) + (self.rg[1] + self.rg[2])


def fold(tiles):
    wide, mid, rest = tiles
    lanes = lax.broadcasted_iota(jnp.int32, (8, 128), 1)
    rows = lax.broadcasted_iota(jnp.int32, (8, 128), 0)
    tail = jnp.zeros((8, 128), f32)
    for n in range(4):
        piece = rest[8 * n : 8 * n + 8]
        piece = pltpu.roll(piece, 32 * n, 1) if n else piece
        tail = jnp.where((lanes >= 32 * n) & (lanes < 32 * n + 32), piece, tail)
    last = jnp.where(rows < 3, wide[24:32], jnp.where(rows < 6, pltpu.roll(mid[24:32], 3, 0), 0.0))
    return jnp.concatenate([wide[:24], mid[:24], tail, last], axis=0)


def unfold(rows):
    tail, last = rows[48:56], rows[56:64]
    rest = jnp.concatenate([tail] + [pltpu.roll(tail, 128 - 32 * n, 1) for n in range(1, 4)], axis=0)
    return [
        jnp.concatenate([rows[:24], last], axis=0),
        jnp.concatenate([rows[24:48], pltpu.roll(last, 5, 0)], axis=0),
        rest,
    ]


def choose(slots, place, blocks):
    value = None
    for i, block in enumerate(blocks):
        term = jnp.where(slots[0, i] == place, block, 0.0)
        value = term if value is None else value + term
    return value


def corner(slots, i):
    return slots[0, i] // GY, slots[0, i] % GY


def pack_shards(w_conv1, w_down, w_conv2, shard_a, shard_b, tmp, wide):
    tmp[...] = jnp.zeros_like(tmp)
    wide[...] = jnp.zeros_like(wide)
    tmp[0, 0:27, 0:72] = w_conv1[...].astype(f32)
    wide[0:8, 0:144] = w_down[...].astype(f32)
    low = lane_tiles(wide[0:8, 0:256])
    for j in range(3):
        tmp[1, pl.ds(j, 8, stride=3), :] = relane(1, [(low, 48 * j, BASE_DOWN, 48)])[0]
    shard_a[...] = (tmp[0] + tmp[1]).astype(bf16)
    wide[0:27, 0:288] = w_conv2[...].astype(f32)
    shard_b[...] = fold(lane_tiles(wide[...])).astype(bf16)


def prepare(slots, count, feats, occupancy, cot, mask, coarse, mp, gp, fine):
    flags = []
    for p in range(GX * GY):
        flag = jnp.where(slots[0, 0] == p, 1.0, 0.0)
        for i in range(1, CAP):
            flag = flag + jnp.where((slots[0, i] == p) & (count[0] > i), 1.0, 0.0)
        flags.append(flag)

    def iotas(rows, lanes):
        return [lax.broadcasted_iota(jnp.int32, (rows, lanes), d) for d in range(2)]

    row, lane = iotas(256, 8)
    pick_z = jnp.where(row % 8 == lane, 1.0, 0.0).astype(bf16)
    row, lane = iotas(256, 32)
    pick_y = row // 8 == lane
    row, lane = iotas(128, 8)
    pair_z = jnp.where(row % 8 == lane // 2, 1.0, 0.0).astype(bf16)
    row, lane = iotas(128, 32)
    pair_y = row // 8 == lane // 2
    ones = jnp.ones((32, 256), bf16)
    if fine:
        mp[1:17, 1:33] = jnp.zeros((16, 32, 8, 128), f32)
    else:
        gp[1:9, 1:17] = jnp.zeros((8, 16, 8, 256), f32)
    for px in range(GX) if fine else ():

        def first(x, carry):
            plane = occupancy[0, x].astype(f32).astype(bf16)
            column = jnp.dot(pick_z, plane, preferred_element_type=f32)
            column = jnp.where(pick_y, column, 0.0).astype(bf16)
            value = jnp.dot(column, ones[:, :128], preferred_element_type=f32).reshape(32, 8, 128)
            for py in range(GY):
                at = slice(py * 8, py * 8 + 8)
                live = value[at] * flags[px * GY + py]
                mask[x, at] = live
                mp[1 + x, 1 + py * 8 : 9 + py * 8, :, 0:C1] = feats[0, x, at].astype(f32) * live[:, :, 0:C1]
            return carry

        lax.fori_loop(px * 8, px * 8 + 8, first, 0, unroll=4)

    for px in range(GX) if not fine else ():

        def second(a, carry):
            plane = (occupancy[0, 2 * a] + occupancy[0, 2 * a + 1]).astype(f32).astype(bf16)
            column = jnp.dot(pair_z, plane, preferred_element_type=f32)
            column = jnp.where(pair_y, column, 0.0).astype(bf16)
            value = jnp.minimum(jnp.dot(column, ones, preferred_element_type=f32), 1.0).reshape(16, 8, 256)
            for py in range(GY):
                at = slice(py * 4, py * 4 + 4)
                live = value[at] * flags[px * GY + py]
                coarse[a, at] = live
                grad = cot[0, a, at].astype(f32) * live[:, 0:4, 0:C2]
                gp[1 + a, 1 + py * 4 : 5 + py * 4, 0:4, 0:C2] = grad
            return carry

        lax.fori_loop(px * 4, px * 4 + 4, second, 0, unroll=4)


def unpack_first(full, w9, wd, w1g, wdg, tmp):
    def unpack(a, carry):
        shards = []
        for b in range(4):
            value = full[a // 4, (a // 2) % 2, (a % 2) * 2 + b // 2, b % 2]
            tmp[b] = value.astype(f32)
            shards.append([value])
        for k in range(3):
            w1g[pl.ds((a * 3 + k) * PITCH_W, 32), :] = to_row(shards, PIECES_ONE[k], 0, 1)[0].astype(f32)
        chunks = [[tmp[b, pl.ds(j, 8, stride=3), :]] for b in range(4) for j in range(3)]
        for k in range(3):
            segments = [(chunks[4 * k + n], BASE_DOWN, 48 * n, 48) for n in range(4)]
            for c, tile in enumerate(relane(2, segments)):
                wdg[c, pl.ds(pl.multiple_of((a * 3 + k) * 8, 8), 8), :] = tile
        return carry

    lax.fori_loop(0, GROUPS, unpack, 0, unroll=4)
    for t in range(27):
        k, oz = t // 3, t % 3
        w9[k * 128 : k * 128 + C1, oz * 128 : (oz + 1) * 128] = w1g[pl.ds(t, C1, stride=PITCH_W), :].astype(bf16)
    for k in range(9):
        w9[k * 128 + C1 : (k + 1) * 128, :] = jnp.zeros((128 - C1, 384), bf16)
    for t in range(8):
        for c in range(2):
            wd[t * 128 : t * 128 + C1, c * 128 : (c + 1) * 128] = wdg[c, pl.ds(t, C1, stride=8), :].astype(bf16)
        wd[t * 128 + C1 : (t + 1) * 128, :] = jnp.zeros((128 - C1, 256), bf16)


def unpack_second(full, w2, big):
    def unpack(a, carry):
        shards = [
            [
                tile.astype(bf16)
                for tile in unfold(full[a // 4, (a // 2) % 2, (a % 2) * 2 + b // 2, b % 2].astype(f32))
            ]
            for b in range(4)
        ]
        for k in range(6):
            for c, tile in enumerate(to_row(shards, PIECES_TWO[k], 0, 2)):
                big[c, pl.ds((a * 6 + k) * PITCH_W, 32), :] = tile.astype(f32)
        return carry

    lax.fori_loop(0, GROUPS, unpack, 0, unroll=4)

    def order(k, carry):
        for oz in range(3):
            for c in range(2):
                w2[pl.ds(pl.multiple_of(k * 256, 256), C2), oz * 256 + c * 128 : oz * 256 + (c + 1) * 128] = big[
                    c, pl.ds(k * 3 + oz, C2, stride=PITCH_W), :
                ].astype(bf16)
        w2[pl.ds(pl.multiple_of(k * 256 + C2, 64), 256 - C2), :] = jnp.zeros((256 - C2, 768), bf16)
        return carry

    lax.fori_loop(0, 9, order, 0, unroll=3)


def windows(dst, i, window, edge, flip):
    lanes = window.shape[-1]
    rows = edge * edge * 8
    for k in range(9):
        ox, oy = k // 3, k % 3
        if flip:
            ox, oy = 2 - ox, 2 - oy
        piece = window[ox : ox + edge, oy : oy + edge].reshape(rows, lanes)
        dst[i * rows : (i + 1) * rows, k * lanes : (k + 1) * lanes] = piece.astype(bf16)


def three(rows, lanes):
    return [rows[:, n * lanes : (n + 1) * lanes].reshape(-1, 8, lanes) for n in range(3)]


def conv(parts):
    low, mid, high = parts
    return (depth_shifts(low)[0] + mid + depth_shifts(high)[2]).reshape(-1, mid.shape[-1])


def spread(value):
    below, mid, above = depth_shifts(value.reshape(-1, 8, value.shape[-1]))
    return jnp.concatenate([v.reshape(value.shape).astype(bf16) for v in (above, mid, below)], axis=1)


def pack_first(packed, r1, rdn, tmp, pair, h):
    def pack(z, carry):
        a = z * 4 + h * 2 + pair
        segments = [[] for _ in range(4)]
        downs = []
        for k in range(3):
            ci = a * 3 + k
            tiles = [r1[pl.ds(ci, 32, stride=PITCH_S), :].astype(bf16)]
            for s, at, lane, n in PIECES_ONE[k]:
                segments[s].append((tiles, lane, at, n))
            downs.append([rdn[c, pl.ds(ci, 8, stride=PITCH_S), :] for c in range(2)])
        for b in range(4):
            for j in range(3):
                m = 3 * b + j
                tmp[b, pl.ds(j, 8, stride=3), :] = relane(1, [(downs[m // 4], m % 4 * 48, BASE_DOWN, 48)])[0]
            value = relane(1, segments[b])[0].astype(f32) + tmp[b]
            packed[z, h, pair * 2 + b // 2, b % 2] = value.astype(bf16)
        return carry

    lax.fori_loop(0, 8, pack, 0, unroll=4)


def pack_second(packed, big, pair, h):
    def pack(z, carry):
        a = z * 4 + h * 2 + pair
        segments = [[] for _ in range(4)]
        for k in range(6):
            tiles = [big[c, pl.ds(a * 6 + k, 32, stride=PITCH_R), :].astype(bf16) for c in range(2)]
            for s, at, lane, n in PIECES_TWO[k]:
                segments[s].append((tiles, lane, at, n))
        for b in range(4):
            packed[z, h, pair * 2 + b // 2, b % 2] = fold(
                [tile.astype(f32) for tile in relane(3, segments[b])]
            ).astype(bf16)
        return carry

    lax.fori_loop(0, 8, pack, 0, unroll=4)


def whole_kernel(
    slots, count, feats_in, occupancy_in, cot_in, w_conv1, w_down, w_conv2, out, grad_conv1, grad_down, grad_conv2,
    feats, occupancy, cot, total_a, total_b, mask, coarse, shard_a, shard_b, wide,
    full_a, full_b, mp, gp, dp, x9, x2, x3, w9, wd, w2, w1g, wdg, tmp, big, act, pm, hs, gs, r1, rdn,
    packed_a, packed_b, sums_a, rd_a, ry2_a, ry1_a, rz_a, half_a, rg_a,
    sums_b, rd_b, ry2_b, ry1_b, rz_b, half_b, rg_b, send, recv, own,
):
    where = place()
    grp, tx, ty, hi, y, core = where
    cube = cube_peers(grp, tx, hi, y, core)
    around = halo_peers(grp, tx, ty)
    links = Links(send, recv)
    loads = [
        pltpu.make_async_copy(src, dst, own.at[2 + k])
        for k, (src, dst) in enumerate(((feats_in, feats), (occupancy_in, occupancy), (cot_in, cot)))
    ]
    for load in loads:
        load.start()
    greeted = ring_peers(grp, tx, ty) + across_peers(grp, tx, hi, y, core) + [cube[n] for n in ("core", "y1", "y3", "xx", "grp")] + around
    barrier = pltpu.get_barrier_semaphore()
    for peer in greeted:
        pl.semaphore_signal(barrier, inc=1, device_id=peer, device_id_type=MESH)
    pack_shards(w_conv1, w_down, w_conv2, shard_a, shard_b, tmp, wide)
    pl.semaphore_wait(barrier, len(greeted))

    first = Gather(links, where, shard_a, full_a, own.at[0])
    second = Gather(links, where, shard_b, full_b, own.at[1])
    for load in loads:
        load.wait()
    prepare(slots, count, feats, occupancy, cot, mask, coarse, mp, gp, True)
    halo_m = links.halo(mp, mp, around, True)
    first.near()
    prepare(slots, count, feats, occupancy, cot, mask, coarse, mp, gp, False)
    second.near()
    first.far()
    halo_g = links.halo(gp, gp, around, True)
    for copy in halo_m:
        copy.wait_recv()
    clear_edges(mp, tx, ty)
    for i in range(CAP):
        px, py = corner(slots, i)
        windows(x9, i, mp[pl.ds(px * 8, 10), pl.ds(py * 8, 10)], 8, False)
    first.last()
    second.far()
    hs[...] = jnp.zeros_like(hs)
    rdn[...] = jnp.zeros_like(rdn)
    r1[27 * PITCH_S : 32 * PITCH_S, :] = jnp.zeros((5 * PITCH_S, 128), f32)
    big[:, 27 * PITCH_R : 32 * PITCH_R, :] = jnp.zeros((2, 5 * PITCH_R, 128), f32)
    first.done()
    unpack_first(full_a, w9, wd, w1g, wdg, tmp)

    lives, edges = [], []
    for i in range(CAP):
        px, py = corner(slots, i)
        lives.append(mask[pl.ds(px * 8, 8), pl.ds(py * 8, 8)].reshape(512, 128))
        edges.append(coarse[pl.ds(px * 4, 4), pl.ds(py * 4, 4)].reshape(128, 256))
    live = jnp.concatenate(lives, axis=0)
    edge = jnp.concatenate(edges, axis=0)
    value = conv(three(jnp.dot(x9[...], w9[...], preferred_element_type=f32), 128))
    act[...] = value
    hidden = (live * jax.nn.silu(value)).astype(bf16).astype(f32).reshape(CAP, 4, 2, 4, 2, 8, 128)
    for p in range(2):
        for q in range(2):
            for b in range(4):
                hs[:, :, p * 2 + q, b * 16 : b * 16 + 8, :] = hidden[:, :, p, b, q]
    second.last()
    for t in range(8):
        patch = hs[:, :, t // 2, pl.ds(t % 2, 32, stride=2), :].reshape(256, 128)
        pm[:, t * 128 : (t + 1) * 128] = patch.astype(bf16)
    raw = jnp.dot(pm[...], wd[...], preferred_element_type=f32)
    down = (edge * raw).astype(bf16).astype(f32)
    downs = [down[i * 128 : (i + 1) * 128].reshape(4, 4, 8, 256) for i in range(CAP)]
    for p in range(GX * GY):
        px, py = p // GY, p % GY
        dp[1 + px * 4 : 5 + px * 4, 1 + py * 4 : 5 + py * 4] = choose(slots, p, downs)
    halo_d = links.halo(dp, dp, around, True)

    for copy in halo_g:
        copy.wait_recv()
    clear_edges(gp, tx, ty)
    grads = []
    for i in range(CAP):
        px, py = corner(slots, i)
        windows(x3, i, gp[pl.ds(px * 4, 6), pl.ds(py * 4, 6)], 4, True)
        grads.append(gp[pl.ds(px * 4 + 1, 4), pl.ds(py * 4 + 1, 4)].reshape(128, 256))
    grad_two = jnp.concatenate(grads, axis=0)
    spread_two = spread(grad_two)
    second.done()
    unpack_second(full_b, w2, big)
    parts = []
    for oz in range(3):
        part = None
        for k in range(9):
            term = lax.dot_general(
                x3[:, k * 256 : (k + 1) * 256],
                w2[k * 256 : (k + 1) * 256, oz * 256 : (oz + 1) * 256],
                (((1,), (1,)), ((), ())),
                preferred_element_type=f32,
            )
            part = term if part is None else part + term
        parts.append(part.reshape(-1, 8, 256))
    back = conv(parts[::-1])
    grad_in = (grad_two + edge * back).astype(bf16)
    for copy in halo_d:
        copy.wait_recv()
    clear_edges(dp, tx, ty)
    for i in range(CAP):
        px, py = corner(slots, i)
        windows(x2, i, dp[pl.ds(px * 4, 6), pl.ds(py * 4, 6)], 4, False)
    for k in range(9):
        product = lax.dot_general(
            x2[:, k * 256 : (k + 1) * 256], spread_two, (((0,), (0,)), ((), ())), preferred_element_type=f32
        )
        for oz in range(3):
            for c in range(2):
                at = oz * 256 + c * 128
                big[c, (3 * k + oz) * PITCH_R : (3 * k + oz) * PITCH_R + 256, :] = product[:, at : at + 128]
    sum_b = Scatter(links, where, packed_b, total_b, sums_b, rd_b, ry2_b, ry1_b, rz_b, half_b, rg_b)
    for pair, pieces in ((1 - y // 2, (0, 1)), (y // 2, (2, 3))):
        for h in range(2):
            pack_second(packed_b, big, pair, h)
            sum_b.cores(pieces, h)

    for t in range(8):
        product = lax.dot_general(
            pm[:, t * 128 : (t + 1) * 128], grad_in, (((0,), (0,)), ((), ())), preferred_element_type=f32
        )
        for c in range(2):
            rdn[c, t * PITCH_S : t * PITCH_S + 128, :] = product[:, c * 128 : (c + 1) * 128]
    for t in range(8):
        part = lax.dot_general(
            grad_in, wd[t * 128 : (t + 1) * 128, :], (((1,), (1,)), ((), ())), preferred_element_type=f32
        )
        gs[:, :, t // 2, pl.ds(t % 2, 32, stride=2), :] = part.reshape(CAP, 4, 32, 128)
    rows = []
    for p in range(2):
        for b in range(4):
            for q in range(2):
                rows.append(gs[:, :, p * 2 + q, b * 16 : b * 16 + 8, :])
    hidden = jnp.stack(rows, axis=2).reshape(1024, 128)
    value = act[...]
    sig = jax.nn.sigmoid(value)
    spread_one = spread(live * hidden * (sig * (1.0 + value * (1.0 - sig))))
    sum_b.far()
    for k in range(9):
        product = lax.dot_general(
            x9[:, k * 128 : (k + 1) * 128], spread_one, (((0,), (0,)), ((), ())), preferred_element_type=f32
        )
        for oz in range(3):
            at = (3 * k + oz) * PITCH_S
            r1[at : at + 128, :] = product[:, oz * 128 : (oz + 1) * 128]
    tmp[...] = jnp.zeros_like(tmp)
    sum_a = Scatter(links, where, packed_a, total_a, sums_a, rd_a, ry2_a, ry1_a, rz_a, half_a, rg_a)
    for pair, pieces in ((1 - y // 2, (0, 1)), (y // 2, (2, 3))):
        for h in range(2):
            pack_first(packed_a, r1, rdn, tmp, pair, h)
            sum_a.cores(pieces, h)
    sum_b.near()

    parts = [
        jnp.dot(x2[...], w2[:, oz * 256 : (oz + 1) * 256], preferred_element_type=f32).reshape(-1, 8, 256)
        for oz in range(2)
    ]
    sum_a.far()
    parts.append(jnp.dot(x2[...], w2[:, 512:768], preferred_element_type=f32).reshape(-1, 8, 256))
    value = conv(parts)
    sum_b.along()
    blocks = []
    for i in range(CAP):
        px, py = corner(slots, i)
        down = dp[pl.ds(px * 4 + 1, 4), pl.ds(py * 4 + 1, 4)].reshape(128, 256)
        rows = slice(i * 128, (i + 1) * 128)
        blocks.append((edges[i] * (down + value[rows])).reshape(4, 4, 8, 256))
    sum_a.near()
    for p in range(GX * GY):
        px, py = p // GY, p % GY
        out[0, px * 4 : px * 4 + 4, py * 4 : py * 4 + 4] = choose(slots, p, blocks)[:, :, 0:4, 0:C2].astype(bf16)
    sum_a.along()
    sum_b.swap()
    sum_b.done()
    wide = unfold(total_b[...])
    grad_conv2[:, 0:256] = jnp.concatenate(wide[:2], axis=1)[:27]
    grad_conv2[:, 256:288] = wide[2][:27, :32]
    sum_a.swap()
    sum_a.done()
    grad_conv1[...] = total_a[:27, :72]
    low = [(total_a[pl.ds(j, 8, stride=3), :],) for j in range(3)]
    low = relane(2, [(low[j], BASE_DOWN, 48 * j, 48) for j in range(3)])
    grad_down[:, 0:128] = low[0]
    grad_down[:, 128:144] = low[1][:, :16]
    for copy in links.sent:
        copy.wait_send()


def whole(order, count, feats, occupancy, cot, w_conv1, w_down, w_conv2):
    def sums(rows):
        return [
            pltpu.VMEM((8, 2, 4, rows, 128), bf16),
            pltpu.VMEM((8, 2, 4, rows, 128), bf16),
            pltpu.VMEM((2, 8, 2, rows, 128), bf16),
            pltpu.VMEM((8, 2, rows, 128), bf16),
            pltpu.VMEM((7, 2, rows, 128), bf16),
            pltpu.VMEM((2, rows, 128), f32),
            pltpu.VMEM((3, rows, 128), f32),
        ]

    copies = 2 * 30 + 24 + 2 * 30
    return pl.pallas_call(
        whole_kernel,
        in_specs=[pl.BlockSpec(memory_space=pltpu.SMEM)] * 2
        + [pl.BlockSpec(memory_space=pl.ANY)] * 3
        + [pl.BlockSpec(memory_space=pltpu.VMEM)] * 3,
        out_specs=[pl.BlockSpec(memory_space=pltpu.VMEM)] * 4,
        out_shape=[
            jax.ShapeDtypeStruct((1, 8, 16, 4, C2), bf16),
            jax.ShapeDtypeStruct((27, 72), f32),
            jax.ShapeDtypeStruct((8, 144), f32),
            jax.ShapeDtypeStruct((27, 288), f32),
        ],
        scratch_shapes=[
            pltpu.VMEM((1, 16, 32, 8, C1), bf16),
            pltpu.VMEM((1, 16, 8, 32), jnp.int32),
            pltpu.VMEM((1, 8, 16, 4, C2), bf16),
            pltpu.VMEM((32, 128), f32),
            pltpu.VMEM((64, 128), f32),
            pltpu.VMEM((16, 32, 8, 128), f32),
            pltpu.VMEM((8, 16, 8, 256), f32),
            pltpu.VMEM((32, 128), bf16),
            pltpu.VMEM((64, 128), bf16),
            pltpu.VMEM((32, 384), f32),
            pltpu.VMEM((8, 2, 4, 2, 32, 128), bf16),
            pltpu.VMEM((8, 2, 4, 2, 64, 128), bf16),
            pltpu.VMEM((18, 34, 8, 128), f32),
            pltpu.VMEM((10, 18, 8, 256), f32),
            pltpu.VMEM((10, 18, 8, 256), f32),
            pltpu.VMEM((1024, 9 * 128), bf16),
            pltpu.VMEM((256, 9 * 256), bf16),
            pltpu.VMEM((256, 9 * 256), bf16),
            pltpu.VMEM((9 * 128, 384), bf16),
            pltpu.VMEM((1024, 256), bf16),
            pltpu.VMEM((9 * 256, 768), bf16),
            pltpu.VMEM((C1 * PITCH_W + 8, 128), f32),
            pltpu.VMEM((2, C1 * 8, 128), f32),
            pltpu.VMEM((4, 32, 128), f32),
            pltpu.VMEM((2, 32 * PITCH_R, 128), f32),
            pltpu.VMEM((1024, 128), f32),
            pltpu.VMEM((256, 1024), bf16),
            pltpu.VMEM((CAP, 4, 4, 64, 128), f32),
            pltpu.VMEM((CAP, 4, 4, 64, 128), f32),
            pltpu.VMEM((32 * PITCH_S, 128), f32),
            pltpu.VMEM((2, 8 * PITCH_S, 128), f32),
            pltpu.VMEM((8, 2, 4, 2, 32, 128), bf16),
            pltpu.VMEM((8, 2, 4, 2, 64, 128), bf16),
        ]
        + sums(32)
        + sums(64)
        + [
            pltpu.SemaphoreType.DMA((copies,)),
            pltpu.SemaphoreType.DMA((copies,)),
            pltpu.SemaphoreType.DMA((5,)),
        ],
        compiler_params=pltpu.CompilerParams(collective_id=0, has_side_effects=True, vmem_limit_bytes=VMEM_LIMIT),
        name="whole",
    )(order, count, feats, occupancy, cot, w_conv1, w_down, w_conv2)


def local(features, voxel_mask, brick_order, brick_count, w_conv1, w_down, w_conv2, cotangent):
    return tuple(
        whole(brick_order, brick_count, features, voxel_mask.transpose(0, 1, 3, 2), cotangent, w_conv1, w_down, w_conv2)
    )


def solution(mesh):
    return jax.shard_map(
        local,
        mesh=mesh,
        in_specs=(
            P("grp", "tx", "ty", None, None),
            P("grp", "tx", "ty", None),
            P(("grp", "tx", "ty"), None),
            P(("grp", "tx", "ty")),
            P(None, ("tx", "ty")),
            P(None, ("tx", "ty")),
            P(None, ("tx", "ty")),
            P("grp", "tx", "ty", None, None),
        ),
        out_specs=(
            P("grp", "tx", "ty", None, None),
            P(None, ("tx", "ty")),
            P(None, ("tx", "ty")),
            P(None, ("tx", "ty")),
        ),
        check_vma=False,
    )
```

```python
import jax
import jax.numpy as jnp
from jax import lax
from jax.experimental import pallas as pl
from jax.experimental.pallas import tpu as pltpu
from jax.sharding import PartitionSpec as P

C1 = 96
C2 = 192
GX = 2
GY = 4
CAP = 2
GROUPS = 32
N_TX = 8
N_TY = 16
PITCH_W = 33
PITCH_R = 264
PITCH_S = 136
MESH = pl.DeviceIdType.MESH
f32 = jnp.float32
bf16 = jnp.bfloat16
TAPS = [(ox, oy, oz) for ox in range(3) for oy in range(3) for oz in range(3)]
VMEM_LIMIT = 60 * 1024 * 1024


def lane_tiles(rows):
    return [rows[:, i * 128 : (i + 1) * 128] for i in range(rows.shape[1] // 128)]


def relane(count, segments):
    lanes = lax.broadcasted_iota(jnp.int32, segments[0][0][0].shape, 1)
    out = [None] * count
    rolled = {}
    for tiles, src, dst, length in segments:
        while length > 0:
            step = min(length, 128 - src % 128, 128 - dst % 128)
            tile, shift = tiles[src // 128], (dst - src) % 128
            key = (id(tile), shift)
            if key not in rolled:
                rolled[key] = pltpu.roll(tile, shift, 1) if shift else tile
            low, high, target = dst % 128, dst % 128 + step, dst // 128
            base = jnp.zeros_like(tile) if out[target] is None else out[target]
            if step == 128:
                out[target] = rolled[key]
            else:
                inside = lanes < high
                if low:
                    inside = inside & (lanes >= low)
                out[target] = jnp.where(inside, rolled[key], base)
            src, dst, length = src + step, dst + step, length - step
    return [jnp.zeros_like(segments[0][0][0]) if t is None else t for t in out]


PIECES_ONE = [[(0, 0, 0, 72), (1, 0, 72, 24)], [(1, 24, 0, 48), (2, 0, 48, 48)], [(2, 48, 0, 24), (3, 0, 24, 72)]]
PIECES_TWO = [
    [(0, 0, 0, 192)],
    [(0, 192, 0, 96), (1, 0, 96, 96)],
    [(1, 96, 0, 192)],
    [(2, 0, 0, 192)],
    [(2, 192, 0, 96), (3, 0, 96, 96)],
    [(3, 96, 0, 192)],
]
BASE_DOWN = 72


def to_row(shards, pieces, base, count):
    return relane(count, [(shards[s], base + a, b, n) for s, a, b, n in pieces])


def join(tiles):
    return tiles[0] if len(tiles) == 1 else jnp.concatenate(tiles, axis=1)


def depth_shifts(slab):
    axis = slab.ndim - 2
    depth = lax.broadcasted_iota(jnp.int32, slab.shape, axis)
    below = jnp.where(depth == 0, 0.0, pltpu.roll(slab, 1, axis))
    above = jnp.where(depth == 7, 0.0, pltpu.roll(slab, 7, axis))
    return below, slab, above


def barrier_with(peers):
    barrier = pltpu.get_barrier_semaphore()
    for peer in peers:
        pl.semaphore_signal(barrier, inc=1, device_id=peer, device_id_type=MESH)
    pl.semaphore_wait(barrier, len(peers))


def place():
    grp, tx, ty = lax.axis_index("grp"), lax.axis_index("tx"), lax.axis_index("ty")
    return grp, tx, ty, ty // 8, (ty // 2) % 4, ty % 2


def other(value, bits):
    if bits == 1:
        return value + 1 - 2 * (value % 2)
    if bits == 2:
        return (value + 2) % 4
    return 3 - value


def ring_peers(grp, tx, ty):
    return [(grp, (tx + d) % N_TX, ty) for d in range(1, N_TX)]


def across_peers(grp, tx, hi, y, core):
    return [(1 - grp, (tx + d) % N_TX, (1 - hi) * 8 + y * 2 + core) for d in range(N_TX)]


def cube_peers(grp, tx, hi, y, core):
    def ty_of(h, v, c):
        return h * 8 + v * 2 + c

    return {
        "core": (grp, tx, ty_of(hi, y, 1 - core)),
        "y1": (grp, tx, ty_of(hi, other(y, 1), core)),
        "y3": (grp, tx, ty_of(hi, other(y, 3), core)),
        "x": (1 - grp, tx, ty_of(1 - hi, y, core)),
        "xx": (grp, tx, ty_of(1 - hi, y, core)),
        "grp": (1 - grp, tx, ty_of(hi, y, core)),
    }


STEPS = [(dx, dy) for dx in (-1, 0, 1) for dy in (-1, 0, 1) if dx or dy]


def halo_peers(grp, tx, ty):
    return [(grp, (tx + dx + N_TX) % N_TX, (ty + dy + N_TY) % N_TY) for dx, dy in STEPS]


def edge_out(step, size, shift):
    return pl.ds(shift, 1) if step < 0 else pl.ds(size - 1 + shift, 1) if step > 0 else pl.ds(shift, size)


def edge_in(step, size):
    return pl.ds(size + 1, 1) if step < 0 else pl.ds(0, 1) if step > 0 else pl.ds(1, size)


def squeeze(slabs, narrow):
    if narrow:
        pairs = slabs.reshape(slabs.shape[0] // 2, 2, 8, slabs.shape[2])
        slabs = pairs[:, 0] + pltpu.roll(pairs[:, 1], 4, 1)
    return slabs.reshape(-1, slabs.shape[2]).astype(bf16)


def widen(rows, narrow):
    slabs = rows.astype(f32).reshape(-1, 8, rows.shape[1])
    if not narrow:
        return slabs
    low = lax.broadcasted_iota(jnp.int32, slabs.shape, 1) < 4
    pairs = [jnp.where(low, slabs, 0.0), jnp.where(low, pltpu.roll(slabs, 4, 1), 0.0)]
    return jnp.stack(pairs, axis=1).reshape(-1, 8, rows.shape[1])


def land(dst, copies, bufs, narrow):
    size_x, size_y = dst.shape[0] - 2, dst.shape[1] - 2
    for copy in copies:
        copy.wait_recv()
    for n, (at_x, at_y) in enumerate(((0, 0), (size_x + 1, size_y + 1))):
        side_x, side_y = widen(bufs[2][n], narrow), widen(bufs[3][n], narrow)
        dst[at_x : at_x + 1, 1 : size_y + 1] = side_x.reshape(1, size_y, 8, -1)
        dst[1 : size_x + 1, at_y : at_y + 1] = side_y.reshape(size_x, 1, 8, -1)


def clear_edges(dst, tx, ty):
    size_x, size_y = dst.shape[0], dst.shape[1]

    @pl.when(tx == 0)
    def _():
        dst[0:1] = jnp.zeros((1,) + dst.shape[1:], dst.dtype)

    @pl.when(tx == N_TX - 1)
    def _():
        dst[size_x - 1 : size_x] = jnp.zeros((1,) + dst.shape[1:], dst.dtype)

    @pl.when(ty == 0)
    def _():
        dst[:, 0:1] = jnp.zeros((size_x, 1) + dst.shape[2:], dst.dtype)

    @pl.when(ty == N_TY - 1)
    def _():
        dst[:, size_y - 1 : size_y] = jnp.zeros((size_x, 1) + dst.shape[2:], dst.dtype)


class Links:
    def __init__(self, send, recv):
        self.send, self.recv, self.sent = send, recv, []

    def start(self, src, dst, peer):
        k = len(self.sent)
        copy = pltpu.make_async_remote_copy(
            src_ref=src,
            dst_ref=dst,
            send_sem=self.send.at[k],
            recv_sem=self.recv.at[k],
            device_id=peer,
            device_id_type=MESH,
        )
        copy.start()
        self.sent.append(copy)
        return copy

    def halo(self, dst, peers, bufs, narrow):
        send_x, send_y, recv_x, recv_y = bufs
        size_x, size_y = dst.shape[0] - 2, dst.shape[1] - 2
        for n, (at_x, at_y) in enumerate(((1, 1), (size_x, size_y))):
            send_x[n] = squeeze(dst[at_x, 1 : size_y + 1], narrow)
            send_y[n] = squeeze(dst[1 : size_x + 1, at_y], narrow)
        copies = []
        for peer, (dx, dy) in zip(peers, STEPS):
            side = (dx + dy + 1) // 2
            if dy == 0:
                src, to = send_x.at[side], recv_x.at[1 - side]
            elif dx == 0:
                src, to = send_y.at[side], recv_y.at[1 - side]
            else:
                src = dst.at[edge_out(dx, size_x, 1), edge_out(dy, size_y, 1)]
                to = dst.at[edge_in(dx, size_x), edge_in(dy, size_y)]
            copies.append(self.start(src, to, peer))
        return copies


def halves(rows):
    return pl.ds(0, rows // 2), pl.ds(rows // 2, rows // 2)


class Gather:
    def __init__(self, links, where, shard, full, own):
        self.links, self.where, self.full = links, where, full
        self.first, self.second = halves(shard.shape[0])
        grp, tx, ty, hi, y, core = where
        self.cube = cube_peers(grp, tx, hi, y, core)
        mine = full.at[tx, hi, y, core]
        self.line = [links.start(shard, mine, peer) for peer in ring_peers(grp, tx, ty)]
        self.line += [links.start(shard, mine, peer) for peer in across_peers(grp, tx, hi, y, core)]
        self.own = pltpu.make_async_copy(shard, mine, own)
        self.own.start()
        self.partner = []

    def part(self, v, rows):
        return self.full.at[:, :, v, self.where[5], rows]

    def to_core(self, ref):
        self.partner.append(self.links.start(ref, ref, self.cube["core"]))

    def near(self):
        grp, tx, ty, hi, y, core = self.where
        self.own.wait()
        for copy in self.line:
            copy.wait_recv()
        first, second = self.part(y, self.first), self.part(y, self.second)
        self.step = [
            self.links.start(first, first, self.cube["y1"]),
            self.links.start(second, second, self.cube["y3"]),
        ]
        self.to_core(self.full.at[:, :, y, core])

    def far(self):
        y = self.where[4]
        y1, y3 = other(y, 1), other(y, 3)
        for copy in self.step:
            copy.wait_recv()
        self.step = []
        for v, rows, name in ((y, self.first, "y3"), (y1, self.first, "y3"), (y, self.second, "y1"), (y3, self.second, "y1")):
            self.step.append(self.links.start(self.part(v, rows), self.part(v, rows), self.cube[name]))
        self.to_core(self.part(y1, self.first))
        self.to_core(self.part(y3, self.second))

    def last(self):
        y = self.where[4]
        y1, y2, y3 = other(y, 1), other(y, 2), other(y, 3)
        arrived = [(y3, self.first), (y2, self.first), (y1, self.second), (y2, self.second)]
        for copy, (v, rows) in zip(self.step, arrived):
            copy.wait_recv()
            self.to_core(self.part(v, rows))

    def done(self):
        for copy in self.partner:
            copy.wait_recv()


class Scatter:
    def __init__(self, links, where, packed, total, sums, rd, ry2, ry1, rz, half, rg):
        self.links, self.where, self.packed, self.total = links, where, packed, total
        self.sums, self.rd, self.ry2, self.ry1 = sums, rd, ry2, ry1
        self.rz, self.half, self.rg = rz, half, rg
        grp, tx, ty, hi, y, core = where
        self.cube = cube_peers(grp, tx, hi, y, core)
        self.line = ring_peers(grp, tx, ty)
        rows = half.shape[1]
        self.whole, (self.first, self.second) = pl.ds(0, rows), halves(rows)
        self.pieces = {}
        self.ys = [other(y, 2), other(y, 3), other(y, 1), y]

    def add(self, z, h, v, rows, left, right):
        both = left[...].astype(f32) + right[...].astype(f32)
        self.sums[z, h, v, rows, :] = both.astype(bf16)

    def part(self, v, rows):
        return self.sums.at[:, :, v, rows]

    def wait(self):
        for copy in self.step:
            copy.wait_recv()

    def cores(self, pieces, h):
        core = self.where[5]
        for k in pieces:
            v = self.ys[k]
            copy = self.links.start(
                self.packed.at[:, h, v, 1 - core], self.rd.at[:, h, v], self.cube["core"]
            )
            self.pieces[k, h] = copy

    def far(self):
        core = self.where[5]
        y2, y3, y1, y = self.ys
        self.step = []
        for (k, h), copy in self.pieces.items():
            v = self.ys[k]
            copy.wait_recv()

            def take(z, carry):
                self.add(z, h, v, self.whole, self.packed.at[z, h, v, core], self.rd.at[z, h, v])
                return carry

            lax.fori_loop(0, 8, take, 0, unroll=2)
            if k in (1, 2):
                rows, name = (self.first, "y3") if k == 1 else (self.second, "y1")
                for n, u in enumerate((v, y2)):
                    self.step.append(
                        self.links.start(
                            self.sums.at[:, h, u, rows], self.ry2.at[n, :, h, rows], self.cube[name]
                        )
                    )

    def near(self):
        y2, y3, y1, y = self.ys
        far, self.step = self.step, []
        for h in range(2):
            for copy in far[2 * h : 2 * h + 2] + far[4 + 2 * h : 6 + 2 * h]:
                copy.wait_recv()

            def take(z, carry):
                self.add(z, h, y, self.whole, self.sums.at[z, h, y], self.ry2.at[0, z, h])
                self.add(z, h, y1, self.first, self.sums.at[z, h, y1, self.first], self.ry2.at[1, z, h, self.first])
                self.add(
                    z, h, y3, self.second, self.sums.at[z, h, y3, self.second], self.ry2.at[1, z, h, self.second]
                )
                return carry

            lax.fori_loop(0, 8, take, 0, unroll=2)
            for v, rows, name in ((y1, self.first, "y1"), (y3, self.second, "y3")):
                self.step.append(
                    self.links.start(self.sums.at[:, h, v, rows], self.ry1.at[:, h, rows], self.cube[name])
                )

    def along(self):
        tx, y = self.where[1], self.where[4]
        self.wait()

        def take(z, carry):
            for h in range(2):
                self.add(z, h, y, self.whole, self.sums.at[z, h, y], self.ry1.at[z, h])
            return carry

        lax.fori_loop(0, 8, take, 0)
        self.step = [
            self.links.start(self.sums.at[(tx + d + 1) % N_TX, :, y], self.rz.at[d], peer)
            for d, peer in enumerate(self.line)
        ]

    def swap(self):
        tx, hi, y = self.where[1], self.where[3], self.where[4]
        self.wait()
        for h in range(2):
            value = self.sums[tx, h, y].astype(f32)
            for d in range(N_TX - 1):
                value = value + self.rz[d, h].astype(f32)
            self.half[h] = value
        self.step = [
            self.links.start(self.half.at[hi], self.rg.at[0], self.cube["grp"]),
            self.links.start(self.half.at[1 - hi], self.rg.at[1], self.cube["x"]),
            self.links.start(self.half.at[1 - hi], self.rg.at[2], self.cube["xx"]),
        ]

    def done(self):
        self.wait()
        self.total[...] = (self.half[self.where[3]] + self.rg[0]) + (self.rg[1] + self.rg[2])


def fold(tiles):
    wide, mid, rest = tiles
    lanes = lax.broadcasted_iota(jnp.int32, (8, 128), 1)
    rows = lax.broadcasted_iota(jnp.int32, (8, 128), 0)
    tail = jnp.zeros((8, 128), f32)
    for n in range(4):
        piece = rest[8 * n : 8 * n + 8]
        piece = pltpu.roll(piece, 32 * n, 1) if n else piece
        tail = jnp.where((lanes >= 32 * n) & (lanes < 32 * n + 32), piece, tail)
    last = jnp.where(rows < 3, wide[24:32], jnp.where(rows < 6, pltpu.roll(mid[24:32], 3, 0), 0.0))
    return jnp.concatenate([wide[:24], mid[:24], tail, last], axis=0)


def unfold(rows):
    tail, last = rows[48:56], rows[56:64]
    rest = jnp.concatenate([tail] + [pltpu.roll(tail, 128 - 32 * n, 1) for n in range(1, 4)], axis=0)
    return [
        jnp.concatenate([rows[:24], last], axis=0),
        jnp.concatenate([rows[24:48], pltpu.roll(last, 5, 0)], axis=0),
        rest,
    ]


def choose(slots, place, blocks):
    value = None
    for i, block in enumerate(blocks):
        term = jnp.where(slots[0, i] == place, block, 0.0)
        value = term if value is None else value + term
    return value


def corner(slots, i):
    return slots[0, i] // GY, slots[0, i] % GY


def pack_shards(w_conv1, w_down, w_conv2, shard_a, shard_b, tmp, wide):
    tmp[...] = jnp.zeros_like(tmp)
    wide[...] = jnp.zeros_like(wide)
    tmp[0, 0:27, 0:72] = w_conv1[...].astype(f32)
    wide[0:8, 0:144] = w_down[...].astype(f32)
    low = lane_tiles(wide[0:8, 0:256])
    for j in range(3):
        tmp[1, pl.ds(j, 8, stride=3), :] = relane(1, [(low, 48 * j, BASE_DOWN, 48)])[0]
    shard_a[...] = (tmp[0] + tmp[1]).astype(bf16)
    wide[0:27, 0:288] = w_conv2[...].astype(f32)
    shard_b[...] = fold(lane_tiles(wide[...])).astype(bf16)


def prepare(slots, count, feats, occupancy, cot, mask, coarse, mp, gp, fine):
    flags = []
    for p in range(GX * GY):
        flag = jnp.where(slots[0, 0] == p, 1.0, 0.0)
        for i in range(1, CAP):
            flag = flag + jnp.where((slots[0, i] == p) & (count[0] > i), 1.0, 0.0)
        flags.append(flag)

    def iotas(rows, lanes):
        return [lax.broadcasted_iota(jnp.int32, (rows, lanes), d) for d in range(2)]

    row, lane = iotas(256, 8)
    pick_z = jnp.where(row % 8 == lane, 1.0, 0.0).astype(bf16)
    row, lane = iotas(256, 32)
    pick_y = row // 8 == lane
    row, lane = iotas(128, 8)
    pair_z = jnp.where(row % 8 == lane // 2, 1.0, 0.0).astype(bf16)
    row, lane = iotas(128, 32)
    pair_y = row // 8 == lane // 2
    ones = jnp.ones((32, 256), bf16)
    if fine:
        mp[1:17, 1:33] = jnp.zeros((16, 32, 8, 128), f32)
    else:
        gp[1:9, 1:17] = jnp.zeros((8, 16, 8, 256), f32)
    for px in range(GX) if fine else ():

        def first(x, carry):
            plane = occupancy[0, x].astype(f32).astype(bf16)
            column = jnp.dot(pick_z, plane, preferred_element_type=f32)
            column = jnp.where(pick_y, column, 0.0).astype(bf16)
            value = jnp.dot(column, ones[:, :128], preferred_element_type=f32).reshape(32, 8, 128)
            for py in range(GY):
                at = slice(py * 8, py * 8 + 8)
                live = value[at] * flags[px * GY + py]
                mask[x, at] = live
                mp[1 + x, 1 + py * 8 : 9 + py * 8, :, 0:C1] = feats[0, x, at].astype(f32) * live[:, :, 0:C1]
            return carry

        lax.fori_loop(px * 8, px * 8 + 8, first, 0, unroll=4)

    for px in range(GX) if not fine else ():

        def second(a, carry):
            plane = (occupancy[0, 2 * a] + occupancy[0, 2 * a + 1]).astype(f32).astype(bf16)
            column = jnp.dot(pair_z, plane, preferred_element_type=f32)
            column = jnp.where(pair_y, column, 0.0).astype(bf16)
            value = jnp.minimum(jnp.dot(column, ones, preferred_element_type=f32), 1.0).reshape(16, 8, 256)
            for py in range(GY):
                at = slice(py * 4, py * 4 + 4)
                live = value[at] * flags[px * GY + py]
                coarse[a, at] = live
                grad = cot[0, a, at].astype(f32) * live[:, 0:4, 0:C2]
                gp[1 + a, 1 + py * 4 : 5 + py * 4, 0:4, 0:C2] = grad
            return carry

        lax.fori_loop(px * 4, px * 4 + 4, second, 0, unroll=4)


def unpack_first(full, w9, wd, w1g, wdg, tmp):
    def unpack(a, carry):
        shards = []
        for b in range(4):
            value = full[a // 4, (a // 2) % 2, (a % 2) * 2 + b // 2, b % 2]
            tmp[b] = value.astype(f32)
            shards.append([value])
        for k in range(3):
            w1g[pl.ds((a * 3 + k) * PITCH_W, 32), :] = to_row(shards, PIECES_ONE[k], 0, 1)[0].astype(f32)
        chunks = [[tmp[b, pl.ds(j, 8, stride=3), :]] for b in range(4) for j in range(3)]
        for k in range(3):
            segments = [(chunks[4 * k + n], BASE_DOWN, 48 * n, 48) for n in range(4)]
            for c, tile in enumerate(relane(2, segments)):
                wdg[c, pl.ds(pl.multiple_of((a * 3 + k) * 8, 8), 8), :] = tile
        return carry

    lax.fori_loop(0, GROUPS, unpack, 0, unroll=4)
    for t in range(27):
        k, oz = t // 3, t % 3
        w9[k * 128 : k * 128 + C1, oz * 128 : (oz + 1) * 128] = w1g[pl.ds(t, C1, stride=PITCH_W), :].astype(bf16)
    for k in range(9):
        w9[k * 128 + C1 : (k + 1) * 128, :] = jnp.zeros((128 - C1, 384), bf16)
    for t in range(8):
        for c in range(2):
            wd[t * 128 : t * 128 + C1, c * 128 : (c + 1) * 128] = wdg[c, pl.ds(t, C1, stride=8), :].astype(bf16)
        wd[t * 128 + C1 : (t + 1) * 128, :] = jnp.zeros((128 - C1, 256), bf16)


def unpack_second(full, w2, big):
    def unpack(a, carry):
        shards = [
            [
                tile.astype(bf16)
                for tile in unfold(full[a // 4, (a // 2) % 2, (a % 2) * 2 + b // 2, b % 2].astype(f32))
            ]
            for b in range(4)
        ]
        for k in range(6):
            for c, tile in enumerate(to_row(shards, PIECES_TWO[k], 0, 2)):
                big[c, pl.ds((a * 6 + k) * PITCH_W, 32), :] = tile.astype(f32)
        return carry

    lax.fori_loop(0, GROUPS, unpack, 0, unroll=4)

    def order(k, carry):
        for oz in range(3):
            for c in range(2):
                w2[pl.ds(pl.multiple_of(k * 256, 256), C2), oz * 256 + c * 128 : oz * 256 + (c + 1) * 128] = big[
                    c, pl.ds(k * 3 + oz, C2, stride=PITCH_W), :
                ].astype(bf16)
        w2[pl.ds(pl.multiple_of(k * 256 + C2, 64), 256 - C2), :] = jnp.zeros((256 - C2, 768), bf16)
        return carry

    lax.fori_loop(0, 9, order, 0, unroll=3)


def windows(dst, i, window, edge, flip):
    lanes = window.shape[-1]
    rows = edge * edge * 8
    for k in range(9):
        ox, oy = k // 3, k % 3
        if flip:
            ox, oy = 2 - ox, 2 - oy
        piece = window[ox : ox + edge, oy : oy + edge].reshape(rows, lanes)
        dst[i * rows : (i + 1) * rows, k * lanes : (k + 1) * lanes] = piece.astype(bf16)


def three(rows, lanes):
    return [rows[:, n * lanes : (n + 1) * lanes].reshape(-1, 8, lanes) for n in range(3)]


def conv(parts):
    low, mid, high = parts
    return (depth_shifts(low)[0] + mid + depth_shifts(high)[2]).reshape(-1, mid.shape[-1])


def spread(value):
    below, mid, above = depth_shifts(value.reshape(-1, 8, value.shape[-1]))
    return jnp.concatenate([v.reshape(value.shape).astype(bf16) for v in (above, mid, below)], axis=1)


def pack_first(packed, r1, rdn, tmp, pair, h):
    def pack(z, carry):
        a = z * 4 + h * 2 + pair
        segments = [[] for _ in range(4)]
        downs = []
        for k in range(3):
            ci = a * 3 + k
            tiles = [r1[pl.ds(ci, 32, stride=PITCH_S), :].astype(bf16)]
            for s, at, lane, n in PIECES_ONE[k]:
                segments[s].append((tiles, lane, at, n))
            downs.append([rdn[c, pl.ds(ci, 8, stride=PITCH_S), :] for c in range(2)])
        for b in range(4):
            for j in range(3):
                m = 3 * b + j
                tmp[b, pl.ds(j, 8, stride=3), :] = relane(1, [(downs[m // 4], m % 4 * 48, BASE_DOWN, 48)])[0]
            value = relane(1, segments[b])[0].astype(f32) + tmp[b]
            packed[z, h, pair * 2 + b // 2, b % 2] = value.astype(bf16)
        return carry

    lax.fori_loop(0, 8, pack, 0, unroll=4)


def pack_second(packed, big, pair, h):
    def pack(z, carry):
        a = z * 4 + h * 2 + pair
        segments = [[] for _ in range(4)]
        for k in range(6):
            tiles = [big[c, pl.ds(a * 6 + k, 32, stride=PITCH_R), :].astype(bf16) for c in range(2)]
            for s, at, lane, n in PIECES_TWO[k]:
                segments[s].append((tiles, lane, at, n))
        for b in range(4):
            packed[z, h, pair * 2 + b // 2, b % 2] = fold(
                [tile.astype(f32) for tile in relane(3, segments[b])]
            ).astype(bf16)
        return carry

    lax.fori_loop(0, 8, pack, 0, unroll=4)


def whole_kernel(
    slots, count, feats_in, occupancy_in, cot_in, w_conv1, w_down, w_conv2, out, grad_conv1, grad_down, grad_conv2,
    feats, occupancy, cot, total_a, total_b, mask, coarse, shard_a, shard_b, wide,
    full_a, full_b, mp, gp, dp, x9, x2, x3, w9, wd, w2, w1g, wdg, tmp, big, act, pm, hs, gs, r1, rdn,
    packed_a, packed_b, sums_a, rd_a, ry2_a, ry1_a, rz_a, half_a, rg_a,
    sums_b, rd_b, ry2_b, ry1_b, rz_b, half_b, rg_b, *rest,
):
    bufs_m, bufs_g, bufs_d = rest[0:4], rest[4:8], rest[8:12]
    send, recv, own = rest[12:]
    where = place()
    grp, tx, ty, hi, y, core = where
    cube = cube_peers(grp, tx, hi, y, core)
    around = halo_peers(grp, tx, ty)
    links = Links(send, recv)
    loads = [
        pltpu.make_async_copy(src, dst, own.at[2 + k])
        for k, (src, dst) in enumerate(((feats_in, feats), (occupancy_in, occupancy), (cot_in, cot)))
    ]
    for load in loads:
        load.start()
    greeted = ring_peers(grp, tx, ty) + across_peers(grp, tx, hi, y, core) + [cube[n] for n in ("core", "y1", "y3", "xx", "grp")] + around
    barrier = pltpu.get_barrier_semaphore()
    for peer in greeted:
        pl.semaphore_signal(barrier, inc=1, device_id=peer, device_id_type=MESH)
    pack_shards(w_conv1, w_down, w_conv2, shard_a, shard_b, tmp, wide)
    pl.semaphore_wait(barrier, len(greeted))

    first = Gather(links, where, shard_a, full_a, own.at[0])
    second = Gather(links, where, shard_b, full_b, own.at[1])
    for load in loads:
        load.wait()
    prepare(slots, count, feats, occupancy, cot, mask, coarse, mp, gp, True)
    halo_m = links.halo(mp, around, bufs_m, False)
    first.near()
    prepare(slots, count, feats, occupancy, cot, mask, coarse, mp, gp, False)
    second.near()
    first.far()
    halo_g = links.halo(gp, around, bufs_g, True)
    land(mp, halo_m, bufs_m, False)
    clear_edges(mp, tx, ty)
    for i in range(CAP):
        px, py = corner(slots, i)
        windows(x9, i, mp[pl.ds(px * 8, 10), pl.ds(py * 8, 10)], 8, False)
    second.far()
    first.last()
    hs[...] = jnp.zeros_like(hs)
    rdn[...] = jnp.zeros_like(rdn)
    r1[27 * PITCH_S : 32 * PITCH_S, :] = jnp.zeros((5 * PITCH_S, 128), f32)
    big[:, 27 * PITCH_R : 32 * PITCH_R, :] = jnp.zeros((2, 5 * PITCH_R, 128), f32)
    first.done()
    unpack_first(full_a, w9, wd, w1g, wdg, tmp)

    lives, edges = [], []
    for i in range(CAP):
        px, py = corner(slots, i)
        lives.append(mask[pl.ds(px * 8, 8), pl.ds(py * 8, 8)].reshape(512, 128))
        edges.append(coarse[pl.ds(px * 4, 4), pl.ds(py * 4, 4)].reshape(128, 256))
    live = jnp.concatenate(lives, axis=0)
    edge = jnp.concatenate(edges, axis=0)
    value = conv(three(jnp.dot(x9[...], w9[...], preferred_element_type=f32), 128))
    act[...] = value
    hidden = (live * jax.nn.silu(value)).astype(bf16).astype(f32).reshape(CAP, 4, 2, 4, 2, 8, 128)
    for p in range(2):
        for q in range(2):
            for b in range(4):
                hs[:, :, p * 2 + q, b * 16 : b * 16 + 8, :] = hidden[:, :, p, b, q]
    second.last()
    for t in range(8):
        patch = hs[:, :, t // 2, pl.ds(t % 2, 32, stride=2), :].reshape(256, 128)
        pm[:, t * 128 : (t + 1) * 128] = patch.astype(bf16)
    raw = jnp.dot(pm[...], wd[...], preferred_element_type=f32)
    down = (edge * raw).astype(bf16).astype(f32)
    downs = [down[i * 128 : (i + 1) * 128].reshape(4, 4, 8, 256) for i in range(CAP)]
    for p in range(GX * GY):
        px, py = p // GY, p % GY
        dp[1 + px * 4 : 5 + px * 4, 1 + py * 4 : 5 + py * 4] = choose(slots, p, downs)
    halo_d = links.halo(dp, around, bufs_d, True)

    land(gp, halo_g, bufs_g, True)
    clear_edges(gp, tx, ty)
    grads = []
    for i in range(CAP):
        px, py = corner(slots, i)
        windows(x3, i, gp[pl.ds(px * 4, 6), pl.ds(py * 4, 6)], 4, True)
        grads.append(gp[pl.ds(px * 4 + 1, 4), pl.ds(py * 4 + 1, 4)].reshape(128, 256))
    grad_two = jnp.concatenate(grads, axis=0)
    spread_two = spread(grad_two)
    second.done()
    unpack_second(full_b, w2, big)
    parts = []
    for oz in range(3):
        part = None
        for k in range(9):
            term = lax.dot_general(
                x3[:, k * 256 : (k + 1) * 256],
                w2[k * 256 : (k + 1) * 256, oz * 256 : (oz + 1) * 256],
                (((1,), (1,)), ((), ())),
                preferred_element_type=f32,
            )
            part = term if part is None else part + term
        parts.append(part.reshape(-1, 8, 256))
    back = conv(parts[::-1])
    grad_in = (grad_two + edge * back).astype(bf16)
    land(dp, halo_d, bufs_d, True)
    clear_edges(dp, tx, ty)
    for i in range(CAP):
        px, py = corner(slots, i)
        windows(x2, i, dp[pl.ds(px * 4, 6), pl.ds(py * 4, 6)], 4, False)
    for k in range(9):
        product = lax.dot_general(
            x2[:, k * 256 : (k + 1) * 256], spread_two, (((0,), (0,)), ((), ())), preferred_element_type=f32
        )
        for oz in range(3):
            for c in range(2):
                at = oz * 256 + c * 128
                big[c, (3 * k + oz) * PITCH_R : (3 * k + oz) * PITCH_R + 256, :] = product[:, at : at + 128]
    sum_b = Scatter(links, where, packed_b, total_b, sums_b, rd_b, ry2_b, ry1_b, rz_b, half_b, rg_b)
    for pair, pieces in ((1 - y // 2, (0, 1)), (y // 2, (2, 3))):
        for h in range(2):
            pack_second(packed_b, big, pair, h)
            sum_b.cores(pieces, h)

    for t in range(8):
        product = lax.dot_general(
            pm[:, t * 128 : (t + 1) * 128], grad_in, (((0,), (0,)), ((), ())), preferred_element_type=f32
        )
        for c in range(2):
            rdn[c, t * PITCH_S : t * PITCH_S + 128, :] = product[:, c * 128 : (c + 1) * 128]
    for t in range(8):
        part = lax.dot_general(
            grad_in, wd[t * 128 : (t + 1) * 128, :], (((1,), (1,)), ((), ())), preferred_element_type=f32
        )
        gs[:, :, t // 2, pl.ds(t % 2, 32, stride=2), :] = part.reshape(CAP, 4, 32, 128)
    sum_b.far()
    rows = []
    for p in range(2):
        for b in range(4):
            for q in range(2):
                rows.append(gs[:, :, p * 2 + q, b * 16 : b * 16 + 8, :])
    hidden = jnp.stack(rows, axis=2).reshape(1024, 128)
    value = act[...]
    sig = jax.nn.sigmoid(value)
    spread_one = spread(live * hidden * (sig * (1.0 + value * (1.0 - sig))))
    for k in range(9):
        product = lax.dot_general(
            x9[:, k * 128 : (k + 1) * 128], spread_one, (((0,), (0,)), ((), ())), preferred_element_type=f32
        )
        for oz in range(3):
            at = (3 * k + oz) * PITCH_S
            r1[at : at + 128, :] = product[:, oz * 128 : (oz + 1) * 128]
    tmp[...] = jnp.zeros_like(tmp)
    sum_a = Scatter(links, where, packed_a, total_a, sums_a, rd_a, ry2_a, ry1_a, rz_a, half_a, rg_a)
    for pair, pieces in ((1 - y // 2, (0, 1)), (y // 2, (2, 3))):
        for h in range(2):
            pack_first(packed_a, r1, rdn, tmp, pair, h)
            sum_a.cores(pieces, h)
    sum_b.near()

    parts = [
        jnp.dot(x2[...], w2[:, oz * 256 : (oz + 1) * 256], preferred_element_type=f32).reshape(-1, 8, 256)
        for oz in range(2)
    ]
    sum_a.far()
    parts.append(jnp.dot(x2[...], w2[:, 512:768], preferred_element_type=f32).reshape(-1, 8, 256))
    value = conv(parts)
    sum_b.along()
    blocks = []
    for i in range(CAP):
        px, py = corner(slots, i)
        down = dp[pl.ds(px * 4 + 1, 4), pl.ds(py * 4 + 1, 4)].reshape(128, 256)
        rows = slice(i * 128, (i + 1) * 128)
        blocks.append((edges[i] * (down + value[rows])).reshape(4, 4, 8, 256))
    sum_a.near()
    for p in range(GX * GY):
        px, py = p // GY, p % GY
        out[0, px * 4 : px * 4 + 4, py * 4 : py * 4 + 4] = choose(slots, p, blocks)[:, :, 0:4, 0:C2].astype(bf16)
    sum_a.along()
    sum_b.swap()
    sum_a.swap()
    sum_b.done()
    wide = unfold(total_b[...])
    grad_conv2[:, 0:256] = jnp.concatenate(wide[:2], axis=1)[:27]
    grad_conv2[:, 256:288] = wide[2][:27, :32]
    sum_a.done()
    grad_conv1[...] = total_a[:27, :72]
    low = [(total_a[pl.ds(j, 8, stride=3), :],) for j in range(3)]
    low = relane(2, [(low[j], BASE_DOWN, 48 * j, 48) for j in range(3)])
    grad_down[:, 0:128] = low[0]
    grad_down[:, 128:144] = low[1][:, :16]
    for copy in links.sent:
        copy.wait_send()


def whole(order, count, feats, occupancy, cot, w_conv1, w_down, w_conv2):
    def sums(rows):
        return [
            pltpu.VMEM((8, 2, 4, rows, 128), bf16),
            pltpu.VMEM((8, 2, 4, rows, 128), bf16),
            pltpu.VMEM((2, 8, 2, rows, 128), bf16),
            pltpu.VMEM((8, 2, rows, 128), bf16),
            pltpu.VMEM((7, 2, rows, 128), bf16),
            pltpu.VMEM((2, rows, 128), f32),
            pltpu.VMEM((3, rows, 128), f32),
        ]

    copies = 2 * 30 + 24 + 2 * 30
    return pl.pallas_call(
        whole_kernel,
        in_specs=[pl.BlockSpec(memory_space=pltpu.SMEM)] * 2
        + [pl.BlockSpec(memory_space=pl.ANY)] * 3
        + [pl.BlockSpec(memory_space=pltpu.VMEM)] * 3,
        out_specs=[pl.BlockSpec(memory_space=pltpu.VMEM)] * 4,
        out_shape=[
            jax.ShapeDtypeStruct((1, 8, 16, 4, C2), bf16),
            jax.ShapeDtypeStruct((27, 72), f32),
            jax.ShapeDtypeStruct((8, 144), f32),
            jax.ShapeDtypeStruct((27, 288), f32),
        ],
        scratch_shapes=[
            pltpu.VMEM((1, 16, 32, 8, C1), bf16),
            pltpu.VMEM((1, 16, 8, 32), jnp.int32),
            pltpu.VMEM((1, 8, 16, 4, C2), bf16),
            pltpu.VMEM((32, 128), f32),
            pltpu.VMEM((64, 128), f32),
            pltpu.VMEM((16, 32, 8, 128), f32),
            pltpu.VMEM((8, 16, 8, 256), f32),
            pltpu.VMEM((32, 128), bf16),
            pltpu.VMEM((64, 128), bf16),
            pltpu.VMEM((32, 384), f32),
            pltpu.VMEM((8, 2, 4, 2, 32, 128), bf16),
            pltpu.VMEM((8, 2, 4, 2, 64, 128), bf16),
            pltpu.VMEM((18, 34, 8, 128), f32),
            pltpu.VMEM((10, 18, 8, 256), f32),
            pltpu.VMEM((10, 18, 8, 256), f32),
            pltpu.VMEM((1024, 9 * 128), bf16),
            pltpu.VMEM((256, 9 * 256), bf16),
            pltpu.VMEM((256, 9 * 256), bf16),
            pltpu.VMEM((9 * 128, 384), bf16),
            pltpu.VMEM((1024, 256), bf16),
            pltpu.VMEM((9 * 256, 768), bf16),
            pltpu.VMEM((C1 * PITCH_W + 8, 128), f32),
            pltpu.VMEM((2, C1 * 8, 128), f32),
            pltpu.VMEM((4, 32, 128), f32),
            pltpu.VMEM((2, 32 * PITCH_R, 128), f32),
            pltpu.VMEM((1024, 128), f32),
            pltpu.VMEM((256, 1024), bf16),
            pltpu.VMEM((CAP, 4, 4, 64, 128), f32),
            pltpu.VMEM((CAP, 4, 4, 64, 128), f32),
            pltpu.VMEM((32 * PITCH_S, 128), f32),
            pltpu.VMEM((2, 8 * PITCH_S, 128), f32),
            pltpu.VMEM((8, 2, 4, 2, 32, 128), bf16),
            pltpu.VMEM((8, 2, 4, 2, 64, 128), bf16),
        ]
        + sums(32)
        + sums(64)
        + [
            pltpu.VMEM((2, rows, lanes), bf16)
            for sides, lanes in (((256, 128), 128), ((64, 32), 256), ((64, 32), 256))
            for rows in sides + sides
        ]
        + [
            pltpu.SemaphoreType.DMA((copies,)),
            pltpu.SemaphoreType.DMA((copies,)),
            pltpu.SemaphoreType.DMA((5,)),
        ],
        compiler_params=pltpu.CompilerParams(collective_id=0, has_side_effects=True, vmem_limit_bytes=VMEM_LIMIT),
        name="whole",
    )(order, count, feats, occupancy, cot, w_conv1, w_down, w_conv2)


def local(features, voxel_mask, brick_order, brick_count, w_conv1, w_down, w_conv2, cotangent):
    return tuple(
        whole(brick_order, brick_count, features, voxel_mask.transpose(0, 1, 3, 2), cotangent, w_conv1, w_down, w_conv2)
    )


def solution(mesh):
    return jax.shard_map(
        local,
        mesh=mesh,
        in_specs=(
            P("grp", "tx", "ty", None, None),
            P("grp", "tx", "ty", None),
            P(("grp", "tx", "ty"), None),
            P(("grp", "tx", "ty")),
            P(None, ("tx", "ty")),
            P(None, ("tx", "ty")),
            P(None, ("tx", "ty")),
            P("grp", "tx", "ty", None, None),
        ),
        out_specs=(
            P("grp", "tx", "ty", None, None),
            P(None, ("tx", "ty")),
            P(None, ("tx", "ty")),
            P(None, ("tx", "ty")),
        ),
        check_vma=False,
    )
```

```python
import jax
import jax.numpy as jnp
from jax import lax
from jax.experimental import pallas as pl
from jax.experimental.pallas import tpu as pltpu
from jax.sharding import PartitionSpec as P

C1 = 96
C2 = 192
GX = 2
GY = 4
CAP = 2
GROUPS = 32
N_TX = 8
N_TY = 16
PITCH_W = 33
PITCH_R = 264
PITCH_S = 136
MESH = pl.DeviceIdType.MESH
f32 = jnp.float32
bf16 = jnp.bfloat16
TAPS = [(ox, oy, oz) for ox in range(3) for oy in range(3) for oz in range(3)]
VMEM_LIMIT = 60 * 1024 * 1024


def lane_tiles(rows):
    return [rows[:, i * 128 : (i + 1) * 128] for i in range(rows.shape[1] // 128)]


def relane(count, segments):
    lanes = lax.broadcasted_iota(jnp.int32, segments[0][0][0].shape, 1)
    out = [None] * count
    rolled = {}
    for tiles, src, dst, length in segments:
        while length > 0:
            step = min(length, 128 - src % 128, 128 - dst % 128)
            tile, shift = tiles[src // 128], (dst - src) % 128
            key = (id(tile), shift)
            if key not in rolled:
                rolled[key] = pltpu.roll(tile, shift, 1) if shift else tile
            low, high, target = dst % 128, dst % 128 + step, dst // 128
            base = jnp.zeros_like(tile) if out[target] is None else out[target]
            if step == 128:
                out[target] = rolled[key]
            else:
                inside = lanes < high
                if low:
                    inside = inside & (lanes >= low)
                out[target] = jnp.where(inside, rolled[key], base)
            src, dst, length = src + step, dst + step, length - step
    return [jnp.zeros_like(segments[0][0][0]) if t is None else t for t in out]


PIECES_ONE = [[(0, 0, 0, 72), (1, 0, 72, 24)], [(1, 24, 0, 48), (2, 0, 48, 48)], [(2, 48, 0, 24), (3, 0, 24, 72)]]
PIECES_TWO = [
    [(0, 0, 0, 192)],
    [(0, 192, 0, 96), (1, 0, 96, 96)],
    [(1, 96, 0, 192)],
    [(2, 0, 0, 192)],
    [(2, 192, 0, 96), (3, 0, 96, 96)],
    [(3, 96, 0, 192)],
]
BASE_DOWN = 72


def to_row(shards, pieces, base, count):
    return relane(count, [(shards[s], base + a, b, n) for s, a, b, n in pieces])


def join(tiles):
    return tiles[0] if len(tiles) == 1 else jnp.concatenate(tiles, axis=1)


def depth_shifts(slab):
    axis = slab.ndim - 2
    depth = lax.broadcasted_iota(jnp.int32, slab.shape, axis)
    below = jnp.where(depth == 0, 0.0, pltpu.roll(slab, 1, axis))
    above = jnp.where(depth == 7, 0.0, pltpu.roll(slab, 7, axis))
    return below, slab, above


def barrier_with(peers):
    barrier = pltpu.get_barrier_semaphore()
    for peer in peers:
        pl.semaphore_signal(barrier, inc=1, device_id=peer, device_id_type=MESH)
    pl.semaphore_wait(barrier, len(peers))


def place():
    grp, tx, ty = lax.axis_index("grp"), lax.axis_index("tx"), lax.axis_index("ty")
    return grp, tx, ty, ty // 8, (ty // 2) % 4, ty % 2


def other(value, bits):
    if bits == 1:
        return value + 1 - 2 * (value % 2)
    if bits == 2:
        return (value + 2) % 4
    return 3 - value


def ring_peers(grp, tx, ty):
    return [(grp, (tx + d) % N_TX, ty) for d in range(1, N_TX)]


def across_peers(grp, tx, hi, y, core):
    return [(1 - grp, (tx + d) % N_TX, (1 - hi) * 8 + y * 2 + core) for d in range(N_TX)]


def cube_peers(grp, tx, hi, y, core):
    def ty_of(h, v, c):
        return h * 8 + v * 2 + c

    return {
        "core": (grp, tx, ty_of(hi, y, 1 - core)),
        "y1": (grp, tx, ty_of(hi, other(y, 1), core)),
        "y3": (grp, tx, ty_of(hi, other(y, 3), core)),
        "x": (1 - grp, tx, ty_of(1 - hi, y, core)),
        "xx": (grp, tx, ty_of(1 - hi, y, core)),
        "grp": (1 - grp, tx, ty_of(hi, y, core)),
    }


STEPS = [(dx, dy) for dx in (-1, 0, 1) for dy in (-1, 0, 1) if dx or dy]


def halo_peers(grp, tx, ty):
    return [(grp, (tx + dx + N_TX) % N_TX, (ty + dy + N_TY) % N_TY) for dx, dy in STEPS]


def edge_out(step, size, shift):
    return pl.ds(shift, 1) if step < 0 else pl.ds(size - 1 + shift, 1) if step > 0 else pl.ds(shift, size)


def edge_in(step, size):
    return pl.ds(size + 1, 1) if step < 0 else pl.ds(0, 1) if step > 0 else pl.ds(1, size)


def squeeze(slabs, narrow):
    if narrow:
        pairs = slabs.reshape(slabs.shape[0] // 2, 2, 8, slabs.shape[2])
        slabs = pairs[:, 0] + pltpu.roll(pairs[:, 1], 4, 1)
    return slabs.reshape(-1, slabs.shape[2]).astype(bf16)


def widen(rows, narrow):
    slabs = rows.astype(f32).reshape(-1, 8, rows.shape[1])
    if not narrow:
        return slabs
    low = lax.broadcasted_iota(jnp.int32, slabs.shape, 1) < 4
    pairs = [jnp.where(low, slabs, 0.0), jnp.where(low, pltpu.roll(slabs, 4, 1), 0.0)]
    return jnp.stack(pairs, axis=1).reshape(-1, 8, rows.shape[1])


def land(dst, copies, bufs, narrow):
    size_x, size_y = dst.shape[0] - 2, dst.shape[1] - 2
    for copy in copies:
        copy.wait_recv()
    for n, (at_x, at_y) in enumerate(((0, 0), (size_x + 1, size_y + 1))):
        side_x, side_y = widen(bufs[2][n], narrow), widen(bufs[3][n], narrow)
        dst[at_x : at_x + 1, 1 : size_y + 1] = side_x.reshape(1, size_y, 8, -1)
        dst[1 : size_x + 1, at_y : at_y + 1] = side_y.reshape(size_x, 1, 8, -1)


def clear_edges(dst, tx, ty):
    size_x, size_y = dst.shape[0], dst.shape[1]

    @pl.when(tx == 0)
    def _():
        dst[0:1] = jnp.zeros((1,) + dst.shape[1:], dst.dtype)

    @pl.when(tx == N_TX - 1)
    def _():
        dst[size_x - 1 : size_x] = jnp.zeros((1,) + dst.shape[1:], dst.dtype)

    @pl.when(ty == 0)
    def _():
        dst[:, 0:1] = jnp.zeros((size_x, 1) + dst.shape[2:], dst.dtype)

    @pl.when(ty == N_TY - 1)
    def _():
        dst[:, size_y - 1 : size_y] = jnp.zeros((size_x, 1) + dst.shape[2:], dst.dtype)


class Links:
    def __init__(self, send, recv):
        self.send, self.recv, self.sent, self.left = send, recv, [], 0

    def start(self, src, dst, peer):
        k = len(self.sent)
        copy = pltpu.make_async_remote_copy(
            src_ref=src,
            dst_ref=dst,
            send_sem=self.send.at[k],
            recv_sem=self.recv.at[k],
            device_id=peer,
            device_id_type=MESH,
        )
        copy.start()
        self.sent.append(copy)
        return copy

    def flush(self, upto):
        for copy in self.sent[self.left : upto]:
            copy.wait_send()
        self.left = upto

    def halo(self, dst, peers, bufs, narrow):
        send_x, send_y, recv_x, recv_y = bufs
        size_x, size_y = dst.shape[0] - 2, dst.shape[1] - 2
        for n, (at_x, at_y) in enumerate(((1, 1), (size_x, size_y))):
            send_x[n] = squeeze(dst[at_x, 1 : size_y + 1], narrow)
            send_y[n] = squeeze(dst[1 : size_x + 1, at_y], narrow)
        copies = []
        for peer, (dx, dy) in zip(peers, STEPS):
            side = (dx + dy + 1) // 2
            if dy == 0:
                src, to = send_x.at[side], recv_x.at[1 - side]
            elif dx == 0:
                src, to = send_y.at[side], recv_y.at[1 - side]
            else:
                src = dst.at[edge_out(dx, size_x, 1), edge_out(dy, size_y, 1)]
                to = dst.at[edge_in(dx, size_x), edge_in(dy, size_y)]
            copies.append(self.start(src, to, peer))
        return copies


def halves(rows):
    return pl.ds(0, rows // 2), pl.ds(rows // 2, rows // 2)


class Gather:
    def __init__(self, links, where, shard, full, own):
        self.links, self.where, self.full = links, where, full
        self.first, self.second = halves(shard.shape[0])
        grp, tx, ty, hi, y, core = where
        self.cube = cube_peers(grp, tx, hi, y, core)
        mine = full.at[tx, hi, y, core]
        self.line = [links.start(shard, mine, peer) for peer in ring_peers(grp, tx, ty)]
        self.line += [links.start(shard, mine, peer) for peer in across_peers(grp, tx, hi, y, core)]
        self.own = pltpu.make_async_copy(shard, mine, own)
        self.own.start()
        self.partner = []

    def part(self, v, rows):
        return self.full.at[:, :, v, self.where[5], rows]

    def to_core(self, ref):
        self.partner.append(self.links.start(ref, ref, self.cube["core"]))

    def near(self):
        grp, tx, ty, hi, y, core = self.where
        self.own.wait()
        for copy in self.line:
            copy.wait_recv()
        first, second = self.part(y, self.first), self.part(y, self.second)
        self.step = [
            self.links.start(first, first, self.cube["y1"]),
            self.links.start(second, second, self.cube["y3"]),
        ]
        self.to_core(self.full.at[:, :, y, core])

    def far(self):
        y = self.where[4]
        y1, y3 = other(y, 1), other(y, 3)
        for copy in self.step:
            copy.wait_recv()
        self.step = []
        for v, rows, name in ((y, self.first, "y3"), (y1, self.first, "y3"), (y, self.second, "y1"), (y3, self.second, "y1")):
            self.step.append(self.links.start(self.part(v, rows), self.part(v, rows), self.cube[name]))
        self.to_core(self.part(y1, self.first))
        self.to_core(self.part(y3, self.second))

    def last(self):
        y = self.where[4]
        y1, y2, y3 = other(y, 1), other(y, 2), other(y, 3)
        arrived = [(y3, self.first), (y2, self.first), (y1, self.second), (y2, self.second)]
        for copy, (v, rows) in zip(self.step, arrived):
            copy.wait_recv()
            self.to_core(self.part(v, rows))

    def done(self):
        for copy in self.partner:
            copy.wait_recv()


class Scatter:
    def __init__(self, links, where, packed, total, sums, rd, ry2, ry1, rz, half, rg):
        self.links, self.where, self.packed, self.total = links, where, packed, total
        self.sums, self.rd, self.ry2, self.ry1 = sums, rd, ry2, ry1
        self.rz, self.half, self.rg = rz, half, rg
        grp, tx, ty, hi, y, core = where
        self.cube = cube_peers(grp, tx, hi, y, core)
        self.line = ring_peers(grp, tx, ty)
        rows = half.shape[1]
        self.whole, (self.first, self.second) = pl.ds(0, rows), halves(rows)
        self.pieces = {}
        self.ys = [other(y, 2), other(y, 3), other(y, 1), y]

    def add(self, z, h, v, rows, left, right):
        both = left[...].astype(f32) + right[...].astype(f32)
        self.sums[z, h, v, rows, :] = both.astype(bf16)

    def part(self, v, rows):
        return self.sums.at[:, :, v, rows]

    def wait(self):
        for copy in self.step:
            copy.wait_recv()

    def cores(self, pieces, h):
        core = self.where[5]
        for k in pieces:
            v = self.ys[k]
            copy = self.links.start(
                self.packed.at[:, h, v, 1 - core], self.rd.at[:, h, v], self.cube["core"]
            )
            self.pieces[k, h] = copy

    def far(self):
        core = self.where[5]
        y2, y3, y1, y = self.ys
        self.step = []
        for (k, h), copy in self.pieces.items():
            v = self.ys[k]
            copy.wait_recv()

            def take(z, carry):
                self.add(z, h, v, self.whole, self.packed.at[z, h, v, core], self.rd.at[z, h, v])
                return carry

            lax.fori_loop(0, 8, take, 0, unroll=2)
            if k in (1, 2):
                rows, name = (self.first, "y3") if k == 1 else (self.second, "y1")
                for n, u in enumerate((v, y2)):
                    self.step.append(
                        self.links.start(
                            self.sums.at[:, h, u, rows], self.ry2.at[n, :, h, rows], self.cube[name]
                        )
                    )

    def near(self):
        y2, y3, y1, y = self.ys
        far, self.step = self.step, []
        for h in range(2):
            for copy in far[2 * h : 2 * h + 2] + far[4 + 2 * h : 6 + 2 * h]:
                copy.wait_recv()

            def take(z, carry):
                self.add(z, h, y, self.whole, self.sums.at[z, h, y], self.ry2.at[0, z, h])
                self.add(z, h, y1, self.first, self.sums.at[z, h, y1, self.first], self.ry2.at[1, z, h, self.first])
                self.add(
                    z, h, y3, self.second, self.sums.at[z, h, y3, self.second], self.ry2.at[1, z, h, self.second]
                )
                return carry

            lax.fori_loop(0, 8, take, 0, unroll=2)
            for v, rows, name in ((y1, self.first, "y1"), (y3, self.second, "y3")):
                self.step.append(
                    self.links.start(self.sums.at[:, h, v, rows], self.ry1.at[:, h, rows], self.cube[name])
                )

    def along(self):
        tx, y = self.where[1], self.where[4]
        self.wait()

        def take(z, carry):
            for h in range(2):
                self.add(z, h, y, self.whole, self.sums.at[z, h, y], self.ry1.at[z, h])
            return carry

        lax.fori_loop(0, 8, take, 0)
        self.step = [
            self.links.start(self.sums.at[(tx + d + 1) % N_TX, :, y], self.rz.at[d], peer)
            for d, peer in enumerate(self.line)
        ]

    def swap(self):
        tx, hi, y = self.where[1], self.where[3], self.where[4]
        self.wait()
        for h in range(2):
            value = self.sums[tx, h, y].astype(f32)
            for d in range(N_TX - 1):
                value = value + self.rz[d, h].astype(f32)
            self.half[h] = value
        self.step = [
            self.links.start(self.half.at[hi], self.rg.at[0], self.cube["grp"]),
            self.links.start(self.half.at[1 - hi], self.rg.at[1], self.cube["x"]),
            self.links.start(self.half.at[1 - hi], self.rg.at[2], self.cube["xx"]),
        ]

    def done(self):
        self.wait()
        self.total[...] = (self.half[self.where[3]] + self.rg[0]) + (self.rg[1] + self.rg[2])


def fold(tiles):
    wide, mid, rest = tiles
    lanes = lax.broadcasted_iota(jnp.int32, (8, 128), 1)
    rows = lax.broadcasted_iota(jnp.int32, (8, 128), 0)
    tail = jnp.zeros((8, 128), f32)
    for n in range(4):
        piece = rest[8 * n : 8 * n + 8]
        piece = pltpu.roll(piece, 32 * n, 1) if n else piece
        tail = jnp.where((lanes >= 32 * n) & (lanes < 32 * n + 32), piece, tail)
    last = jnp.where(rows < 3, wide[24:32], jnp.where(rows < 6, pltpu.roll(mid[24:32], 3, 0), 0.0))
    return jnp.concatenate([wide[:24], mid[:24], tail, last], axis=0)


def unfold(rows):
    tail, last = rows[48:56], rows[56:64]
    rest = jnp.concatenate([tail] + [pltpu.roll(tail, 128 - 32 * n, 1) for n in range(1, 4)], axis=0)
    return [
        jnp.concatenate([rows[:24], last], axis=0),
        jnp.concatenate([rows[24:48], pltpu.roll(last, 5, 0)], axis=0),
        rest,
    ]


def choose(slots, place, blocks):
    value = None
    for i, block in enumerate(blocks):
        term = jnp.where(slots[0, i] == place, block, 0.0)
        value = term if value is None else value + term
    return value


def corner(slots, i):
    return slots[0, i] // GY, slots[0, i] % GY


def pack_shards(w_conv1, w_down, w_conv2, shard_a, shard_b, tmp, wide):
    tmp[...] = jnp.zeros_like(tmp)
    wide[...] = jnp.zeros_like(wide)
    tmp[0, 0:27, 0:72] = w_conv1[...].astype(f32)
    wide[0:8, 0:144] = w_down[...].astype(f32)
    low = lane_tiles(wide[0:8, 0:256])
    for j in range(3):
        tmp[1, pl.ds(j, 8, stride=3), :] = relane(1, [(low, 48 * j, BASE_DOWN, 48)])[0]
    shard_a[...] = (tmp[0] + tmp[1]).astype(bf16)
    wide[0:27, 0:288] = w_conv2[...].astype(f32)
    shard_b[...] = fold(lane_tiles(wide[...])).astype(bf16)


def prepare(slots, count, feats, occupancy, cot, mask, coarse, mp, gp, fine):
    flags = []
    for p in range(GX * GY):
        flag = jnp.where(slots[0, 0] == p, 1.0, 0.0)
        for i in range(1, CAP):
            flag = flag + jnp.where((slots[0, i] == p) & (count[0] > i), 1.0, 0.0)
        flags.append(flag)

    def iotas(rows, lanes):
        return [lax.broadcasted_iota(jnp.int32, (rows, lanes), d) for d in range(2)]

    row, lane = iotas(256, 8)
    pick_z = jnp.where(row % 8 == lane, 1.0, 0.0).astype(bf16)
    row, lane = iotas(256, 32)
    pick_y = row // 8 == lane
    row, lane = iotas(128, 8)
    pair_z = jnp.where(row % 8 == lane // 2, 1.0, 0.0).astype(bf16)
    row, lane = iotas(128, 32)
    pair_y = row // 8 == lane // 2
    ones = jnp.ones((32, 256), bf16)
    if fine:
        mp[1:17, 1:33] = jnp.zeros((16, 32, 8, 128), f32)
    else:
        gp[1:9, 1:17] = jnp.zeros((8, 16, 8, 256), f32)
    for px in range(GX) if fine else ():

        def first(x, carry):
            plane = occupancy[0, x].astype(f32).astype(bf16)
            column = jnp.dot(pick_z, plane, preferred_element_type=f32)
            column = jnp.where(pick_y, column, 0.0).astype(bf16)
            value = jnp.dot(column, ones[:, :128], preferred_element_type=f32).reshape(32, 8, 128)
            for py in range(GY):
                at = slice(py * 8, py * 8 + 8)
                live = value[at] * flags[px * GY + py]
                mask[x, at] = live
                mp[1 + x, 1 + py * 8 : 9 + py * 8, :, 0:C1] = feats[0, x, at].astype(f32) * live[:, :, 0:C1]
            return carry

        lax.fori_loop(px * 8, px * 8 + 8, first, 0, unroll=4)

    for px in range(GX) if not fine else ():

        def second(a, carry):
            plane = (occupancy[0, 2 * a] + occupancy[0, 2 * a + 1]).astype(f32).astype(bf16)
            column = jnp.dot(pair_z, plane, preferred_element_type=f32)
            column = jnp.where(pair_y, column, 0.0).astype(bf16)
            value = jnp.minimum(jnp.dot(column, ones, preferred_element_type=f32), 1.0).reshape(16, 8, 256)
            for py in range(GY):
                at = slice(py * 4, py * 4 + 4)
                live = value[at] * flags[px * GY + py]
                coarse[a, at] = live
                grad = cot[0, a, at].astype(f32) * live[:, 0:4, 0:C2]
                gp[1 + a, 1 + py * 4 : 5 + py * 4, 0:4, 0:C2] = grad
            return carry

        lax.fori_loop(px * 4, px * 4 + 4, second, 0, unroll=4)


def unpack_first(full, w9, wd, w1g, wdg, tmp):
    def unpack(a, carry):
        shards = []
        for b in range(4):
            value = full[a // 4, (a // 2) % 2, (a % 2) * 2 + b // 2, b % 2]
            tmp[b] = value.astype(f32)
            shards.append([value])
        for k in range(3):
            w1g[pl.ds((a * 3 + k) * PITCH_W, 32), :] = to_row(shards, PIECES_ONE[k], 0, 1)[0].astype(f32)
        chunks = [[tmp[b, pl.ds(j, 8, stride=3), :]] for b in range(4) for j in range(3)]
        for k in range(3):
            segments = [(chunks[4 * k + n], BASE_DOWN, 48 * n, 48) for n in range(4)]
            for c, tile in enumerate(relane(2, segments)):
                wdg[c, pl.ds(pl.multiple_of((a * 3 + k) * 8, 8), 8), :] = tile
        return carry

    lax.fori_loop(0, GROUPS, unpack, 0, unroll=4)
    for t in range(27):
        k, oz = t // 3, t % 3
        w9[k * 128 : k * 128 + C1, oz * 128 : (oz + 1) * 128] = w1g[pl.ds(t, C1, stride=PITCH_W), :].astype(bf16)
    for k in range(9):
        w9[k * 128 + C1 : (k + 1) * 128, :] = jnp.zeros((128 - C1, 384), bf16)
    for t in range(8):
        for c in range(2):
            wd[t * 128 : t * 128 + C1, c * 128 : (c + 1) * 128] = wdg[c, pl.ds(t, C1, stride=8), :].astype(bf16)
        wd[t * 128 + C1 : (t + 1) * 128, :] = jnp.zeros((128 - C1, 256), bf16)


def unpack_second(full, w2, big):
    def unpack(a, carry):
        shards = [
            [
                tile.astype(bf16)
                for tile in unfold(full[a // 4, (a // 2) % 2, (a % 2) * 2 + b // 2, b % 2].astype(f32))
            ]
            for b in range(4)
        ]
        for k in range(6):
            for c, tile in enumerate(to_row(shards, PIECES_TWO[k], 0, 2)):
                big[c, pl.ds((a * 6 + k) * PITCH_W, 32), :] = tile.astype(f32)
        return carry

    lax.fori_loop(0, GROUPS, unpack, 0, unroll=4)

    def order(k, carry):
        for oz in range(3):
            for c in range(2):
                w2[pl.ds(pl.multiple_of(k * 256, 256), C2), oz * 256 + c * 128 : oz * 256 + (c + 1) * 128] = big[
                    c, pl.ds(k * 3 + oz, C2, stride=PITCH_W), :
                ].astype(bf16)
        w2[pl.ds(pl.multiple_of(k * 256 + C2, 64), 256 - C2), :] = jnp.zeros((256 - C2, 768), bf16)
        return carry

    lax.fori_loop(0, 9, order, 0, unroll=3)


def windows(dst, i, window, edge, flip):
    lanes = window.shape[-1]
    rows = edge * edge * 8
    for k in range(9):
        ox, oy = k // 3, k % 3
        if flip:
            ox, oy = 2 - ox, 2 - oy
        piece = window[ox : ox + edge, oy : oy + edge].reshape(rows, lanes)
        dst[i * rows : (i + 1) * rows, k * lanes : (k + 1) * lanes] = piece.astype(bf16)


def three(rows, lanes):
    return [rows[:, n * lanes : (n + 1) * lanes].reshape(-1, 8, lanes) for n in range(3)]


def conv(parts):
    low, mid, high = parts
    return (depth_shifts(low)[0] + mid + depth_shifts(high)[2]).reshape(-1, mid.shape[-1])


def spread(value):
    below, mid, above = depth_shifts(value.reshape(-1, 8, value.shape[-1]))
    return jnp.concatenate([v.reshape(value.shape).astype(bf16) for v in (above, mid, below)], axis=1)


def pack_first(packed, r1, rdn, tmp, pair, h):
    def pack(z, carry):
        a = z * 4 + h * 2 + pair
        segments = [[] for _ in range(4)]
        downs = []
        for k in range(3):
            ci = a * 3 + k
            tiles = [r1[pl.ds(ci, 32, stride=PITCH_S), :].astype(bf16)]
            for s, at, lane, n in PIECES_ONE[k]:
                segments[s].append((tiles, lane, at, n))
            downs.append([rdn[c, pl.ds(ci, 8, stride=PITCH_S), :] for c in range(2)])
        for b in range(4):
            for j in range(3):
                m = 3 * b + j
                tmp[b, pl.ds(j, 8, stride=3), :] = relane(1, [(downs[m // 4], m % 4 * 48, BASE_DOWN, 48)])[0]
            value = relane(1, segments[b])[0].astype(f32) + tmp[b]
            packed[z, h, pair * 2 + b // 2, b % 2] = value.astype(bf16)
        return carry

    lax.fori_loop(0, 8, pack, 0, unroll=4)


def pack_second(packed, big, pair, h):
    def pack(z, carry):
        a = z * 4 + h * 2 + pair
        segments = [[] for _ in range(4)]
        for k in range(6):
            tiles = [big[c, pl.ds(a * 6 + k, 32, stride=PITCH_R), :].astype(bf16) for c in range(2)]
            for s, at, lane, n in PIECES_TWO[k]:
                segments[s].append((tiles, lane, at, n))
        for b in range(4):
            packed[z, h, pair * 2 + b // 2, b % 2] = fold(
                [tile.astype(f32) for tile in relane(3, segments[b])]
            ).astype(bf16)
        return carry

    lax.fori_loop(0, 8, pack, 0, unroll=4)


def whole_kernel(
    slots, count, feats_in, occupancy_in, cot_in, w_conv1, w_down, w_conv2, out, grad_conv1, grad_down, grad_conv2,
    feats, occupancy, cot, total_a, total_b, mask, coarse, shard_a, shard_b, wide,
    full_a, full_b, mp, gp, dp, x9, x2, x3, w9, wd, w2, w1g, wdg, tmp, big, act, pm, hs, gs, r1, rdn,
    packed_a, packed_b, sums_a, rd_a, ry2_a, ry1_a, rz_a, half_a, rg_a,
    sums_b, rd_b, ry2_b, ry1_b, rz_b, half_b, rg_b, *rest,
):
    bufs_m, bufs_g, bufs_d = rest[0:4], rest[4:8], rest[8:12]
    send, recv, own = rest[12:]
    where = place()
    grp, tx, ty, hi, y, core = where
    cube = cube_peers(grp, tx, hi, y, core)
    around = halo_peers(grp, tx, ty)
    links = Links(send, recv)
    loads = [
        pltpu.make_async_copy(src, dst, own.at[2 + k])
        for k, (src, dst) in enumerate(((feats_in, feats), (occupancy_in, occupancy), (cot_in, cot)))
    ]
    for load in loads:
        load.start()
    greeted = ring_peers(grp, tx, ty) + across_peers(grp, tx, hi, y, core) + [cube[n] for n in ("core", "y1", "y3", "xx", "grp")] + around
    barrier = pltpu.get_barrier_semaphore()
    for peer in greeted:
        pl.semaphore_signal(barrier, inc=1, device_id=peer, device_id_type=MESH)
    pack_shards(w_conv1, w_down, w_conv2, shard_a, shard_b, tmp, wide)
    pl.semaphore_wait(barrier, len(greeted))

    first = Gather(links, where, shard_a, full_a, own.at[0])
    second = Gather(links, where, shard_b, full_b, own.at[1])
    for load in loads:
        load.wait()
    prepare(slots, count, feats, occupancy, cot, mask, coarse, mp, gp, True)
    halo_m = links.halo(mp, around, bufs_m, False)
    first.near()
    prepare(slots, count, feats, occupancy, cot, mask, coarse, mp, gp, False)
    second.near()
    first.far()
    halo_g = links.halo(gp, around, bufs_g, True)
    land(mp, halo_m, bufs_m, False)
    clear_edges(mp, tx, ty)
    for i in range(CAP):
        px, py = corner(slots, i)
        windows(x9, i, mp[pl.ds(px * 8, 10), pl.ds(py * 8, 10)], 8, False)
    second.far()
    first.last()
    hs[...] = jnp.zeros_like(hs)
    rdn[...] = jnp.zeros_like(rdn)
    r1[27 * PITCH_S : 32 * PITCH_S, :] = jnp.zeros((5 * PITCH_S, 128), f32)
    big[:, 27 * PITCH_R : 32 * PITCH_R, :] = jnp.zeros((2, 5 * PITCH_R, 128), f32)
    first.done()
    unpack_first(full_a, w9, wd, w1g, wdg, tmp)

    lives, edges = [], []
    for i in range(CAP):
        px, py = corner(slots, i)
        lives.append(mask[pl.ds(px * 8, 8), pl.ds(py * 8, 8)].reshape(512, 128))
        edges.append(coarse[pl.ds(px * 4, 4), pl.ds(py * 4, 4)].reshape(128, 256))
    live = jnp.concatenate(lives, axis=0)
    edge = jnp.concatenate(edges, axis=0)
    value = conv(three(jnp.dot(x9[...], w9[...], preferred_element_type=f32), 128))
    act[...] = value
    hidden = (live * jax.nn.silu(value)).astype(bf16).astype(f32).reshape(CAP, 4, 2, 4, 2, 8, 128)
    for p in range(2):
        for q in range(2):
            for b in range(4):
                hs[:, :, p * 2 + q, b * 16 : b * 16 + 8, :] = hidden[:, :, p, b, q]
    second.last()
    for t in range(8):
        patch = hs[:, :, t // 2, pl.ds(t % 2, 32, stride=2), :].reshape(256, 128)
        pm[:, t * 128 : (t + 1) * 128] = patch.astype(bf16)
    raw = jnp.dot(pm[...], wd[...], preferred_element_type=f32)
    down = (edge * raw).astype(bf16).astype(f32)
    downs = [down[i * 128 : (i + 1) * 128].reshape(4, 4, 8, 256) for i in range(CAP)]
    for p in range(GX * GY):
        px, py = p // GY, p % GY
        dp[1 + px * 4 : 5 + px * 4, 1 + py * 4 : 5 + py * 4] = choose(slots, p, downs)
    halo_d = links.halo(dp, around, bufs_d, True)

    land(gp, halo_g, bufs_g, True)
    clear_edges(gp, tx, ty)
    grads = []
    for i in range(CAP):
        px, py = corner(slots, i)
        windows(x3, i, gp[pl.ds(px * 4, 6), pl.ds(py * 4, 6)], 4, True)
        grads.append(gp[pl.ds(px * 4 + 1, 4), pl.ds(py * 4 + 1, 4)].reshape(128, 256))
    grad_two = jnp.concatenate(grads, axis=0)
    spread_two = spread(grad_two)
    second.done()
    unpack_second(full_b, w2, big)
    parts = []
    for oz in range(3):
        part = None
        for k in range(9):
            term = lax.dot_general(
                x3[:, k * 256 : (k + 1) * 256],
                w2[k * 256 : (k + 1) * 256, oz * 256 : (oz + 1) * 256],
                (((1,), (1,)), ((), ())),
                preferred_element_type=f32,
            )
            part = term if part is None else part + term
        parts.append(part.reshape(-1, 8, 256))
    back = conv(parts[::-1])
    grad_in = (grad_two + edge * back).astype(bf16)
    land(dp, halo_d, bufs_d, True)
    clear_edges(dp, tx, ty)
    for i in range(CAP):
        px, py = corner(slots, i)
        windows(x2, i, dp[pl.ds(px * 4, 6), pl.ds(py * 4, 6)], 4, False)
    for k in range(9):
        product = lax.dot_general(
            x2[:, k * 256 : (k + 1) * 256], spread_two, (((0,), (0,)), ((), ())), preferred_element_type=f32
        )
        for oz in range(3):
            for c in range(2):
                at = oz * 256 + c * 128
                big[c, (3 * k + oz) * PITCH_R : (3 * k + oz) * PITCH_R + 256, :] = product[:, at : at + 128]
    sum_b = Scatter(links, where, packed_b, total_b, sums_b, rd_b, ry2_b, ry1_b, rz_b, half_b, rg_b)
    for pair, pieces in ((1 - y // 2, (0, 1)), (y // 2, (2, 3))):
        for h in range(2):
            pack_second(packed_b, big, pair, h)
            sum_b.cores(pieces, h)

    for t in range(8):
        product = lax.dot_general(
            pm[:, t * 128 : (t + 1) * 128], grad_in, (((0,), (0,)), ((), ())), preferred_element_type=f32
        )
        for c in range(2):
            rdn[c, t * PITCH_S : t * PITCH_S + 128, :] = product[:, c * 128 : (c + 1) * 128]
    for t in range(8):
        part = lax.dot_general(
            grad_in, wd[t * 128 : (t + 1) * 128, :], (((1,), (1,)), ((), ())), preferred_element_type=f32
        )
        gs[:, :, t // 2, pl.ds(t % 2, 32, stride=2), :] = part.reshape(CAP, 4, 32, 128)
    sum_b.far()
    rows = []
    for p in range(2):
        for b in range(4):
            for q in range(2):
                rows.append(gs[:, :, p * 2 + q, b * 16 : b * 16 + 8, :])
    hidden = jnp.stack(rows, axis=2).reshape(1024, 128)
    value = act[...]
    sig = jax.nn.sigmoid(value)
    spread_one = spread(live * hidden * (sig * (1.0 + value * (1.0 - sig))))
    for k in range(9):
        product = lax.dot_general(
            x9[:, k * 128 : (k + 1) * 128], spread_one, (((0,), (0,)), ((), ())), preferred_element_type=f32
        )
        for oz in range(3):
            at = (3 * k + oz) * PITCH_S
            r1[at : at + 128, :] = product[:, oz * 128 : (oz + 1) * 128]
    tmp[...] = jnp.zeros_like(tmp)
    sum_a = Scatter(links, where, packed_a, total_a, sums_a, rd_a, ry2_a, ry1_a, rz_a, half_a, rg_a)
    for pair, pieces in ((1 - y // 2, (0, 1)), (y // 2, (2, 3))):
        for h in range(2):
            pack_first(packed_a, r1, rdn, tmp, pair, h)
            sum_a.cores(pieces, h)
    sum_b.near()

    parts = [
        jnp.dot(x2[...], w2[:, oz * 256 : (oz + 1) * 256], preferred_element_type=f32).reshape(-1, 8, 256)
        for oz in range(2)
    ]
    sum_a.far()
    parts.append(jnp.dot(x2[...], w2[:, 512:768], preferred_element_type=f32).reshape(-1, 8, 256))
    value = conv(parts)
    sum_b.along()
    blocks = []
    for i in range(CAP):
        px, py = corner(slots, i)
        down = dp[pl.ds(px * 4 + 1, 4), pl.ds(py * 4 + 1, 4)].reshape(128, 256)
        rows = slice(i * 128, (i + 1) * 128)
        blocks.append((edges[i] * (down + value[rows])).reshape(4, 4, 8, 256))
    sum_a.near()
    for p in range(GX * GY):
        px, py = p // GY, p % GY
        out[0, px * 4 : px * 4 + 4, py * 4 : py * 4 + 4] = choose(slots, p, blocks)[:, :, 0:4, 0:C2].astype(bf16)
    before = len(links.sent)
    sum_a.along()
    links.flush(before)
    before = len(links.sent)
    sum_b.swap()
    sum_a.swap()
    links.flush(before)
    sum_b.done()
    wide = unfold(total_b[...])
    grad_conv2[:, 0:256] = jnp.concatenate(wide[:2], axis=1)[:27]
    grad_conv2[:, 256:288] = wide[2][:27, :32]
    sum_a.done()
    grad_conv1[...] = total_a[:27, :72]
    low = [(total_a[pl.ds(j, 8, stride=3), :],) for j in range(3)]
    low = relane(2, [(low[j], BASE_DOWN, 48 * j, 48) for j in range(3)])
    grad_down[:, 0:128] = low[0]
    grad_down[:, 128:144] = low[1][:, :16]
    links.flush(len(links.sent))


def whole(order, count, feats, occupancy, cot, w_conv1, w_down, w_conv2):
    def sums(rows):
        return [
            pltpu.VMEM((8, 2, 4, rows, 128), bf16),
            pltpu.VMEM((8, 2, 4, rows, 128), bf16),
            pltpu.VMEM((2, 8, 2, rows, 128), bf16),
            pltpu.VMEM((8, 2, rows, 128), bf16),
            pltpu.VMEM((7, 2, rows, 128), bf16),
            pltpu.VMEM((2, rows, 128), f32),
            pltpu.VMEM((3, rows, 128), f32),
        ]

    copies = 2 * 30 + 24 + 2 * 30
    return pl.pallas_call(
        whole_kernel,
        in_specs=[pl.BlockSpec(memory_space=pltpu.SMEM)] * 2
        + [pl.BlockSpec(memory_space=pl.ANY)] * 3
        + [pl.BlockSpec(memory_space=pltpu.VMEM)] * 3,
        out_specs=[pl.BlockSpec(memory_space=pltpu.VMEM)] * 4,
        out_shape=[
            jax.ShapeDtypeStruct((1, 8, 16, 4, C2), bf16),
            jax.ShapeDtypeStruct((27, 72), f32),
            jax.ShapeDtypeStruct((8, 144), f32),
            jax.ShapeDtypeStruct((27, 288), f32),
        ],
        scratch_shapes=[
            pltpu.VMEM((1, 16, 32, 8, C1), bf16),
            pltpu.VMEM((1, 16, 8, 32), jnp.int32),
            pltpu.VMEM((1, 8, 16, 4, C2), bf16),
            pltpu.VMEM((32, 128), f32),
            pltpu.VMEM((64, 128), f32),
            pltpu.VMEM((16, 32, 8, 128), f32),
            pltpu.VMEM((8, 16, 8, 256), f32),
            pltpu.VMEM((32, 128), bf16),
            pltpu.VMEM((64, 128), bf16),
            pltpu.VMEM((32, 384), f32),
            pltpu.VMEM((8, 2, 4, 2, 32, 128), bf16),
            pltpu.VMEM((8, 2, 4, 2, 64, 128), bf16),
            pltpu.VMEM((18, 34, 8, 128), f32),
            pltpu.VMEM((10, 18, 8, 256), f32),
            pltpu.VMEM((10, 18, 8, 256), f32),
            pltpu.VMEM((1024, 9 * 128), bf16),
            pltpu.VMEM((256, 9 * 256), bf16),
            pltpu.VMEM((256, 9 * 256), bf16),
            pltpu.VMEM((9 * 128, 384), bf16),
            pltpu.VMEM((1024, 256), bf16),
            pltpu.VMEM((9 * 256, 768), bf16),
            pltpu.VMEM((C1 * PITCH_W + 8, 128), f32),
            pltpu.VMEM((2, C1 * 8, 128), f32),
            pltpu.VMEM((4, 32, 128), f32),
            pltpu.VMEM((2, 32 * PITCH_R, 128), f32),
            pltpu.VMEM((1024, 128), f32),
            pltpu.VMEM((256, 1024), bf16),
            pltpu.VMEM((CAP, 4, 4, 64, 128), f32),
            pltpu.VMEM((CAP, 4, 4, 64, 128), f32),
            pltpu.VMEM((32 * PITCH_S, 128), f32),
            pltpu.VMEM((2, 8 * PITCH_S, 128), f32),
            pltpu.VMEM((8, 2, 4, 2, 32, 128), bf16),
            pltpu.VMEM((8, 2, 4, 2, 64, 128), bf16),
        ]
        + sums(32)
        + sums(64)
        + [
            pltpu.VMEM((2, rows, lanes), bf16)
            for sides, lanes in (((256, 128), 128), ((64, 32), 256), ((64, 32), 256))
            for rows in sides + sides
        ]
        + [
            pltpu.SemaphoreType.DMA((copies,)),
            pltpu.SemaphoreType.DMA((copies,)),
            pltpu.SemaphoreType.DMA((5,)),
        ],
        compiler_params=pltpu.CompilerParams(collective_id=0, has_side_effects=True, vmem_limit_bytes=VMEM_LIMIT),
        name="whole",
    )(order, count, feats, occupancy, cot, w_conv1, w_down, w_conv2)


def local(features, voxel_mask, brick_order, brick_count, w_conv1, w_down, w_conv2, cotangent):
    return tuple(
        whole(brick_order, brick_count, features, voxel_mask.transpose(0, 1, 3, 2), cotangent, w_conv1, w_down, w_conv2)
    )


def solution(mesh):
    return jax.shard_map(
        local,
        mesh=mesh,
        in_specs=(
            P("grp", "tx", "ty", None, None),
            P("grp", "tx", "ty", None),
            P(("grp", "tx", "ty"), None),
            P(("grp", "tx", "ty")),
            P(None, ("tx", "ty")),
            P(None, ("tx", "ty")),
            P(None, ("tx", "ty")),
            P("grp", "tx", "ty", None, None),
        ),
        out_specs=(
            P("grp", "tx", "ty", None, None),
            P(None, ("tx", "ty")),
            P(None, ("tx", "ty")),
            P(None, ("tx", "ty")),
        ),
        check_vma=False,
    )
```
